768 devices in a mesh: cell: 16 (over y, core), vel: 48 (over x, z).
Axes of the slice: x: 4, y: 8, z: 12, core: 2. Of those that a mesh axis runs over, the one named last changes fastest.
Arguments:
- distribution: float32 [3072, 16, 384], P('vel', 'cell'), may hold values from 0.1 to 2
- gain_left: float32 [2, 3072], replicated, may hold values from -3 to 3
- gain_right: float32 [2, 3072], replicated, may hold values from -3 to 3
- loss_kernel: float32 [3072], replicated, may hold values from 0.1 to 1.5
- wall_cell: int32 [16, 48, 8], P('cell', 'vel'), may hold values from 0 to 7
- wall_count: int32 [16, 48], P('cell', 'vel'), may hold values from 0 to 8, as said below
- wall_panel: int32 [16, 48, 8], P('cell', 'vel'), may hold values from 0 to 3071, as said below
Outputs:
- final_distribution: float32 [3072, 16, 384], P('vel', 'cell')
- panel_loads: float32 [4, 3072], P(None, ('cell', 'vel'))
The draws below stay inside these ranges and needn't reach their ends.
Inputs may be any that keep to these rules, and one draw needn't show every extreme that they name: `wall_count`: slots from the count on are padding; some column uses all 8 slots. The panel of a slot in column (x, y) satisfies (wall_panel // 4) % 48 == y; padding slots hold valid panel numbers.
All inputs are finite; a program needn't handle non-finite values.
Results may differ from the reference program's by a relative error of at most 0.0001.
Values sent between devices are 32-bit elements; how exact they have to be, the bound alone decides.
A program may use at most 32 MiB of HBM per device.

```python
import math
import jax
import jax.numpy as jnp
from jax import lax

NVX = 16
NVY = 16
NVZ = 12
V = 3072
DIRS = 2
MOMENTS = 4
STEPS = 3
NZ = 8
WALL_SLOTS = 8
PANEL_DEV = 4
NX = 16
NY = 48
PANELS = 3072


def draw_wall_count(key, part):
    counts = jax.random.randint(key, (NX, NY), 0, WALL_SLOTS + 1, dtype=jnp.int32)
    return counts.at[0, 0].set(WALL_SLOTS)


def draw_wall_panel(key, part):
    first_key = jax.random.fold_in(key, 11)
    second_key = jax.random.fold_in(key, 23)
    third_key = jax.random.fold_in(key, 37)
    owner_one = jax.random.randint(first_key, (NX, NY, WALL_SLOTS), 0, NX, dtype=jnp.int32)
    owner_two = jax.random.randint(second_key, (NX, NY, WALL_SLOTS), 0, NX, dtype=jnp.int32)
    owner = jnp.minimum(owner_one, owner_two)
    within = jax.random.randint(third_key, (NX, NY, WALL_SLOTS), 0, PANEL_DEV, dtype=jnp.int32)
    column_y = jnp.arange(NY, dtype=jnp.int32)[None, :, None]
    return (owner * NY + column_y) * PANEL_DEV + within


def set_ends(result, rng, low, top_value):
    longest = result.shape.index(max(result.shape))
    spots = []
    for shift in (0, 1):
        where = [jax.random.randint(jax.random.fold_in(rng, axis), (), 0, length) for axis, length in enumerate(result.shape)]
        where[longest] = (where[longest] + shift) % result.shape[longest]
        spots.append(tuple(where))
    return result.at[spots[0]].set(low).at[spots[1]].set(top_value)


def steps_of(own_key, shape, shards, least, top_value):
    factor_of = 1.0
    for position, shards_of in shards:
        heights = jax.random.uniform(jax.random.fold_in(jax.random.fold_in(own_key, 6), position), (shards_of,), jnp.float32, least / len(shards), top_value / len(shards))
        factor_of = factor_of * jnp.repeat(jnp.exp(heights), shape[position] // shards_of).reshape((-1,) + (1,) * (len(shape) - 1 - position))
    return factor_of


def noise(rng, dims, scale, bound, kind=jnp.bfloat16):
    drawn = scale * jax.random.normal(rng, dims, jnp.float32)
    return jnp.clip(drawn, min=-bound, max=bound).astype(kind)


def setup_inputs(seed: int = 0) -> dict:
    arg_keys = jax.random.split(jax.random.key(seed), 8)
    return {
        "distribution": jnp.clip(jnp.exp(math.log(2.0) - 2.9957323 * jax.random.uniform(arg_keys[0], (V, NX, NY * NZ), jnp.float32) ** steps_of(arg_keys[0], (V, NX, NY * NZ), ((0, 48), (1, 16)), -0.2, 0.2)), 0.1, 2.0),
        "gain_left": noise(arg_keys[1], (DIRS, V), 0.5, 3.0, jnp.float32),
        "gain_right": noise(arg_keys[2], (DIRS, V), 0.5, 3.0, jnp.float32),
        "loss_kernel": jnp.clip(jax.random.uniform(arg_keys[3], (V,), jnp.float32, 0.1, 1.5), 0.1, 1.5),
        "wall_cell": set_ends(jax.random.randint(arg_keys[4], (NX, NY, WALL_SLOTS), 0, NZ), jax.random.fold_in(arg_keys[4], 1), 0, NZ - 1).astype(jnp.int32),
        "wall_count": draw_wall_count(jax.random.fold_in(arg_keys[7], 71), 0),
        "wall_panel": draw_wall_panel(jax.random.fold_in(arg_keys[7], 71), 0),
    }


SPACING = 0.5
COURANT = 0.09
COLLISION_STEP = 0.3


def velocity_components(index):
    first = index // (NVY * NVZ)
    second = (index // NVZ) % NVY
    third = index % NVZ
    speed_x = (2 * first - (NVX - 1)).astype(jnp.float32) * (0.5 * SPACING)
    speed_y = (2 * second - (NVY - 1)).astype(jnp.float32) * (0.5 * SPACING)
    speed_z = (2 * third - (NVZ - 1)).astype(jnp.float32) * (0.5 * SPACING)
    return speed_x, speed_y, speed_z


def one_flux(speed, center, behind, ahead):
    speed = speed.reshape(-1, 1, 1, 1)
    return jnp.maximum(speed, 0.0) * (center - behind) + jnp.minimum(speed, 0.0) * (ahead - center)


def upwind(padded, speeds):
    center = padded[:, 1:-1, 1:-1, 1:-1]
    fluxes = one_flux(speeds[0], center, padded[:, :-2, 1:-1, 1:-1], padded[:, 2:, 1:-1, 1:-1])
    fluxes = fluxes + one_flux(speeds[1], center, padded[:, 1:-1, :-2, 1:-1], padded[:, 1:-1, 2:, 1:-1])
    fluxes = fluxes + one_flux(speeds[2], center, padded[:, 1:-1, 1:-1, :-2], padded[:, 1:-1, 1:-1, 2:])
    return center - COURANT * fluxes


def collide_plane(plane, kernels):
    shape = plane.shape
    values = plane.reshape(NVX, NVY, NVZ, -1)
    spectrum = jnp.fft.fftn(values, axes=(0, 1, 2))
    spectra = kernels.reshape(-1, NVX, NVY, NVZ, 1)
    convolved = jnp.real(jnp.fft.ifftn(spectra * spectrum[None], axes=(1, 2, 3)))
    gains = jnp.sum(convolved[:DIRS] * convolved[DIRS:2 * DIRS], axis=0)
    change = gains - values * convolved[2 * DIRS]
    return (values + COLLISION_STEP * change).reshape(shape)


def reference(distribution, gain_left, gain_right, loss_kernel, wall_cell, wall_count, wall_panel):
    kernels = jnp.concatenate([gain_left, gain_right, loss_kernel[None]], axis=0)
    speeds = velocity_components(jnp.arange(NVX * NVY * NVZ, dtype=jnp.int32))
    current = distribution.reshape(NVX * NVY * NVZ, NX, NY, NZ)

    def collide_one(plane):
        return collide_plane(plane, kernels)

    for iteration in range(STEPS):
        padded = jnp.pad(current, ((0, 0), (1, 1), (1, 1), (1, 1)))
        moved = upwind(padded, speeds)
        collided = lax.map(collide_one, jnp.moveaxis(moved, 1, 0))
        current = jnp.moveaxis(collided, 0, 1)
    weights = jnp.stack([speeds[0], speeds[1], speeds[2],
                         speeds[0] * speeds[0] + speeds[1] * speeds[1] + speeds[2] * speeds[2]]) * (SPACING ** 3)
    moments = jnp.einsum("qv,vxyz->qxyz", weights, current, precision=lax.Precision.HIGHEST)
    picked = jnp.take_along_axis(moments, wall_cell[None], axis=3)
    in_use = jnp.arange(WALL_SLOTS, dtype=jnp.int32)[None, None, :] < wall_count[:, :, None]
    values = jnp.where(in_use[None], picked, 0.0).reshape(MOMENTS, -1)
    loads = jax.ops.segment_sum(values.T, wall_panel.reshape(-1), num_segments=PANELS).T
    return current.reshape(NVX * NVY * NVZ, NX, NY * NZ), loads
```

```python
import functools
import math

import jax
import jax.numpy as jnp
import ml_dtypes
import numpy as np
from jax import lax
from jax.experimental import pallas as pl
from jax.experimental.pallas import tpu as pltpu
from jax.sharding import PartitionSpec as P

NVY = 16
NVZ = 12
PLANE = NVY * NVZ
HALF = PLANE // 2
KEPT = NVZ // 2 + 1
KERNELS = 5
DIRS = 2
MOMENTS = 4
STEPS = 3
NZ = 8
WALL_SLOTS = 8
PANEL_DEV = 4
LOCAL_V = 64
PARTS = PLANE // LOCAL_V
LANES = 128

SPACING = 0.5
COURANT = 0.09
COLLISION_STEP = 0.3

MESH = pl.DeviceIdType.MESH


def split(values):
    high = values.astype(ml_dtypes.bfloat16)
    low = (values - high.astype(np.float64)).astype(ml_dtypes.bfloat16)
    return high, low


def plane_matrices():
    table = np.zeros((2 * LANES, 2 * LANES))
    for point in range(PLANE):
        b, c = divmod(point, NVZ)
        row = b // (NVY // 2) * LANES + point % HALF
        for kb in range(NVY):
            for kc in range(KEPT):
                angle = 2.0 * math.pi * ((b * kb % NVY) / NVY + (c * kc % NVZ) / NVZ)
                table[row, kb * KEPT + kc] = math.cos(angle)
                table[row, LANES + kb * KEPT + kc] = -math.sin(angle)
    high, low = split(table)
    return np.concatenate([high, low, high.T, low.T], axis=0)


def lane_tables():
    lane = np.arange(LANES)
    used = (lane < HALF).astype(np.float64)
    vz = (2 * (lane % NVZ) - (NVZ - 1)) * 0.5 * SPACING * used
    vy = [(2 * (lane // NVZ + h * NVY // 2) - (NVY - 1)) * 0.5 * SPACING * used for h in (0, 1)]
    z = np.arange(NZ)[:, None]
    rows = []
    for h in (0, 1):
        rows.append(1.0 - COURANT * (np.abs(vy[h]) + np.abs(vz)) + 0.0 * z)
    for h in (0, 1):
        rows.append(COURANT * np.abs(vy[h]) + 0.0 * z)
    rows.append(COURANT * np.maximum(vz, 0.0) * (z > 0))
    rows.append(COURANT * np.maximum(-vz, 0.0) * (z < NZ - 1))
    cube = SPACING**3
    rows.append(cube * vy[0] + 0.0 * z)
    rows.append(cube * vy[1] + 0.0 * z)
    rows.append(cube * vz + 0.0 * z)
    rows.append(cube * (vy[0] ** 2 + vz**2) + 0.0 * z)
    rows.append(cube * (vy[1] ** 2 + vz**2) + 0.0 * z)
    return np.stack(rows).astype(np.float32)


def fourier(real, imag, sign):
    count = len(real)
    if count == 1:
        return real, imag
    even_r, even_i = fourier(real[::2], imag[::2], sign)
    odd_r, odd_i = fourier(real[1::2], imag[1::2], sign)
    out_r, out_i = [None] * count, [None] * count
    half = count // 2
    for k in range(half):
        r, i = odd_r[k], odd_i[k]
        if k == 0:
            pass
        elif 4 * k == count:
            r, i = (-i, r) if sign > 0 else (i, -r)
        else:
            cos = math.cos(2.0 * math.pi * k / count)
            sin = sign * math.sin(2.0 * math.pi * k / count)
            if 8 * k == count or 8 * k == 3 * count:
                size = math.sqrt(0.5)
                up, across = cos / abs(cos), sin / abs(sin)
                first = r - i if up == across else r + i
                second = r + i if up == across else (i - r)
                if up > 0:
                    r, i = (first * size, second * size)
                else:
                    r, i = (first * -size, second * -size)
            else:
                r, i = r * cos - i * sin, r * sin + i * cos
        out_r[k], out_i[k] = even_r[k] + r, even_i[k] + i
        out_r[k + half], out_i[k + half] = even_r[k] - r, even_i[k] - i
    return out_r, out_i


def exact_dot(values, high, low):
    top = values.astype(jnp.bfloat16)
    rest = (values - top.astype(jnp.float32)).astype(jnp.bfloat16)
    dot = functools.partial(jnp.dot, preferred_element_type=jnp.float32)
    return dot(top, high) + (dot(rest, high) + dot(top, low))


def kernel(
    cells, columns,
    x_in, mats_in, sym_in, lanes_in, wall_cell_in, wall_count_in, wall_panel_in,
    out, loads,
    x_v, mats, sym, lanes, wall_cell, wall_count, wall_panel,
    packed, arrived, packed_back, arrived_back, state, halo_x, halo_y,
    spec, back, mine, others,
    in_sems, halo_send, halo_recv, swap_send, swap_recv, load_send, load_recv,
):
    nvx = columns // PARTS
    mid = nvx // 2
    me_c = lax.axis_index("cell")
    me_v = lax.axis_index("vel")

    pairs = [
        (x_in, x_v), (mats_in, mats), (sym_in, sym), (lanes_in, lanes),
        (wall_cell_in, wall_cell), (wall_count_in, wall_count), (wall_panel_in, wall_panel),
    ]
    loads_in = [pltpu.make_async_copy(src, dst, in_sems.at[n]) for n, (src, dst) in enumerate(pairs)]
    for copy in loads_in:
        copy.start()

    barrier = pltpu.get_barrier_semaphore()

    def greet_column(j, carry):
        to = lax.rem(me_v + j, columns)
        pl.semaphore_signal(barrier, inc=1, device_id=(me_c, to), device_id_type=MESH)
        return carry

    def greet_row(j, carry):
        to = lax.rem(me_c + j, cells)
        pl.semaphore_signal(barrier, inc=1, device_id=(to, me_v), device_id_type=MESH)
        return carry

    lax.fori_loop(1, columns, greet_column, 0)
    lax.fori_loop(1, cells, greet_row, 0)

    has_low_x, has_high_x = me_c > 0, me_c < cells - 1
    has_low_y, has_high_y = me_v > 0, me_v < columns - 1

    @pl.when(jnp.logical_not(has_low_x))
    def _():
        halo_x[:, :, mid:] = jnp.zeros((STEPS, 2, mid, NZ, LANES), jnp.float32)

    @pl.when(jnp.logical_not(has_high_x))
    def _():
        halo_x[:, :, :mid] = jnp.zeros((STEPS, 2, mid, NZ, LANES), jnp.float32)

    @pl.when(jnp.logical_not(has_low_y))
    def _():
        halo_y[:, 1] = jnp.zeros((STEPS, nvx, NZ, LANES), jnp.float32)

    @pl.when(jnp.logical_not(has_high_y))
    def _():
        halo_y[:, 0] = jnp.zeros((STEPS, nvx, NZ, LANES), jnp.float32)

    loads_in[0].wait()
    width = NZ * columns
    for start in range(0, width, LANES):
        stop = min(start + LANES, width)
        tile = x_v[:, 0, start:stop]
        shifted = jnp.concatenate([tile[:, NZ // 2 :], tile[:, : NZ // 2]], axis=1)
        turned = jnp.transpose(jnp.concatenate([tile, shifted], axis=0))
        turned = turned.reshape((stop - start) // NZ, NZ, LANES)
        packed[start // NZ : stop // NZ] = turned[:, : NZ // 2]
    arrived[pl.ds(me_v, 1)] = packed[pl.ds(me_v, 1)]

    pl.semaphore_wait(barrier, columns - 1 + cells - 1)

    def exchange(source, target, which):
        def send(j, carry):
            to = lax.rem(me_v + j, columns)
            pltpu.make_async_remote_copy(
                src_ref=source.at[to],
                dst_ref=target.at[me_v],
                send_sem=swap_send.at[which],
                recv_sem=swap_recv.at[which],
                device_id=(me_c, to),
                device_id_type=MESH,
            ).start()
            return carry

        lax.fori_loop(1, columns, send, 0)

    def arrivals(target, which):
        rest = target.at[pl.ds(0, columns - 1)]
        pltpu.make_async_copy(rest, rest, swap_recv.at[which]).wait()

    def departures(source, which):
        rest = source.at[pl.ds(0, columns - 1)]
        pltpu.make_async_copy(rest, rest, swap_send.at[which]).wait()

    exchange(packed, arrived, 0)
    for copy in loads_in[1:]:
        copy.wait()
    arrivals(arrived, 0)

    lane = lax.broadcasted_iota(jnp.int32, (1, 1, LANES), 2)
    used = lane < HALF
    quarter = LOCAL_V // 2

    def turn(values, by):
        return pltpu.roll(values, by, values.ndim - 1)

    blocks = arrived[...].reshape(nvx, PARTS, NZ // 2, LANES)
    wide = []
    for part in range(PARTS):
        block = blocks[:, part]
        wide.append(jnp.concatenate([block, turn(block, LOCAL_V)], axis=1))
    state[0, 0] = jnp.where(lane < LOCAL_V, wide[0], jnp.where(used, turn(wide[1], LOCAL_V), 0.0))
    state[0, 1] = jnp.where(
        lane < quarter, turn(wide[1], LANES - quarter), jnp.where(used, turn(wide[2], quarter), 0.0)
    )

    def halo_copies(step):
        routes = [
            (state.at[step, :, pl.ds(mid, mid)], halo_x.at[step, :, pl.ds(mid, mid)], (me_c + 1, me_v)),
            (state.at[step, :, pl.ds(0, mid)], halo_x.at[step, :, pl.ds(0, mid)], (me_c - 1, me_v)),
            (state.at[step, 1], halo_y.at[step, 1], (me_c, me_v + 1)),
            (state.at[step, 0], halo_y.at[step, 0], (me_c, me_v - 1)),
        ]
        return [
            pltpu.make_async_remote_copy(
                src_ref=src,
                dst_ref=dst,
                send_sem=halo_send.at[n, step],
                recv_sem=halo_recv.at[n, step],
                device_id=to,
                device_id_type=MESH,
            )
            for n, (src, dst, to) in enumerate(routes)
        ]

    sends = [has_high_x, has_low_x, has_high_y, has_low_y]
    receives = [has_low_x, has_high_x, has_low_y, has_high_y]

    def speed_x(a):
        return (2 * a - (nvx - 1)) * 0.5 * SPACING

    def advance(step, carry):
        copies = halo_copies(step)
        for copy, present in zip(copies, sends):
            pl.when(present)(copy.start)

        own = []
        for h in (0, 1):
            here = state[step, h]
            own.append(
                here * lanes[h]
                + pltpu.roll(here, 1, 1) * lanes[4]
                + pltpu.roll(here, NZ - 1, 1) * lanes[5]
            )

        for copy, present in zip(copies, receives):
            pl.when(present)(copy.wait_recv)

        moved = []
        for h in (0, 1):
            side = []
            for a in range(nvx):
                weight = COURANT * abs(speed_x(a))
                side.append(own[h][a] + (halo_x[step, h, a] - state[step, h, a]) * weight)
            moved.append(jnp.stack(side) + halo_y[step, h] * lanes[2 + h])
        rows = jnp.concatenate([side.reshape(nvx * NZ, LANES) for side in moved], axis=1)

        span = 2 * LANES
        plane = exact_dot(rows, mats[:span], mats[span : 2 * span]).reshape(nvx, NZ, span)
        real, imag = fourier(
            [plane[a, :, :LANES] for a in range(nvx)], [plane[a, :, LANES:] for a in range(nvx)], -1
        )
        spec[0] = jnp.stack(real)
        spec[1] = jnp.stack(imag)

        def weigh(w, carry):
            gains = [sym[w, pl.ds(a, 1), :] for a in range(nvx)]
            real, imag = fourier(
                [spec[0, a] * gains[a] for a in range(nvx)], [spec[1, a] * gains[a] for a in range(nvx)], 1
            )
            line = jnp.concatenate(
                [jnp.concatenate(real, axis=0), jnp.concatenate(imag, axis=0)], axis=1
            )
            back[w] = exact_dot(line, mats[2 * span : 3 * span], mats[3 * span :])
            return carry

        lax.fori_loop(0, KERNELS, weigh, 0, unroll=True)
        change = back[0] * back[2] + back[1] * back[3] - rows * back[4]
        after = rows + COLLISION_STEP * change
        for h in (0, 1):
            state[step + 1, h] = after[:, h * LANES : (h + 1) * LANES].reshape(nvx, NZ, LANES)
        return carry

    lax.fori_loop(0, STEPS, advance, 0)

    low, high = state[STEPS, 0], state[STEPS, 1]
    parts = [
        low,
        jnp.where(lane < quarter, turn(low, LOCAL_V), turn(high, quarter)),
        turn(high, LANES - quarter),
    ]
    stacked = [
        jnp.where(lane < LOCAL_V, part[:, : NZ // 2], turn(part, LOCAL_V)[:, NZ // 2 :]) for part in parts
    ]
    packed_back[...] = jnp.stack(stacked, axis=1).reshape(columns, NZ // 2, LANES)
    exchange(packed_back, arrived_back, 1)
    arrived_back[pl.ds(me_v, 1)] = packed_back[pl.ds(me_v, 1)]

    both = low + high
    sums_low, sums_high = jnp.sum(low, axis=0), jnp.sum(high, axis=0)
    along, squared = 0.0, 0.0
    for a in range(nvx):
        along = along + both[a] * (SPACING**3 * speed_x(a))
        squared = squared + both[a] * (SPACING**3 * speed_x(a) ** 2)
    totals = [
        along,
        sums_low * lanes[6] + sums_high * lanes[7],
        (sums_low + sums_high) * lanes[8],
        squared + sums_low * lanes[9] + sums_high * lanes[10],
    ]
    depth = lax.broadcasted_iota(jnp.int32, (NZ, LANES), 0)
    slot = lax.broadcasted_iota(jnp.int32, (NZ, LANES), 1)
    uses = jnp.zeros((NZ, LANES), jnp.float32)
    per_owner = PANEL_DEV * columns
    for n in range(WALL_SLOTS):
        panel = wall_panel[0, 0, n]
        target = panel // per_owner * PANEL_DEV + lax.rem(panel, PANEL_DEV)
        target = jnp.where(n < wall_count[0, 0], target, -1)
        hit = jnp.logical_and(depth == wall_cell[0, 0, n], slot == target)
        uses = uses + jnp.where(hit, 1.0, 0.0)
    shares = [
        jnp.sum(jnp.sum(total, axis=1, keepdims=True) * uses, axis=0, keepdims=True) for total in totals
    ]
    shares.append(jnp.zeros((NZ - MOMENTS, LANES), jnp.float32))
    share = jnp.concatenate(shares, axis=0)
    mine[...] = share
    others[pl.ds(me_c, 1)] = share[None]

    def give(j, carry):
        to = lax.rem(me_c + j, cells)
        pltpu.make_async_remote_copy(
            src_ref=mine,
            dst_ref=others.at[me_c],
            send_sem=load_send,
            recv_sem=load_recv,
            device_id=(to, me_v),
            device_id_type=MESH,
        ).start()
        return carry

    lax.fori_loop(1, cells, give, 0)

    rest = others.at[pl.ds(0, cells - 1)]
    pltpu.make_async_copy(rest, rest, load_recv).wait()
    summed = jnp.sum(others[...], axis=0)
    picked = slot - PANEL_DEV * me_c
    columns_out = [
        jnp.sum(jnp.where(picked == k, summed, 0.0), axis=1, keepdims=True) for k in range(PANEL_DEV)
    ]
    loads[...] = jnp.concatenate(columns_out, axis=1)[:MOMENTS]

    arrivals(arrived_back, 1)
    for start in range(0, columns, LANES // NZ):
        stop = min(start + LANES // NZ, columns)
        block = arrived_back[start:stop]
        tall = jnp.concatenate([block, turn(block, LOCAL_V)], axis=1).reshape((stop - start) * NZ, LANES)
        out[:, start * NZ : stop * NZ] = jnp.transpose(tall)[:LOCAL_V]

    departures(packed, 0)
    departures(packed_back, 1)
    pltpu.make_async_copy(rest, rest, load_send).wait()

    def finish(step, carry):
        for copy, present in zip(halo_copies(step), sends):
            pl.when(present)(copy.wait_send)
        return carry

    lax.fori_loop(0, STEPS, finish, 0)


def even_weights(gain_left, gain_right, loss_kernel):
    kernels = jnp.concatenate([gain_left, gain_right, loss_kernel[None]], axis=0)
    full = kernels.reshape(KERNELS, -1, NVY, NVZ)
    mirrored = full
    for axis in (1, 2, 3):
        mirrored = jnp.roll(jnp.flip(mirrored, axis), 1, axis)
    count = full.shape[1] * PLANE
    twice = np.full(KEPT, 2.0)
    twice[0] = twice[-1] = 1.0
    scale = jnp.asarray((0.5 * twice / count).astype(np.float32))
    kept = (full + mirrored)[..., :KEPT] * scale
    flat = kept.reshape(KERNELS, full.shape[1], NVY * KEPT)
    return jnp.pad(flat, ((0, 0), (0, 0), (0, LANES - NVY * KEPT)))


def per_device(cells, columns, distribution, gain_left, gain_right, loss_kernel, wall_cell, wall_count, wall_panel):
    nvx = columns // PARTS
    local, _, width = distribution.shape
    f32 = jnp.float32
    sym = even_weights(gain_left, gain_right, loss_kernel)
    mats = jnp.asarray(plane_matrices())
    tables = jnp.asarray(lane_tables())
    anywhere = pl.BlockSpec(memory_space=pl.ANY)
    in_vmem = pl.BlockSpec(memory_space=pltpu.VMEM)
    dma = pltpu.SemaphoreType.DMA
    out, loads = pl.pallas_call(
        functools.partial(kernel, cells, columns),
        out_shape=(
            jax.ShapeDtypeStruct((local, width), f32),
            jax.ShapeDtypeStruct((MOMENTS, PANEL_DEV), f32),
        ),
        in_specs=[anywhere] * 7,
        out_specs=(in_vmem, in_vmem),
        scratch_shapes=[
            pltpu.VMEM(distribution.shape, f32),
            pltpu.VMEM(mats.shape, jnp.bfloat16),
            pltpu.VMEM(sym.shape, f32),
            pltpu.VMEM(tables.shape, f32),
            pltpu.SMEM(wall_cell.shape, jnp.int32),
            pltpu.SMEM(wall_count.shape, jnp.int32),
            pltpu.SMEM(wall_panel.shape, jnp.int32),
            pltpu.VMEM((columns, NZ // 2, LANES), f32),
            pltpu.VMEM((columns, NZ // 2, LANES), f32),
            pltpu.VMEM((columns, NZ // 2, LANES), f32),
            pltpu.VMEM((columns, NZ // 2, LANES), f32),
            pltpu.VMEM((STEPS + 1, 2, nvx, NZ, LANES), f32),
            pltpu.VMEM((STEPS, 2, nvx, NZ, LANES), f32),
            pltpu.VMEM((STEPS, 2, nvx, NZ, LANES), f32),
            pltpu.VMEM((2, nvx, NZ, LANES), f32),
            pltpu.VMEM((KERNELS, nvx * NZ, 2 * LANES), f32),
            pltpu.VMEM((NZ, LANES), f32),
            pltpu.VMEM((cells, NZ, LANES), f32),
            dma((7,)),
            dma((4, STEPS)),
            dma((4, STEPS)),
            dma((2,)),
            dma((2,)),
            dma,
            dma,
        ],
        compiler_params=pltpu.CompilerParams(
            collective_id=0, has_side_effects=True, vmem_limit_bytes=32 * 1024 * 1024
        ),
        cost_estimate=pl.CostEstimate(flops=1_000_000_000, bytes_accessed=2_000_000, transcendentals=0),
        name="collide",
    )(distribution, mats, sym, tables, wall_cell, wall_count, wall_panel)
    return out.reshape(local, 1, width), loads


def solution(mesh):
    placed = (
        P("vel", "cell", None),
        P(),
        P(),
        P(),
        P("cell", "vel", None),
        P("cell", "vel"),
        P("cell", "vel", None),
    )
    return jax.shard_map(
        functools.partial(per_device, mesh.shape["cell"], mesh.shape["vel"]),
        mesh=mesh,
        in_specs=placed,
        out_specs=(P("vel", "cell", None), P(None, ("cell", "vel"))),
        check_vma=False,
    )
```

```python
import functools
import math

import jax
import jax.numpy as jnp
import ml_dtypes
import numpy as np
from jax import lax
from jax.experimental import pallas as pl
from jax.experimental.pallas import tpu as pltpu
from jax.sharding import PartitionSpec as P

NVY = 16
NVZ = 12
PLANE = NVY * NVZ
HALF = PLANE // 2
KEPT = NVZ // 2 + 1
KERNELS = 5
DIRS = 2
MOMENTS = 4
STEPS = 3
NZ = 8
WALL_SLOTS = 8
PANEL_DEV = 4
LOCAL_V = 64
PARTS = PLANE // LOCAL_V
LANES = 128
VMEM_LIMIT = 60 * 1024 * 1024

SPACING = 0.5
COURANT = 0.09
COLLISION_STEP = 0.3

MESH = pl.DeviceIdType.MESH


def split(values):
    high = values.astype(ml_dtypes.bfloat16)
    low = (values - high.astype(np.float64)).astype(ml_dtypes.bfloat16)
    return high, low


def plane_matrices():
    table = np.zeros((2 * LANES, 2 * LANES))
    for point in range(PLANE):
        b, c = divmod(point, NVZ)
        row = b // (NVY // 2) * LANES + point % HALF
        for kb in range(NVY):
            for kc in range(KEPT):
                angle = 2.0 * math.pi * ((b * kb % NVY) / NVY + (c * kc % NVZ) / NVZ)
                table[row, kb * KEPT + kc] = math.cos(angle)
                table[row, LANES + kb * KEPT + kc] = -math.sin(angle)
    high, low = split(table)
    return np.concatenate([high, low, high.T, low.T], axis=0)


def weight_selectors():
    table = np.zeros((2 * PLANE, 4 * LANES))
    for kb in range(NVY):
        for kc in range(KEPT):
            share = 0.5 if kc in (0, KEPT - 1) else 1.0
            column = kb * KEPT + kc
            there = kb * NVZ + kc
            mirror = -kb % NVY * NVZ + -kc % NVZ
            for half in (0, 1):
                table[half * PLANE + there, half * LANES + column] = share
                table[half * PLANE + mirror, (2 + half) * LANES + column] = share
    return table.astype(ml_dtypes.bfloat16)


def lane_tables():
    lane = np.arange(LANES)
    used = (lane < HALF).astype(np.float64)
    vz = (2 * (lane % NVZ) - (NVZ - 1)) * 0.5 * SPACING * used
    vy = [(2 * (lane // NVZ + h * NVY // 2) - (NVY - 1)) * 0.5 * SPACING * used for h in (0, 1)]
    z = np.arange(NZ)[:, None]
    rows = []
    for h in (0, 1):
        rows.append(1.0 - COURANT * (np.abs(vy[h]) + np.abs(vz)) + 0.0 * z)
    for h in (0, 1):
        rows.append(COURANT * np.abs(vy[h]) + 0.0 * z)
    rows.append(COURANT * np.maximum(vz, 0.0) * (z > 0))
    rows.append(COURANT * np.maximum(-vz, 0.0) * (z < NZ - 1))
    cube = SPACING**3
    rows.append(cube * vy[0] + 0.0 * z)
    rows.append(cube * vy[1] + 0.0 * z)
    rows.append(cube * vz + 0.0 * z)
    rows.append(cube * (vy[0] ** 2 + vz**2) + 0.0 * z)
    rows.append(cube * (vy[1] ** 2 + vz**2) + 0.0 * z)
    return np.stack(rows).astype(np.float32)


def fourier(real, imag, sign):
    count = len(real)
    if count == 1:
        return real, imag
    even_r, even_i = fourier(real[::2], imag[::2], sign)
    odd_r, odd_i = fourier(real[1::2], imag[1::2], sign)
    out_r, out_i = [None] * count, [None] * count
    half = count // 2
    for k in range(half):
        r, i = odd_r[k], odd_i[k]
        if k == 0:
            pass
        elif 4 * k == count:
            r, i = (-i, r) if sign > 0 else (i, -r)
        else:
            cos = math.cos(2.0 * math.pi * k / count)
            sin = sign * math.sin(2.0 * math.pi * k / count)
            if 8 * k == count or 8 * k == 3 * count:
                size = math.sqrt(0.5)
                up, across = cos / abs(cos), sin / abs(sin)
                first = r - i if up == across else r + i
                second = r + i if up == across else (i - r)
                if up > 0:
                    r, i = (first * size, second * size)
                else:
                    r, i = (first * -size, second * -size)
            else:
                r, i = r * cos - i * sin, r * sin + i * cos
        out_r[k], out_i[k] = even_r[k] + r, even_i[k] + i
        out_r[k + half], out_i[k + half] = even_r[k] - r, even_i[k] - i
    return out_r, out_i


def exact_dot(values, high, low):
    top = values.astype(jnp.bfloat16)
    rest = (values - top.astype(jnp.float32)).astype(jnp.bfloat16)
    dot = functools.partial(jnp.dot, preferred_element_type=jnp.float32)
    return dot(top, high) + (dot(rest, high) + dot(top, low))


def kernel(
    cells, columns,
    x_in, wall_cell_in, wall_count_in, wall_panel_in, left_in, right_in, loss_in, picks_in, mats_in, lanes_in,
    out, loads,
    x_v, wall_cell, wall_count, wall_panel, left, right, loss, picks, mats, lanes,
    packed, arrived, packed_back, arrived_back, state, halo_x, halo_y,
    planes, sym, spec, back, my_uses, uses, mine, others,
    in_sems, halo_send, halo_recv, swap_send, swap_recv, load_send, load_recv, uses_send, uses_recv,
):
    nvx = columns // PARTS
    mid = nvx // 2
    me_c = lax.axis_index("cell")
    me_v = lax.axis_index("vel")

    lines = 4 if columns % 4 == 0 else 2
    ring = columns // lines

    def owner_of(column):
        line, place = column // ring, lax.rem(column, ring)
        return line * ring + lax.rem(place + 1 - line + ring, ring)

    def column_of(device):
        line, place = device // ring, lax.rem(device, ring)
        return line * ring + lax.rem(place - 1 + line + ring, ring)

    me_y = column_of(me_v)
    my_owner = owner_of(me_v)
    line, place = me_v // ring, lax.rem(me_v, ring)

    def descending(n, count):
        half = (n + 1) // 2
        return lax.rem(count // 2 + jnp.where(lax.rem(n, 2) == 1, half, -half), count)

    def partner(j):
        there = lax.rem(place + descending(j // lines, ring), ring)
        return lax.rem(line + descending(lax.rem(j, lines), lines), lines) * ring + there

    pairs = [
        (x_in, x_v), (wall_cell_in, wall_cell), (wall_count_in, wall_count), (wall_panel_in, wall_panel),
        (left_in, left), (right_in, right), (loss_in, loss), (picks_in, picks), (mats_in, mats), (lanes_in, lanes),
    ]
    loads_in = [pltpu.make_async_copy(src, dst, in_sems.at[n]) for n, (src, dst) in enumerate(pairs)]
    for copy in loads_in:
        copy.start()

    barrier = pltpu.get_barrier_semaphore()

    def greet_column(j, carry):
        pl.semaphore_signal(barrier, inc=1, device_id=(me_c, partner(j)), device_id_type=MESH)
        return carry

    def greet_row(j, carry):
        to = lax.rem(me_c + j, cells)
        pl.semaphore_signal(barrier, inc=1, device_id=(to, my_owner), device_id_type=MESH)
        return carry

    has_low_x, has_high_x = me_c > 0, me_c < cells - 1
    has_low_y, has_high_y = me_y > 0, me_y < columns - 1
    moved_home = my_owner != me_v
    greetings = [(jnp.logical_and(moved_home, has_low_x), -1), (jnp.logical_and(moved_home, has_high_x), 1)]

    lax.fori_loop(0, columns - 1, greet_column, 0)
    lax.fori_loop(1, cells, greet_row, 0)
    greeted = columns - 1 + cells - 1
    for present, way in greetings:
        greeted = greeted + jnp.where(present, 1, 0)

        @pl.when(present)
        def _():
            pl.semaphore_signal(barrier, inc=1, device_id=(me_c + way, me_v), device_id_type=MESH)

    loads_in[0].wait()
    width = NZ * columns
    for start in range(0, width, LANES):
        stop = min(start + LANES, width)
        tile = x_v[:, 0, start:stop]
        shifted = jnp.concatenate([tile[:, NZ // 2 :], tile[:, : NZ // 2]], axis=1)
        turned = jnp.transpose(jnp.concatenate([tile, shifted], axis=0))
        turned = turned.reshape((stop - start) // NZ, NZ, LANES)
        packed[start // NZ : stop // NZ] = turned[:, : NZ // 2]
    arrived[pl.ds(me_v, 1)] = packed[pl.ds(me_y, 1)]

    depth = lax.broadcasted_iota(jnp.int32, (NZ, LANES), 0)
    slot = lax.broadcasted_iota(jnp.int32, (NZ, LANES), 1)
    for copy in loads_in[1:4]:
        copy.wait()
    counted = jnp.zeros((NZ, LANES), jnp.float32)
    per_owner = PANEL_DEV * columns
    for n in range(WALL_SLOTS):
        panel = wall_panel[0, 0, n]
        target = panel // per_owner * PANEL_DEV + lax.rem(panel, PANEL_DEV)
        target = jnp.where(n < wall_count[0, 0], target, -1)
        hit = jnp.logical_and(depth == wall_cell[0, 0, n], slot == target)
        counted = counted + jnp.where(hit, 1.0, 0.0)
    my_uses[...] = counted

    @pl.when(jnp.logical_not(moved_home))
    def _():
        uses[...] = counted

    pl.semaphore_wait(barrier, greeted)

    def exchange(source, target, which, source_slot, target_slot):
        def send(j, carry):
            to = partner(j)
            pltpu.make_async_remote_copy(
                src_ref=source.at[source_slot(to)],
                dst_ref=target.at[target_slot],
                send_sem=swap_send.at[which],
                recv_sem=swap_recv.at[which],
                device_id=(me_c, to),
                device_id_type=MESH,
            ).start()
            return carry

        lax.fori_loop(0, columns - 1, send, 0)

    def arrivals(target, which):
        rest = target.at[pl.ds(0, columns - 1)]
        pltpu.make_async_copy(rest, rest, swap_recv.at[which]).wait()

    def departures(source, which):
        rest = source.at[pl.ds(0, columns - 1)]
        pltpu.make_async_copy(rest, rest, swap_send.at[which]).wait()

    exchange(packed, arrived, 0, column_of, me_v)

    uses_copy = pltpu.make_async_remote_copy(
        src_ref=my_uses,
        dst_ref=uses,
        send_sem=uses_send,
        recv_sem=uses_recv,
        device_id=(me_c, my_owner),
        device_id_type=MESH,
    )
    pl.when(moved_home)(uses_copy.start)

    @pl.when(jnp.logical_not(has_low_x))
    def _():
        halo_x[:, :, mid:] = jnp.zeros((STEPS, 2, mid, NZ, LANES), jnp.float32)

    @pl.when(jnp.logical_not(has_high_x))
    def _():
        halo_x[:, :, :mid] = jnp.zeros((STEPS, 2, mid, NZ, LANES), jnp.float32)

    @pl.when(jnp.logical_not(has_low_y))
    def _():
        halo_y[:, 1] = jnp.zeros((STEPS, nvx, NZ, LANES), jnp.float32)

    @pl.when(jnp.logical_not(has_high_y))
    def _():
        halo_y[:, 0] = jnp.zeros((STEPS, nvx, NZ, LANES), jnp.float32)

    for copy in loads_in[4:]:
        copy.wait()
    for pair in range(nvx // 2):
        span = slice(pair * 2 * PLANE, (pair + 1) * 2 * PLANE)
        planes[pair, :DIRS] = left[:, span]
        planes[pair, DIRS : 2 * DIRS] = right[:, span]
        planes[pair, 2 * DIRS : KERNELS] = loss[:, span]
        planes[pair, KERNELS:] = jnp.zeros((NZ - KERNELS, 2 * PLANE), jnp.float32)
    remaining = planes[...].reshape(nvx // 2 * NZ, 2 * PLANE)
    chosen = 0.0
    for _ in range(3):
        top = remaining.astype(jnp.bfloat16)
        chosen = chosen + jnp.dot(top, picks[...], preferred_element_type=jnp.float32)
        remaining = remaining - top.astype(jnp.float32)
    chosen = (chosen * (1.0 / (nvx * PLANE))).reshape(nvx // 2, NZ, 4 * LANES)
    for a in range(nvx):
        b = -a % nvx
        near, far = a % 2 * LANES, (2 + b % 2) * LANES
        sym[a] = chosen[a // 2, :, near : near + LANES] + chosen[b // 2, :, far : far + LANES]

    arrivals(arrived, 0)

    lane = lax.broadcasted_iota(jnp.int32, (1, 1, LANES), 2)
    used = lane < HALF
    quarter = LOCAL_V // 2

    def turn(values, by):
        return pltpu.roll(values, by, values.ndim - 1)

    blocks = arrived[...].reshape(nvx, PARTS, NZ // 2, LANES)
    wide = []
    for part in range(PARTS):
        block = blocks[:, part]
        wide.append(jnp.concatenate([block, turn(block, LOCAL_V)], axis=1))
    state[0, 0] = jnp.where(lane < LOCAL_V, wide[0], jnp.where(used, turn(wide[1], LOCAL_V), 0.0))
    state[0, 1] = jnp.where(
        lane < quarter, turn(wide[1], LANES - quarter), jnp.where(used, turn(wide[2], quarter), 0.0)
    )

    def halo_copies(step):
        routes = [
            (state.at[step, :, pl.ds(mid, mid)], halo_x.at[step, :, pl.ds(mid, mid)], (me_c + 1, me_v)),
            (state.at[step, :, pl.ds(0, mid)], halo_x.at[step, :, pl.ds(0, mid)], (me_c - 1, me_v)),
            (state.at[step, 1], halo_y.at[step, 1], (me_c, owner_of(me_y + 1))),
            (state.at[step, 0], halo_y.at[step, 0], (me_c, owner_of(me_y - 1))),
        ]
        return [
            pltpu.make_async_remote_copy(
                src_ref=src,
                dst_ref=dst,
                send_sem=halo_send.at[n, step],
                recv_sem=halo_recv.at[n, step],
                device_id=to,
                device_id_type=MESH,
            )
            for n, (src, dst, to) in enumerate(routes)
        ]

    sends = [has_high_x, has_low_x, has_high_y, has_low_y]
    receives = [has_low_x, has_high_x, has_low_y, has_high_y]

    def speed_x(a):
        return (2 * a - (nvx - 1)) * 0.5 * SPACING

    def advance(step, carry):
        copies = halo_copies(step)
        for copy, present in zip(copies, sends):
            pl.when(present)(copy.start)

        own = []
        for h in (0, 1):
            here = state[step, h]
            own.append(
                here * lanes[h]
                + pltpu.roll(here, 1, 1) * lanes[4]
                + pltpu.roll(here, NZ - 1, 1) * lanes[5]
            )

        for copy, present in zip(copies, receives):
            pl.when(present)(copy.wait_recv)

        moved = []
        for h in (0, 1):
            side = []
            for a in range(nvx):
                weight = COURANT * abs(speed_x(a))
                side.append(own[h][a] + (halo_x[step, h, a] - state[step, h, a]) * weight)
            moved.append(jnp.stack(side) + halo_y[step, h] * lanes[2 + h])
        rows = jnp.concatenate([side.reshape(nvx * NZ, LANES) for side in moved], axis=1)

        span = 2 * LANES
        plane = exact_dot(rows, mats[:span], mats[span : 2 * span]).reshape(nvx, NZ, span)
        real, imag = fourier(
            [plane[a, :, :LANES] for a in range(nvx)], [plane[a, :, LANES:] for a in range(nvx)], -1
        )
        spec[0] = jnp.stack(real)
        spec[1] = jnp.stack(imag)

        def weigh(w, carry):
            gains = [sym[a, pl.ds(w, 1), :] for a in range(nvx)]
            real, imag = fourier(
                [spec[0, a] * gains[a] for a in range(nvx)], [spec[1, a] * gains[a] for a in range(nvx)], 1
            )
            line = jnp.concatenate(
                [jnp.concatenate(real, axis=0), jnp.concatenate(imag, axis=0)], axis=1
            )
            back[w] = exact_dot(line, mats[2 * span : 3 * span], mats[3 * span :])
            return carry

        lax.fori_loop(0, KERNELS, weigh, 0, unroll=True)
        change = back[0] * back[2] + back[1] * back[3] - rows * back[4]
        after = rows + COLLISION_STEP * change
        for h in (0, 1):
            state[step + 1, h] = after[:, h * LANES : (h + 1) * LANES].reshape(nvx, NZ, LANES)
        return carry

    lax.fori_loop(0, STEPS, advance, 0)

    low, high = state[STEPS, 0], state[STEPS, 1]
    parts = [
        low,
        jnp.where(lane < quarter, turn(low, LOCAL_V), turn(high, quarter)),
        turn(high, LANES - quarter),
    ]
    stacked = [
        jnp.where(lane < LOCAL_V, part[:, : NZ // 2], turn(part, LOCAL_V)[:, NZ // 2 :]) for part in parts
    ]
    packed_back[...] = jnp.stack(stacked, axis=1).reshape(columns, NZ // 2, LANES)
    exchange(packed_back, arrived_back, 1, lambda to: to, me_y)
    arrived_back[pl.ds(me_y, 1)] = packed_back[pl.ds(me_v, 1)]

    both = low + high
    sums_low, sums_high = jnp.sum(low, axis=0), jnp.sum(high, axis=0)
    along, squared = 0.0, 0.0
    for a in range(nvx):
        along = along + both[a] * (SPACING**3 * speed_x(a))
        squared = squared + both[a] * (SPACING**3 * speed_x(a) ** 2)
    totals = [
        along,
        sums_low * lanes[6] + sums_high * lanes[7],
        (sums_low + sums_high) * lanes[8],
        squared + sums_low * lanes[9] + sums_high * lanes[10],
    ]
    pl.when(moved_home)(uses_copy.wait_recv)
    counted = uses[...]
    shares = [
        jnp.sum(jnp.sum(total, axis=1, keepdims=True) * counted, axis=0, keepdims=True) for total in totals
    ]
    shares.append(jnp.zeros((NZ - MOMENTS, LANES), jnp.float32))
    share = jnp.concatenate(shares, axis=0)
    mine[...] = share
    all_others, rest = others.at[pl.ds(0, cells)], others.at[pl.ds(0, cells - 1)]

    def give(j, carry):
        to = lax.rem(me_c + j, cells)
        pltpu.make_async_remote_copy(
            src_ref=mine,
            dst_ref=others.at[me_c],
            send_sem=load_send,
            recv_sem=load_recv,
            device_id=(to, me_y),
            device_id_type=MESH,
        ).start()
        return carry

    lax.fori_loop(1, cells, give, 0)

    @pl.when(moved_home)
    def _():
        give(0, 0)
        pltpu.make_async_copy(all_others, all_others, load_recv).wait()

    @pl.when(jnp.logical_not(moved_home))
    def _():
        others[pl.ds(me_c, 1)] = share[None]
        pltpu.make_async_copy(rest, rest, load_recv).wait()

    summed = jnp.sum(others[...], axis=0)
    picked = slot - PANEL_DEV * me_c
    columns_out = [
        jnp.sum(jnp.where(picked == k, summed, 0.0), axis=1, keepdims=True) for k in range(PANEL_DEV)
    ]
    loads[...] = jnp.concatenate(columns_out, axis=1)[:MOMENTS]

    arrivals(arrived_back, 1)
    for start in range(0, columns, LANES // NZ):
        stop = min(start + LANES // NZ, columns)
        block = arrived_back[start:stop]
        tall = jnp.concatenate([block, turn(block, LOCAL_V)], axis=1).reshape((stop - start) * NZ, LANES)
        out[:, 0, start * NZ : stop * NZ] = jnp.transpose(tall)[:LOCAL_V]

    departures(packed, 0)
    departures(packed_back, 1)
    pl.when(moved_home)(uses_copy.wait_send)
    pl.when(moved_home)(pltpu.make_async_copy(all_others, all_others, load_send).wait)
    pl.when(jnp.logical_not(moved_home))(pltpu.make_async_copy(rest, rest, load_send).wait)

    def finish(step, carry):
        for copy, present in zip(halo_copies(step), sends):
            pl.when(present)(copy.wait_send)
        return carry

    lax.fori_loop(0, STEPS, finish, 0)


def per_device(cells, columns, distribution, gain_left, gain_right, loss_kernel, wall_cell, wall_count, wall_panel):
    nvx = columns // PARTS
    local, _, width = distribution.shape
    f32 = jnp.float32
    loss = loss_kernel.reshape(1, -1)
    picks = jnp.asarray(weight_selectors())
    mats = jnp.asarray(plane_matrices())
    tables = jnp.asarray(lane_tables())
    anywhere = pl.BlockSpec(memory_space=pl.ANY)
    in_vmem = pl.BlockSpec(memory_space=pltpu.VMEM)
    dma = pltpu.SemaphoreType.DMA
    out, loads = pl.pallas_call(
        functools.partial(kernel, cells, columns),
        out_shape=(
            jax.ShapeDtypeStruct((local, 1, width), f32),
            jax.ShapeDtypeStruct((MOMENTS, PANEL_DEV), f32),
        ),
        in_specs=[anywhere] * 10,
        out_specs=(in_vmem, in_vmem),
        scratch_shapes=[
            pltpu.VMEM(distribution.shape, f32),
            pltpu.SMEM(wall_cell.shape, jnp.int32),
            pltpu.SMEM(wall_count.shape, jnp.int32),
            pltpu.SMEM(wall_panel.shape, jnp.int32),
            pltpu.VMEM(gain_left.shape, f32),
            pltpu.VMEM(gain_right.shape, f32),
            pltpu.VMEM(loss.shape, f32),
            pltpu.VMEM(picks.shape, jnp.bfloat16),
            pltpu.VMEM(mats.shape, jnp.bfloat16),
            pltpu.VMEM(tables.shape, f32),
            pltpu.VMEM((columns, NZ // 2, LANES), f32),
            pltpu.VMEM((columns, NZ // 2, LANES), f32),
            pltpu.VMEM((columns, NZ // 2, LANES), f32),
            pltpu.VMEM((columns, NZ // 2, LANES), f32),
            pltpu.VMEM((STEPS + 1, 2, nvx, NZ, LANES), f32),
            pltpu.VMEM((STEPS, 2, nvx, NZ, LANES), f32),
            pltpu.VMEM((STEPS, 2, nvx, NZ, LANES), f32),
            pltpu.VMEM((nvx // 2, NZ, 2 * PLANE), f32),
            pltpu.VMEM((nvx, NZ, LANES), f32),
            pltpu.VMEM((2, nvx, NZ, LANES), f32),
            pltpu.VMEM((KERNELS, nvx * NZ, 2 * LANES), f32),
            pltpu.VMEM((NZ, LANES), f32),
            pltpu.VMEM((NZ, LANES), f32),
            pltpu.VMEM((NZ, LANES), f32),
            pltpu.VMEM((cells, NZ, LANES), f32),
            dma((10,)),
            dma((4, STEPS)),
            dma((4, STEPS)),
            dma((2,)),
            dma((2,)),
            dma,
            dma,
            dma,
            dma,
        ],
        compiler_params=pltpu.CompilerParams(
            collective_id=0, has_side_effects=True, vmem_limit_bytes=VMEM_LIMIT
        ),
        cost_estimate=pl.CostEstimate(flops=1_000_000_000, bytes_accessed=2_000_000, transcendentals=0),
        name="collide",
    )(distribution, wall_cell, wall_count, wall_panel, gain_left, gain_right, loss, picks, mats, tables)
    return out, loads


def solution(mesh):
    placed = (
        P("vel", "cell", None),
        P(),
        P(),
        P(),
        P("cell", "vel", None),
        P("cell", "vel"),
        P("cell", "vel", None),
    )
    return jax.shard_map(
        functools.partial(per_device, mesh.shape["cell"], mesh.shape["vel"]),
        mesh=mesh,
        in_specs=placed,
        out_specs=(P("vel", "cell", None), P(None, ("cell", "vel"))),
        check_vma=False,
    )
```

```python
import functools
import math

import jax
import jax.numpy as jnp
import ml_dtypes
import numpy as np
from jax import lax
from jax.experimental import pallas as pl
from jax.experimental.pallas import tpu as pltpu
from jax.sharding import PartitionSpec as P

NVY = 16
NVZ = 12
PLANE = NVY * NVZ
HALF = PLANE // 2
KEPT = NVZ // 2 + 1
KERNELS = 5
DIRS = 2
MOMENTS = 4
STEPS = 3
NZ = 8
WALL_SLOTS = 8
PANEL_DEV = 4
LOCAL_V = 64
PARTS = PLANE // LOCAL_V
LANES = 128
VMEM_LIMIT = 60 * 1024 * 1024

SPACING = 0.5
COURANT = 0.09
COLLISION_STEP = 0.3

MESH = pl.DeviceIdType.MESH


def split(values):
    high = values.astype(ml_dtypes.bfloat16)
    low = (values - high.astype(np.float64)).astype(ml_dtypes.bfloat16)
    return high, low


def plane_matrices():
    table = np.zeros((2 * LANES, 2 * LANES))
    for point in range(PLANE):
        b, c = divmod(point, NVZ)
        row = b // (NVY // 2) * LANES + point % HALF
        for kb in range(NVY):
            for kc in range(KEPT):
                angle = 2.0 * math.pi * ((b * kb % NVY) / NVY + (c * kc % NVZ) / NVZ)
                table[row, kb * KEPT + kc] = math.cos(angle)
                table[row, LANES + kb * KEPT + kc] = -math.sin(angle)
    high, low = split(table)
    return np.concatenate([high, low, high.T, low.T], axis=0)


def weight_selectors():
    table = np.zeros((2 * PLANE, 4 * LANES))
    for kb in range(NVY):
        for kc in range(KEPT):
            share = 0.5 if kc in (0, KEPT - 1) else 1.0
            column = kb * KEPT + kc
            there = kb * NVZ + kc
            mirror = -kb % NVY * NVZ + -kc % NVZ
            for half in (0, 1):
                table[half * PLANE + there, half * LANES + column] = share
                table[half * PLANE + mirror, (2 + half) * LANES + column] = share
    return table.astype(ml_dtypes.bfloat16)


def lane_tables():
    lane = np.arange(LANES)
    used = (lane < HALF).astype(np.float64)
    vz = (2 * (lane % NVZ) - (NVZ - 1)) * 0.5 * SPACING * used
    vy = [(2 * (lane // NVZ + h * NVY // 2) - (NVY - 1)) * 0.5 * SPACING * used for h in (0, 1)]
    z = np.arange(NZ)[:, None]
    rows = []
    for h in (0, 1):
        rows.append(1.0 - COURANT * (np.abs(vy[h]) + np.abs(vz)) + 0.0 * z)
    for h in (0, 1):
        rows.append(COURANT * np.abs(vy[h]) + 0.0 * z)
    rows.append(COURANT * np.maximum(vz, 0.0) * (z > 0))
    rows.append(COURANT * np.maximum(-vz, 0.0) * (z < NZ - 1))
    cube = SPACING**3
    rows.append(cube * vy[0] + 0.0 * z)
    rows.append(cube * vy[1] + 0.0 * z)
    rows.append(cube * vz + 0.0 * z)
    rows.append(cube * (vy[0] ** 2 + vz**2) + 0.0 * z)
    rows.append(cube * (vy[1] ** 2 + vz**2) + 0.0 * z)
    return np.stack(rows).astype(np.float32)


def fourier(real, imag, sign):
    count = len(real)
    if count == 1:
        return real, imag
    even_r, even_i = fourier(real[::2], imag[::2], sign)
    odd_r, odd_i = fourier(real[1::2], imag[1::2], sign)
    out_r, out_i = [None] * count, [None] * count
    half = count // 2
    for k in range(half):
        r, i = odd_r[k], odd_i[k]
        if k == 0:
            pass
        elif 4 * k == count:
            r, i = (-i, r) if sign > 0 else (i, -r)
        else:
            cos = math.cos(2.0 * math.pi * k / count)
            sin = sign * math.sin(2.0 * math.pi * k / count)
            if 8 * k == count or 8 * k == 3 * count:
                size = math.sqrt(0.5)
                up, across = cos / abs(cos), sin / abs(sin)
                first = r - i if up == across else r + i
                second = r + i if up == across else (i - r)
                if up > 0:
                    r, i = (first * size, second * size)
                else:
                    r, i = (first * -size, second * -size)
            else:
                r, i = r * cos - i * sin, r * sin + i * cos
        out_r[k], out_i[k] = even_r[k] + r, even_i[k] + i
        out_r[k + half], out_i[k + half] = even_r[k] - r, even_i[k] - i
    return out_r, out_i


def exact_dot(values, high, low):
    top = values.astype(jnp.bfloat16)
    rest = (values - top.astype(jnp.float32)).astype(jnp.bfloat16)
    dot = functools.partial(jnp.dot, preferred_element_type=jnp.float32)
    return dot(top, high) + (dot(rest, high) + dot(top, low))


def kernel(
    cells, columns,
    x_in, wall_cell_in, wall_count_in, wall_panel_in, left_in, right_in, loss_in, picks_in, mats_in, lanes_in,
    out, loads,
    x_v, wall_cell, wall_count, wall_panel, left, right, loss, picks, mats, lanes,
    packed, arrived, packed_back, arrived_back, state, halo_x, halo_y,
    planes, sym, spec, back, my_uses, uses, mine, others,
    in_sems, halo_send, halo_recv, swap_send, swap_recv, load_send, load_recv, uses_send, uses_recv,
):
    nvx = columns // PARTS
    mid = nvx // 2
    me_c = lax.axis_index("cell")
    me_v = lax.axis_index("vel")

    lines = 4 if columns % 4 == 0 else 2
    ring = columns // lines

    def owner_of(column):
        line, place = column // ring, lax.rem(column, ring)
        return line * ring + lax.rem(place + 1 - line + ring, ring)

    def column_of(device):
        line, place = device // ring, lax.rem(device, ring)
        return line * ring + lax.rem(place - 1 + line + ring, ring)

    me_y = column_of(me_v)
    my_owner = owner_of(me_v)
    line, place = me_v // ring, lax.rem(me_v, ring)

    def for_partners(visit, start, stop):
        def visit_round(n, shift, count):
            there = lax.rem(place + shift, ring)
            for m in range(count):
                across = lines // 2 + (m + 1) // 2 * (1 if m % 2 else -1)
                to_line = lax.rem(line + across, lines)
                visit(to_line * ring + there, to_line * ring + lax.rem(there - 1 + to_line + ring, ring))

        def one_round(n, carry):
            half = (n + 1) // 2
            visit_round(n, ring // 2 + jnp.where(lax.rem(n, 2) == 1, half, -half), lines)
            return carry

        lax.fori_loop(start, min(stop, ring - 1), one_round, 0)
        if stop == ring:
            visit_round(ring - 1, 0, lines - 1)

    pairs = [
        (x_in, x_v), (wall_cell_in, wall_cell), (wall_count_in, wall_count), (wall_panel_in, wall_panel),
        (left_in, left), (right_in, right), (loss_in, loss), (picks_in, picks), (mats_in, mats), (lanes_in, lanes),
    ]
    loads_in = [pltpu.make_async_copy(src, dst, in_sems.at[n]) for n, (src, dst) in enumerate(pairs)]
    for copy in loads_in:
        copy.start()

    barrier = pltpu.get_barrier_semaphore()

    def greet_column(to, column):
        pl.semaphore_signal(barrier, inc=1, device_id=(me_c, to), device_id_type=MESH)

    def greet_row(j, carry):
        to = lax.rem(me_c + j, cells)
        pl.semaphore_signal(barrier, inc=1, device_id=(to, my_owner), device_id_type=MESH)
        return carry

    has_low_x, has_high_x = me_c > 0, me_c < cells - 1
    has_low_y, has_high_y = me_y > 0, me_y < columns - 1
    moved_home = my_owner != me_v
    greetings = [(jnp.logical_and(moved_home, has_low_x), -1), (jnp.logical_and(moved_home, has_high_x), 1)]

    for_partners(greet_column, 0, ring)
    lax.fori_loop(1, cells, greet_row, 0)
    greeted = columns - 1 + cells - 1
    for present, way in greetings:
        greeted = greeted + jnp.where(present, 1, 0)

        @pl.when(present)
        def _():
            pl.semaphore_signal(barrier, inc=1, device_id=(me_c + way, me_v), device_id_type=MESH)

    loads_in[0].wait()
    width = NZ * columns
    for start in range(0, width, LANES):
        stop = min(start + LANES, width)
        tile = x_v[:, 0, start:stop]
        shifted = jnp.concatenate([tile[:, NZ // 2 :], tile[:, : NZ // 2]], axis=1)
        turned = jnp.transpose(jnp.concatenate([tile, shifted], axis=0))
        turned = turned.reshape((stop - start) // NZ, NZ, LANES)
        packed[start // NZ : stop // NZ] = turned[:, : NZ // 2]
    arrived[pl.ds(me_v, 1)] = packed[pl.ds(me_y, 1)]

    depth = lax.broadcasted_iota(jnp.int32, (NZ, LANES), 0)
    slot = lax.broadcasted_iota(jnp.int32, (NZ, LANES), 1)
    for copy in loads_in[1:4]:
        copy.wait()
    counted = jnp.zeros((NZ, LANES), jnp.float32)
    per_owner = PANEL_DEV * columns
    for n in range(WALL_SLOTS):
        panel = wall_panel[0, 0, n]
        target = panel // per_owner * PANEL_DEV + lax.rem(panel, PANEL_DEV)
        target = jnp.where(n < wall_count[0, 0], target, -1)
        hit = jnp.logical_and(depth == wall_cell[0, 0, n], slot == target)
        counted = counted + jnp.where(hit, 1.0, 0.0)
    my_uses[...] = counted

    @pl.when(jnp.logical_not(moved_home))
    def _():
        uses[...] = counted

    pl.semaphore_wait(barrier, greeted)

    def exchange(source, target, which, by_column, target_slot, start, stop):
        def send(to, column):
            pltpu.make_async_remote_copy(
                src_ref=source.at[column if by_column else to],
                dst_ref=target.at[target_slot],
                send_sem=swap_send.at[which],
                recv_sem=swap_recv.at[which],
                device_id=(me_c, to),
                device_id_type=MESH,
            ).start()

        for_partners(send, start, stop)

    def arrivals(target, which):
        rest = target.at[pl.ds(0, columns - 1)]
        pltpu.make_async_copy(rest, rest, swap_recv.at[which]).wait()

    def departures(source, which):
        rest = source.at[pl.ds(0, columns - 1)]
        pltpu.make_async_copy(rest, rest, swap_send.at[which]).wait()

    exchange(packed, arrived, 0, True, me_v, 0, ring)

    uses_copy = pltpu.make_async_remote_copy(
        src_ref=my_uses,
        dst_ref=uses,
        send_sem=uses_send,
        recv_sem=uses_recv,
        device_id=(me_c, my_owner),
        device_id_type=MESH,
    )
    pl.when(moved_home)(uses_copy.start)

    @pl.when(jnp.logical_not(has_low_x))
    def _():
        halo_x[:, :, mid:] = jnp.zeros((STEPS, 2, mid, NZ, LANES), jnp.float32)

    @pl.when(jnp.logical_not(has_high_x))
    def _():
        halo_x[:, :, :mid] = jnp.zeros((STEPS, 2, mid, NZ, LANES), jnp.float32)

    @pl.when(jnp.logical_not(has_low_y))
    def _():
        halo_y[:, 1] = jnp.zeros((STEPS, nvx, NZ, LANES), jnp.float32)

    @pl.when(jnp.logical_not(has_high_y))
    def _():
        halo_y[:, 0] = jnp.zeros((STEPS, nvx, NZ, LANES), jnp.float32)

    for copy in loads_in[4:]:
        copy.wait()
    for pair in range(nvx // 2):
        span = slice(pair * 2 * PLANE, (pair + 1) * 2 * PLANE)
        planes[pair, :DIRS] = left[:, span]
        planes[pair, DIRS : 2 * DIRS] = right[:, span]
        planes[pair, 2 * DIRS : KERNELS] = loss[:, span]
        planes[pair, KERNELS:] = jnp.zeros((NZ - KERNELS, 2 * PLANE), jnp.float32)
    remaining = planes[...].reshape(nvx // 2 * NZ, 2 * PLANE)
    chosen = 0.0
    for _ in range(3):
        top = remaining.astype(jnp.bfloat16)
        chosen = chosen + jnp.dot(top, picks[...], preferred_element_type=jnp.float32)
        remaining = remaining - top.astype(jnp.float32)
    chosen = (chosen * (1.0 / (nvx * PLANE))).reshape(nvx // 2, NZ, 4 * LANES)
    for a in range(nvx):
        b = -a % nvx
        near, far = a % 2 * LANES, (2 + b % 2) * LANES
        sym[a] = chosen[a // 2, :, near : near + LANES] + chosen[b // 2, :, far : far + LANES]

    arrivals(arrived, 0)

    lane = lax.broadcasted_iota(jnp.int32, (1, 1, LANES), 2)
    used = lane < HALF
    quarter = LOCAL_V // 2

    def turn(values, by):
        return pltpu.roll(values, by, values.ndim - 1)

    blocks = arrived[...].reshape(nvx, PARTS, NZ // 2, LANES)
    wide = []
    for part in range(PARTS):
        block = blocks[:, part]
        wide.append(jnp.concatenate([block, turn(block, LOCAL_V)], axis=1))
    state[0, 0] = jnp.where(lane < LOCAL_V, wide[0], jnp.where(used, turn(wide[1], LOCAL_V), 0.0))
    state[0, 1] = jnp.where(
        lane < quarter, turn(wide[1], LANES - quarter), jnp.where(used, turn(wide[2], quarter), 0.0)
    )

    def halo_copies(step):
        routes = [
            (state.at[step, :, pl.ds(mid, mid)], halo_x.at[step, :, pl.ds(mid, mid)], (me_c + 1, me_v)),
            (state.at[step, :, pl.ds(0, mid)], halo_x.at[step, :, pl.ds(0, mid)], (me_c - 1, me_v)),
            (state.at[step, 1], halo_y.at[step, 1], (me_c, owner_of(me_y + 1))),
            (state.at[step, 0], halo_y.at[step, 0], (me_c, owner_of(me_y - 1))),
        ]
        return [
            pltpu.make_async_remote_copy(
                src_ref=src,
                dst_ref=dst,
                send_sem=halo_send.at[n, step],
                recv_sem=halo_recv.at[n, step],
                device_id=to,
                device_id_type=MESH,
            )
            for n, (src, dst, to) in enumerate(routes)
        ]

    sends = [has_high_x, has_low_x, has_high_y, has_low_y]
    receives = [has_low_x, has_high_x, has_low_y, has_high_y]

    def speed_x(a):
        return (2 * a - (nvx - 1)) * 0.5 * SPACING

    def advance(step, carry):
        copies = halo_copies(step)
        for copy, present in zip(copies, sends):
            pl.when(present)(copy.start)

        own = []
        for h in (0, 1):
            here = state[step, h]
            own.append(
                here * lanes[h]
                + pltpu.roll(here, 1, 1) * lanes[4]
                + pltpu.roll(here, NZ - 1, 1) * lanes[5]
            )

        for copy, present in zip(copies, receives):
            pl.when(present)(copy.wait_recv)

        moved = []
        for h in (0, 1):
            side = []
            for a in range(nvx):
                weight = COURANT * abs(speed_x(a))
                side.append(own[h][a] + (halo_x[step, h, a] - state[step, h, a]) * weight)
            moved.append(jnp.stack(side) + halo_y[step, h] * lanes[2 + h])
        rows = jnp.concatenate([side.reshape(nvx * NZ, LANES) for side in moved], axis=1)

        span = 2 * LANES
        plane = exact_dot(rows, mats[:span], mats[span : 2 * span]).reshape(nvx, NZ, span)
        real, imag = fourier(
            [plane[a, :, :LANES] for a in range(nvx)], [plane[a, :, LANES:] for a in range(nvx)], -1
        )
        spec[0] = jnp.stack(real)
        spec[1] = jnp.stack(imag)

        def weigh(w, carry):
            gains = [sym[a, pl.ds(w, 1), :] for a in range(nvx)]
            real, imag = fourier(
                [spec[0, a] * gains[a] for a in range(nvx)], [spec[1, a] * gains[a] for a in range(nvx)], 1
            )
            line = jnp.concatenate(
                [jnp.concatenate(real, axis=0), jnp.concatenate(imag, axis=0)], axis=1
            )
            back[w] = exact_dot(line, mats[2 * span : 3 * span], mats[3 * span :])
            return carry

        lax.fori_loop(0, KERNELS, weigh, 0, unroll=True)
        change = back[0] * back[2] + back[1] * back[3] - rows * back[4]
        after = rows + COLLISION_STEP * change
        for h in (0, 1):
            state[step + 1, h] = after[:, h * LANES : (h + 1) * LANES].reshape(nvx, NZ, LANES)
        return carry

    lax.fori_loop(0, STEPS, advance, 0)

    low, high = state[STEPS, 0], state[STEPS, 1]
    parts = [
        low,
        jnp.where(lane < quarter, turn(low, LOCAL_V), turn(high, quarter)),
        turn(high, LANES - quarter),
    ]
    stacked = [
        jnp.where(lane < LOCAL_V, part[:, : NZ // 2], turn(part, LOCAL_V)[:, NZ // 2 :]) for part in parts
    ]
    packed_back[...] = jnp.stack(stacked, axis=1).reshape(columns, NZ // 2, LANES)
    exchange(packed_back, arrived_back, 1, False, me_y, 0, ring // 2)

    both = low + high
    sums_low, sums_high = jnp.sum(low, axis=0), jnp.sum(high, axis=0)
    along, squared = 0.0, 0.0
    for a in range(nvx):
        along = along + both[a] * (SPACING**3 * speed_x(a))
        squared = squared + both[a] * (SPACING**3 * speed_x(a) ** 2)
    totals = [
        along,
        sums_low * lanes[6] + sums_high * lanes[7],
        (sums_low + sums_high) * lanes[8],
        squared + sums_low * lanes[9] + sums_high * lanes[10],
    ]
    pl.when(moved_home)(uses_copy.wait_recv)
    counted = uses[...]
    shares = [
        jnp.sum(jnp.sum(total, axis=1, keepdims=True) * counted, axis=0, keepdims=True) for total in totals
    ]
    shares.append(jnp.zeros((NZ - MOMENTS, LANES), jnp.float32))
    share = jnp.concatenate(shares, axis=0)
    mine[...] = share
    all_others, rest = others.at[pl.ds(0, cells)], others.at[pl.ds(0, cells - 1)]

    def give(j, carry):
        to = lax.rem(me_c + j, cells)
        pltpu.make_async_remote_copy(
            src_ref=mine,
            dst_ref=others.at[me_c],
            send_sem=load_send,
            recv_sem=load_recv,
            device_id=(to, me_y),
            device_id_type=MESH,
        ).start()
        return carry

    lax.fori_loop(1, cells, give, 0)
    pl.when(moved_home)(lambda: give(0, None))

    exchange(packed_back, arrived_back, 1, False, me_y, ring // 2, ring)
    arrived_back[pl.ds(me_y, 1)] = packed_back[pl.ds(me_v, 1)]

    @pl.when(moved_home)
    def _():
        pltpu.make_async_copy(all_others, all_others, load_recv).wait()

    @pl.when(jnp.logical_not(moved_home))
    def _():
        others[pl.ds(me_c, 1)] = share[None]
        pltpu.make_async_copy(rest, rest, load_recv).wait()

    summed = jnp.sum(others[...], axis=0)
    picked = slot - PANEL_DEV * me_c
    columns_out = [
        jnp.sum(jnp.where(picked == k, summed, 0.0), axis=1, keepdims=True) for k in range(PANEL_DEV)
    ]
    loads[...] = jnp.concatenate(columns_out, axis=1)[:MOMENTS]

    arrivals(arrived_back, 1)
    for start in range(0, columns, LANES // NZ):
        stop = min(start + LANES // NZ, columns)
        block = arrived_back[start:stop]
        tall = jnp.concatenate([block, turn(block, LOCAL_V)], axis=1).reshape((stop - start) * NZ, LANES)
        out[:, 0, start * NZ : stop * NZ] = jnp.transpose(tall)[:LOCAL_V]

    departures(packed, 0)
    departures(packed_back, 1)
    pl.when(moved_home)(uses_copy.wait_send)
    pl.when(moved_home)(pltpu.make_async_copy(all_others, all_others, load_send).wait)
    pl.when(jnp.logical_not(moved_home))(pltpu.make_async_copy(rest, rest, load_send).wait)

    def finish(step, carry):
        for copy, present in zip(halo_copies(step), sends):
            pl.when(present)(copy.wait_send)
        return carry

    lax.fori_loop(0, STEPS, finish, 0)


def per_device(cells, columns, distribution, gain_left, gain_right, loss_kernel, wall_cell, wall_count, wall_panel):
    nvx = columns // PARTS
    local, _, width = distribution.shape
    f32 = jnp.float32
    loss = loss_kernel.reshape(1, -1)
    picks = jnp.asarray(weight_selectors())
    mats = jnp.asarray(plane_matrices())
    tables = jnp.asarray(lane_tables())
    anywhere = pl.BlockSpec(memory_space=pl.ANY)
    in_vmem = pl.BlockSpec(memory_space=pltpu.VMEM)
    dma = pltpu.SemaphoreType.DMA
    out, loads = pl.pallas_call(
        functools.partial(kernel, cells, columns),
        out_shape=(
            pltpu.VMEM((local, 1, width), f32),
            pltpu.VMEM((MOMENTS, PANEL_DEV), f32),
        ),
        in_specs=[anywhere] * 10,
        out_specs=(in_vmem, in_vmem),
        scratch_shapes=[
            pltpu.VMEM(distribution.shape, f32),
            pltpu.SMEM(wall_cell.shape, jnp.int32),
            pltpu.SMEM(wall_count.shape, jnp.int32),
            pltpu.SMEM(wall_panel.shape, jnp.int32),
            pltpu.VMEM(gain_left.shape, f32),
            pltpu.VMEM(gain_right.shape, f32),
            pltpu.VMEM(loss.shape, f32),
            pltpu.VMEM(picks.shape, jnp.bfloat16),
            pltpu.VMEM(mats.shape, jnp.bfloat16),
            pltpu.VMEM(tables.shape, f32),
            pltpu.VMEM((columns, NZ // 2, LANES), f32),
            pltpu.VMEM((columns, NZ // 2, LANES), f32),
            pltpu.VMEM((columns, NZ // 2, LANES), f32),
            pltpu.VMEM((columns, NZ // 2, LANES), f32),
            pltpu.VMEM((STEPS + 1, 2, nvx, NZ, LANES), f32),
            pltpu.VMEM((STEPS, 2, nvx, NZ, LANES), f32),
            pltpu.VMEM((STEPS, 2, nvx, NZ, LANES), f32),
            pltpu.VMEM((nvx // 2, NZ, 2 * PLANE), f32),
            pltpu.VMEM((nvx, NZ, LANES), f32),
            pltpu.VMEM((2, nvx, NZ, LANES), f32),
            pltpu.VMEM((KERNELS, nvx * NZ, 2 * LANES), f32),
            pltpu.VMEM((NZ, LANES), f32),
            pltpu.VMEM((NZ, LANES), f32),
            pltpu.VMEM((NZ, LANES), f32),
            pltpu.VMEM((cells, NZ, LANES), f32),
            dma((10,)),
            dma((4, STEPS)),
            dma((4, STEPS)),
            dma((2,)),
            dma((2,)),
            dma,
            dma,
            dma,
            dma,
        ],
        compiler_params=pltpu.CompilerParams(
            collective_id=0, has_side_effects=True, vmem_limit_bytes=VMEM_LIMIT
        ),
        cost_estimate=pl.CostEstimate(flops=1_000_000_000, bytes_accessed=2_000_000, transcendentals=0),
        name="collide",
    )(distribution, wall_cell, wall_count, wall_panel, gain_left, gain_right, loss, picks, mats, tables)
    return out, loads


def solution(mesh):
    placed = (
        P("vel", "cell", None),
        P(),
        P(),
        P(),
        P("cell", "vel", None),
        P("cell", "vel"),
        P("cell", "vel", None),
    )
    return jax.shard_map(
        functools.partial(per_device, mesh.shape["cell"], mesh.shape["vel"]),
        mesh=mesh,
        in_specs=placed,
        out_specs=(P("vel", "cell", None), P(None, ("cell", "vel"))),
        check_vma=False,
    )
```

```python
import functools
import math

import jax
import jax.numpy as jnp
import ml_dtypes
import numpy as np
from jax import lax
from jax.experimental import pallas as pl
from jax.experimental.pallas import tpu as pltpu
from jax.sharding import PartitionSpec as P

NVY = 16
NVZ = 12
PLANE = NVY * NVZ
HALF = PLANE // 2
KEPT = NVZ // 2 + 1
KERNELS = 5
DIRS = 2
MOMENTS = 4
STEPS = 3
NZ = 8
WALL_SLOTS = 8
PANEL_DEV = 4
LOCAL_V = 64
PARTS = PLANE // LOCAL_V
LANES = 128
VMEM_LIMIT = 60 * 1024 * 1024

SPACING = 0.5
COURANT = 0.09
COLLISION_STEP = 0.3

MESH = pl.DeviceIdType.MESH


def split(values):
    high = values.astype(ml_dtypes.bfloat16)
    low = (values - high.astype(np.float64)).astype(ml_dtypes.bfloat16)
    return high, low


def plane_matrices():
    table = np.zeros((2 * LANES, 2 * LANES))
    for point in range(PLANE):
        b, c = divmod(point, NVZ)
        row = b // (NVY // 2) * LANES + point % HALF
        for kb in range(NVY):
            for kc in range(KEPT):
                angle = 2.0 * math.pi * ((b * kb % NVY) / NVY + (c * kc % NVZ) / NVZ)
                table[row, kb * KEPT + kc] = math.cos(angle)
                table[row, LANES + kb * KEPT + kc] = -math.sin(angle)
    high, low = split(table)
    return np.concatenate([high, low, high.T, low.T], axis=0)


def weight_selectors():
    table = np.zeros((2 * PLANE, 4 * LANES))
    for kb in range(NVY):
        for kc in range(KEPT):
            share = 0.5 if kc in (0, KEPT - 1) else 1.0
            column = kb * KEPT + kc
            there = kb * NVZ + kc
            mirror = -kb % NVY * NVZ + -kc % NVZ
            for half in (0, 1):
                table[half * PLANE + there, half * LANES + column] = share
                table[half * PLANE + mirror, (2 + half) * LANES + column] = share
    return table.astype(ml_dtypes.bfloat16)


def lane_tables():
    lane = np.arange(LANES)
    used = (lane < HALF).astype(np.float64)
    vz = (2 * (lane % NVZ) - (NVZ - 1)) * 0.5 * SPACING * used
    vy = [(2 * (lane // NVZ + h * NVY // 2) - (NVY - 1)) * 0.5 * SPACING * used for h in (0, 1)]
    z = np.arange(NZ)[:, None]
    rows = []
    for h in (0, 1):
        rows.append(1.0 - COURANT * (np.abs(vy[h]) + np.abs(vz)) + 0.0 * z)
    for h in (0, 1):
        rows.append(COURANT * np.abs(vy[h]) + 0.0 * z)
    rows.append(COURANT * np.maximum(vz, 0.0) * (z > 0))
    rows.append(COURANT * np.maximum(-vz, 0.0) * (z < NZ - 1))
    cube = SPACING**3
    rows.append(cube * vy[0] + 0.0 * z)
    rows.append(cube * vy[1] + 0.0 * z)
    rows.append(cube * vz + 0.0 * z)
    rows.append(cube * (vy[0] ** 2 + vz**2) + 0.0 * z)
    rows.append(cube * (vy[1] ** 2 + vz**2) + 0.0 * z)
    return np.stack(rows).astype(np.float32)


def row_tables():
    lane = np.arange(LANES)
    z = (np.arange(NZ)[:, None] + lane // LOCAL_V * (NZ // 2)) % NZ
    parts = []
    for part in range(PARTS):
        point = part * LOCAL_V + lane % LOCAL_V
        vy = (2 * (point // NVZ) - (NVY - 1)) * 0.5 * SPACING
        vz = (2 * (point % NVZ) - (NVZ - 1)) * 0.5 * SPACING
        parts.append([
            1.0 - COURANT * (np.abs(vy) + np.abs(vz)) + 0.0 * z,
            COURANT * np.maximum(vy, 0.0) + 0.0 * z,
            COURANT * np.maximum(-vy, 0.0) + 0.0 * z,
            COURANT * np.maximum(vz, 0.0) * (z > 0),
            COURANT * np.maximum(-vz, 0.0) * (z < NZ - 1),
        ])
    return np.array(parts).astype(np.float32)


def fourier(real, imag, sign):
    count = len(real)
    if count == 1:
        return real, imag
    even_r, even_i = fourier(real[::2], imag[::2], sign)
    odd_r, odd_i = fourier(real[1::2], imag[1::2], sign)
    out_r, out_i = [None] * count, [None] * count
    half = count // 2
    for k in range(half):
        r, i = odd_r[k], odd_i[k]
        if k == 0:
            pass
        elif 4 * k == count:
            r, i = (-i, r) if sign > 0 else (i, -r)
        else:
            cos = math.cos(2.0 * math.pi * k / count)
            sin = sign * math.sin(2.0 * math.pi * k / count)
            if 8 * k == count or 8 * k == 3 * count:
                size = math.sqrt(0.5)
                up, across = cos / abs(cos), sin / abs(sin)
                first = r - i if up == across else r + i
                second = r + i if up == across else (i - r)
                if up > 0:
                    r, i = (first * size, second * size)
                else:
                    r, i = (first * -size, second * -size)
            else:
                r, i = r * cos - i * sin, r * sin + i * cos
        out_r[k], out_i[k] = even_r[k] + r, even_i[k] + i
        out_r[k + half], out_i[k + half] = even_r[k] - r, even_i[k] - i
    return out_r, out_i


def exact_dot(values, high, low):
    top = values.astype(jnp.bfloat16)
    rest = (values - top.astype(jnp.float32)).astype(jnp.bfloat16)
    dot = functools.partial(jnp.dot, preferred_element_type=jnp.float32)
    return dot(top, high) + (dot(rest, high) + dot(top, low))


def kernel(
    cells, columns,
    x_in, wall_cell_in, wall_count_in, wall_panel_in, left_in, right_in, loss_in, picks_in, mats_in, lanes_in, own_in,
    out, loads,
    x_v, wall_cell, wall_count, wall_panel, left, right, loss, picks, mats, lanes, own_rows,
    field, packed, packed_on, arrived, arrived_on, moved, packed_back, arrived_back, state, halo_x, halo_y,
    planes, sym, spec, back, my_uses, uses, mine, others,
    in_sems, halo_send, halo_recv, swap_send, swap_recv, on_send, on_recv, load_send, load_recv, uses_send, uses_recv,
):
    nvx = columns // PARTS
    mid = nvx // 2
    me_c = lax.axis_index("cell")
    me_v = lax.axis_index("vel")

    lines = 4 if columns % 4 == 0 else 2
    ring = columns // lines

    def owner_of(column):
        line, place = column // ring, lax.rem(column, ring)
        return line * ring + lax.rem(place + 1 - line + ring, ring)

    def column_of(device):
        line, place = device // ring, lax.rem(device, ring)
        return line * ring + lax.rem(place - 1 + line + ring, ring)

    half = columns // 2
    goes_up = me_v >= half
    next_c = me_c + jnp.where(goes_up, 1, -1)
    has_next = jnp.logical_and(next_c >= 0, next_c < cells)
    me_y = column_of(me_v)
    my_owner = owner_of(me_v)
    line, place = me_v // ring, lax.rem(me_v, ring)

    def for_partners(visit, start, stop):
        def visit_round(n, shift, count):
            there = lax.rem(place + shift, ring)
            for m in range(count):
                across = lines // 2 + (m + 1) // 2 * (1 if m % 2 else -1)
                to_line = lax.rem(line + across, lines)
                visit(to_line * ring + there, to_line * ring + lax.rem(there - 1 + to_line + ring, ring))

        def one_round(n, carry):
            away = (n + 1) // 2
            visit_round(n, ring // 2 + jnp.where(lax.rem(n, 2) == 1, away, -away), lines)
            return carry

        lax.fori_loop(start, min(stop, ring - 1), one_round, 0)
        if stop == ring:
            visit_round(ring - 1, 0, lines - 1)

    pairs = [
        (x_in, x_v), (wall_cell_in, wall_cell), (wall_count_in, wall_count), (wall_panel_in, wall_panel),
        (left_in, left), (right_in, right), (loss_in, loss), (picks_in, picks), (mats_in, mats), (lanes_in, lanes), (own_in, own_rows),
    ]
    loads_in = [pltpu.make_async_copy(src, dst, in_sems.at[n]) for n, (src, dst) in enumerate(pairs)]
    for copy in loads_in:
        copy.start()

    barrier = pltpu.get_barrier_semaphore()

    def greet_column(to, column):
        pl.semaphore_signal(barrier, inc=1, device_id=(me_c, to), device_id_type=MESH)
        greet_sender(to)

    def greet_sender(to):
        upward = to >= half
        present = jnp.logical_or(jnp.logical_and(upward, has_low_x), jnp.logical_and(to < half, has_high_x))

        @pl.when(present)
        def _():
            neighbour = me_c + jnp.where(upward, -1, 1)
            pl.semaphore_signal(barrier, inc=1, device_id=(neighbour, to), device_id_type=MESH)

    def greet_row(j, carry):
        to = lax.rem(me_c + j, cells)
        pl.semaphore_signal(barrier, inc=1, device_id=(to, my_owner), device_id_type=MESH)
        return carry

    has_low_x, has_high_x = me_c > 0, me_c < cells - 1
    has_low_y, has_high_y = me_y > 0, me_y < columns - 1
    moved_home = my_owner != me_v
    greetings = [(jnp.logical_and(moved_home, has_low_x), -1), (jnp.logical_and(moved_home, has_high_x), 1)]

    for_partners(greet_column, 0, ring)
    greet_sender(me_v)
    lax.fori_loop(1, cells, greet_row, 0)
    greeted = columns - 1 + cells - 1 + jnp.where(has_next, columns, 0)
    for present, way in greetings:
        greeted = greeted + jnp.where(present, 1, 0)

        @pl.when(present)
        def _():
            pl.semaphore_signal(barrier, inc=1, device_id=(me_c + way, me_v), device_id_type=MESH)

    loads_in[0].wait()
    width = NZ * columns
    for start in range(0, width, LANES):
        stop = min(start + LANES, width)
        tile = x_v[:, 0, start:stop]
        back_by_half = jnp.concatenate([tile[:, NZ // 2 :], tile[:, : NZ // 2]], axis=1)
        on_by_half = jnp.concatenate([tile[:, -(NZ // 2) :], tile[:, : -(NZ // 2)]], axis=1)
        place_z = lax.rem(lax.broadcasted_iota(jnp.int32, tile.shape, 1), NZ)
        shifted = jnp.where(place_z < NZ // 2, back_by_half, on_by_half)
        turned = jnp.transpose(jnp.concatenate([tile, shifted], axis=0))
        turned = turned.reshape((stop - start) // NZ, NZ, LANES)
        field[1 + start // NZ : 1 + stop // NZ] = turned
    field[0] = jnp.zeros((NZ, LANES), jnp.float32)
    field[columns + 1] = jnp.zeros((NZ, LANES), jnp.float32)

    loads_in[10].wait()
    part = lax.rem(me_v, PARTS)
    weight_x = COURANT * 0.5 * SPACING * jnp.abs(2 * (me_v // PARTS) - (nvx - 1)).astype(jnp.float32)
    here = field[1 : columns + 1]
    stays = (
        here * (own_rows[part, 0] - weight_x)
        + field[:columns] * own_rows[part, 1]
        + field[2:] * own_rows[part, 2]
        + pltpu.roll(here, 1, 1) * own_rows[part, 3]
        + pltpu.roll(here, NZ - 1, 1) * own_rows[part, 4]
    )
    packed[...] = stays[:, : NZ // 2]
    packed_on[...] = here[:, : NZ // 2] * weight_x
    arrived[pl.ds(me_v, 1)] = packed[pl.ds(me_y, 1)]

    @pl.when(jnp.logical_not(has_low_x))
    def _():
        arrived_on[half:] = jnp.zeros((half, NZ // 2, LANES), jnp.float32)

    @pl.when(jnp.logical_not(has_high_x))
    def _():
        arrived_on[:half] = jnp.zeros((half, NZ // 2, LANES), jnp.float32)

    depth = lax.broadcasted_iota(jnp.int32, (NZ, LANES), 0)
    slot = lax.broadcasted_iota(jnp.int32, (NZ, LANES), 1)
    for copy in loads_in[1:4]:
        copy.wait()
    counted = jnp.zeros((NZ, LANES), jnp.float32)
    per_owner = PANEL_DEV * columns
    for n in range(WALL_SLOTS):
        panel = wall_panel[0, 0, n]
        target = panel // per_owner * PANEL_DEV + lax.rem(panel, PANEL_DEV)
        target = jnp.where(n < wall_count[0, 0], target, -1)
        hit = jnp.logical_and(depth == wall_cell[0, 0, n], slot == target)
        counted = counted + jnp.where(hit, 1.0, 0.0)
    my_uses[...] = counted

    @pl.when(jnp.logical_not(moved_home))
    def _():
        uses[...] = counted

    pl.semaphore_wait(barrier, greeted)

    def send_block(source, target, which, to, source_slot, target_slot):
        pltpu.make_async_remote_copy(
            src_ref=source.at[source_slot],
            dst_ref=target.at[target_slot],
            send_sem=swap_send.at[which],
            recv_sem=swap_recv.at[which],
            device_id=(me_c, to),
            device_id_type=MESH,
        ).start()

    def arrivals(target, which):
        rest = target.at[pl.ds(0, columns - 1)]
        pltpu.make_async_copy(rest, rest, swap_recv.at[which]).wait()

    def departures(source, which):
        rest = source.at[pl.ds(0, columns - 1)]
        pltpu.make_async_copy(rest, rest, swap_send.at[which]).wait()

    def send_on(to, column):
        pltpu.make_async_remote_copy(
            src_ref=packed_on.at[column],
            dst_ref=arrived_on.at[me_v],
            send_sem=on_send,
            recv_sem=on_recv.at[jnp.where(goes_up, 0, 1)],
            device_id=(next_c, to),
            device_id_type=MESH,
        ).start()

    def send_both(to, column):
        send_block(packed, arrived, 0, to, column, me_v)
        pl.when(has_next)(lambda: send_on(to, column))

    for_partners(send_both, 0, ring)
    pl.when(has_next)(lambda: send_on(me_v, me_y))

    uses_copy = pltpu.make_async_remote_copy(
        src_ref=my_uses,
        dst_ref=uses,
        send_sem=uses_send,
        recv_sem=uses_recv,
        device_id=(me_c, my_owner),
        device_id_type=MESH,
    )
    pl.when(moved_home)(uses_copy.start)

    @pl.when(jnp.logical_not(has_low_x))
    def _():
        halo_x[:, :, mid:] = jnp.zeros((STEPS - 1, 2, mid, NZ, LANES), jnp.float32)

    @pl.when(jnp.logical_not(has_high_x))
    def _():
        halo_x[:, :, :mid] = jnp.zeros((STEPS - 1, 2, mid, NZ, LANES), jnp.float32)

    @pl.when(jnp.logical_not(has_low_y))
    def _():
        halo_y[:, 1] = jnp.zeros((STEPS - 1, nvx, NZ, LANES), jnp.float32)

    @pl.when(jnp.logical_not(has_high_y))
    def _():
        halo_y[:, 0] = jnp.zeros((STEPS - 1, nvx, NZ, LANES), jnp.float32)

    for copy in loads_in[4:10]:
        copy.wait()
    for pair in range(nvx // 2):
        span = slice(pair * 2 * PLANE, (pair + 1) * 2 * PLANE)
        planes[pair, :DIRS] = left[:, span]
        planes[pair, DIRS : 2 * DIRS] = right[:, span]
        planes[pair, 2 * DIRS : KERNELS] = loss[:, span]
        planes[pair, KERNELS:] = jnp.zeros((NZ - KERNELS, 2 * PLANE), jnp.float32)
    remaining = planes[...].reshape(nvx // 2 * NZ, 2 * PLANE)
    chosen = 0.0
    for _ in range(3):
        top = remaining.astype(jnp.bfloat16)
        chosen = chosen + jnp.dot(top, picks[...], preferred_element_type=jnp.float32)
        remaining = remaining - top.astype(jnp.float32)
    chosen = (chosen * (1.0 / (nvx * PLANE))).reshape(nvx // 2, NZ, 4 * LANES)
    for a in range(nvx):
        b = -a % nvx
        near, far = a % 2 * LANES, (2 + b % 2) * LANES
        sym[a] = chosen[a // 2, :, near : near + LANES] + chosen[b // 2, :, far : far + LANES]

    arrivals(arrived, 0)
    from_low, from_high = arrived_on.at[pl.ds(half, half)], arrived_on.at[pl.ds(0, half)]
    pl.when(has_low_x)(pltpu.make_async_copy(from_low, from_low, on_recv.at[0]).wait)
    pl.when(has_high_x)(pltpu.make_async_copy(from_high, from_high, on_recv.at[1]).wait)

    lane = lax.broadcasted_iota(jnp.int32, (1, 1, LANES), 2)
    used = lane < HALF
    quarter = LOCAL_V // 2

    def turn(values, by):
        return pltpu.roll(values, by, values.ndim - 1)

    blocks = (arrived[...] + arrived_on[...]).reshape(nvx, PARTS, NZ // 2, LANES)
    wide = []
    for part in range(PARTS):
        block = blocks[:, part]
        wide.append(jnp.concatenate([block, turn(block, LOCAL_V)], axis=1))
    moved[0] = jnp.where(lane < LOCAL_V, wide[0], jnp.where(used, turn(wide[1], LOCAL_V), 0.0))
    moved[1] = jnp.where(
        lane < quarter, turn(wide[1], LANES - quarter), jnp.where(used, turn(wide[2], quarter), 0.0)
    )

    def halo_copies(step):
        routes = [
            (state.at[step, :, pl.ds(mid, mid)], halo_x.at[step, :, pl.ds(mid, mid)], (me_c + 1, me_v)),
            (state.at[step, :, pl.ds(0, mid)], halo_x.at[step, :, pl.ds(0, mid)], (me_c - 1, me_v)),
            (state.at[step, 1], halo_y.at[step, 1], (me_c, owner_of(me_y + 1))),
            (state.at[step, 0], halo_y.at[step, 0], (me_c, owner_of(me_y - 1))),
        ]
        return [
            pltpu.make_async_remote_copy(
                src_ref=src,
                dst_ref=dst,
                send_sem=halo_send.at[n, step],
                recv_sem=halo_recv.at[n, step],
                device_id=to,
                device_id_type=MESH,
            )
            for n, (src, dst, to) in enumerate(routes)
        ]

    sends = [has_high_x, has_low_x, has_high_y, has_low_y]
    receives = [has_low_x, has_high_x, has_low_y, has_high_y]

    def speed_x(a):
        return (2 * a - (nvx - 1)) * 0.5 * SPACING

    def transport(step):
        copies = halo_copies(step)
        for copy, present in zip(copies, sends):
            pl.when(present)(copy.start)

        own = []
        for h in (0, 1):
            here = state[step, h]
            own.append(
                here * lanes[h]
                + pltpu.roll(here, 1, 1) * lanes[4]
                + pltpu.roll(here, NZ - 1, 1) * lanes[5]
            )

        for copy, present in zip(copies, receives):
            pl.when(present)(copy.wait_recv)

        for h in (0, 1):
            side = []
            for a in range(nvx):
                weight = COURANT * abs(speed_x(a))
                side.append(own[h][a] + (halo_x[step, h, a] - state[step, h, a]) * weight)
            moved[h] = jnp.stack(side) + halo_y[step, h] * lanes[2 + h]

    def advance(step, carry):
        rows = jnp.concatenate([moved[h].reshape(nvx * NZ, LANES) for h in (0, 1)], axis=1)

        span = 2 * LANES
        plane = exact_dot(rows, mats[:span], mats[span : 2 * span]).reshape(nvx, NZ, span)
        real, imag = fourier(
            [plane[a, :, :LANES] for a in range(nvx)], [plane[a, :, LANES:] for a in range(nvx)], -1
        )
        spec[0] = jnp.stack(real)
        spec[1] = jnp.stack(imag)

        def weigh(w, carry):
            gains = [sym[a, pl.ds(w, 1), :] for a in range(nvx)]
            real, imag = fourier(
                [spec[0, a] * gains[a] for a in range(nvx)], [spec[1, a] * gains[a] for a in range(nvx)], 1
            )
            line = jnp.concatenate(
                [jnp.concatenate(real, axis=0), jnp.concatenate(imag, axis=0)], axis=1
            )
            back[w] = exact_dot(line, mats[2 * span : 3 * span], mats[3 * span :])
            return carry

        lax.fori_loop(0, KERNELS, weigh, 0, unroll=True)
        change = back[0] * back[2] + back[1] * back[3] - rows * back[4]
        after = rows + COLLISION_STEP * change
        for h in (0, 1):
            state[step, h] = after[:, h * LANES : (h + 1) * LANES].reshape(nvx, NZ, LANES)
        pl.when(step < STEPS - 1)(lambda: transport(step))
        return carry

    lax.fori_loop(0, STEPS, advance, 0)

    low, high = state[STEPS - 1, 0], state[STEPS - 1, 1]
    parts = [
        low,
        jnp.where(lane < quarter, turn(low, LOCAL_V), turn(high, quarter)),
        turn(high, LANES - quarter),
    ]
    stacked = [
        jnp.where(lane < LOCAL_V, part[:, : NZ // 2], turn(part, LOCAL_V)[:, NZ // 2 :]) for part in parts
    ]
    packed_back[...] = jnp.stack(stacked, axis=1).reshape(columns, NZ // 2, LANES)
    def send_home(to, column):
        send_block(packed_back, arrived_back, 1, to, to, me_y)

    for_partners(send_home, 0, ring // 2)

    both = low + high
    sums_low, sums_high = jnp.sum(low, axis=0), jnp.sum(high, axis=0)
    along, squared = 0.0, 0.0
    for a in range(nvx):
        along = along + both[a] * (SPACING**3 * speed_x(a))
        squared = squared + both[a] * (SPACING**3 * speed_x(a) ** 2)
    totals = [
        along,
        sums_low * lanes[6] + sums_high * lanes[7],
        (sums_low + sums_high) * lanes[8],
        squared + sums_low * lanes[9] + sums_high * lanes[10],
    ]
    pl.when(moved_home)(uses_copy.wait_recv)
    counted = uses[...]
    shares = [
        jnp.sum(jnp.sum(total, axis=1, keepdims=True) * counted, axis=0, keepdims=True) for total in totals
    ]
    shares.append(jnp.zeros((NZ - MOMENTS, LANES), jnp.float32))
    share = jnp.concatenate(shares, axis=0)
    mine[...] = share
    all_others, rest = others.at[pl.ds(0, cells)], others.at[pl.ds(0, cells - 1)]

    def give(j, carry):
        to = lax.rem(me_c + j, cells)
        pltpu.make_async_remote_copy(
            src_ref=mine,
            dst_ref=others.at[me_c],
            send_sem=load_send,
            recv_sem=load_recv,
            device_id=(to, me_y),
            device_id_type=MESH,
        ).start()
        return carry

    lax.fori_loop(1, cells, give, 0)
    pl.when(moved_home)(lambda: give(0, None))

    for_partners(send_home, ring // 2, ring)
    arrived_back[pl.ds(me_y, 1)] = packed_back[pl.ds(me_v, 1)]

    @pl.when(moved_home)
    def _():
        pltpu.make_async_copy(all_others, all_others, load_recv).wait()

    @pl.when(jnp.logical_not(moved_home))
    def _():
        others[pl.ds(me_c, 1)] = share[None]
        pltpu.make_async_copy(rest, rest, load_recv).wait()

    summed = jnp.sum(others[...], axis=0)
    picked = slot - PANEL_DEV * me_c
    columns_out = [
        jnp.sum(jnp.where(picked == k, summed, 0.0), axis=1, keepdims=True) for k in range(PANEL_DEV)
    ]
    loads[...] = jnp.concatenate(columns_out, axis=1)[:MOMENTS]

    arrivals(arrived_back, 1)
    for start in range(0, columns, LANES // NZ):
        stop = min(start + LANES // NZ, columns)
        block = arrived_back[start:stop]
        tall = jnp.concatenate([block, turn(block, LOCAL_V)], axis=1).reshape((stop - start) * NZ, LANES)
        out[:, 0, start * NZ : stop * NZ] = jnp.transpose(tall)[:LOCAL_V]

    departures(packed, 0)
    pl.when(has_next)(pltpu.make_async_copy(packed_on, packed_on, on_send).wait)
    departures(packed_back, 1)
    pl.when(moved_home)(uses_copy.wait_send)
    pl.when(moved_home)(pltpu.make_async_copy(all_others, all_others, load_send).wait)
    pl.when(jnp.logical_not(moved_home))(pltpu.make_async_copy(rest, rest, load_send).wait)

    def finish(step, carry):
        for copy, present in zip(halo_copies(step), sends):
            pl.when(present)(copy.wait_send)
        return carry

    lax.fori_loop(0, STEPS - 1, finish, 0)


def per_device(cells, columns, distribution, gain_left, gain_right, loss_kernel, wall_cell, wall_count, wall_panel):
    nvx = columns // PARTS
    local, _, width = distribution.shape
    f32 = jnp.float32
    loss = loss_kernel.reshape(1, -1)
    picks = jnp.asarray(weight_selectors())
    mats = jnp.asarray(plane_matrices())
    tables = jnp.asarray(lane_tables())
    rows = jnp.asarray(row_tables())
    anywhere = pl.BlockSpec(memory_space=pl.ANY)
    in_vmem = pl.BlockSpec(memory_space=pltpu.VMEM)
    dma = pltpu.SemaphoreType.DMA
    out, loads = pl.pallas_call(
        functools.partial(kernel, cells, columns),
        out_shape=(
            pltpu.VMEM((local, 1, width), f32),
            pltpu.VMEM((MOMENTS, PANEL_DEV), f32),
        ),
        in_specs=[anywhere] * 11,
        out_specs=(in_vmem, in_vmem),
        scratch_shapes=[
            pltpu.VMEM(distribution.shape, f32),
            pltpu.SMEM(wall_cell.shape, jnp.int32),
            pltpu.SMEM(wall_count.shape, jnp.int32),
            pltpu.SMEM(wall_panel.shape, jnp.int32),
            pltpu.VMEM(gain_left.shape, f32),
            pltpu.VMEM(gain_right.shape, f32),
            pltpu.VMEM(loss.shape, f32),
            pltpu.VMEM(picks.shape, jnp.bfloat16),
            pltpu.VMEM(mats.shape, jnp.bfloat16),
            pltpu.VMEM(tables.shape, f32),
            pltpu.VMEM(rows.shape, f32),
            pltpu.VMEM((columns + 2, NZ, LANES), f32),
            pltpu.VMEM((columns, NZ // 2, LANES), f32),
            pltpu.VMEM((columns, NZ // 2, LANES), f32),
            pltpu.VMEM((columns, NZ // 2, LANES), f32),
            pltpu.VMEM((columns, NZ // 2, LANES), f32),
            pltpu.VMEM((2, nvx, NZ, LANES), f32),
            pltpu.VMEM((columns, NZ // 2, LANES), f32),
            pltpu.VMEM((columns, NZ // 2, LANES), f32),
            pltpu.VMEM((STEPS, 2, nvx, NZ, LANES), f32),
            pltpu.VMEM((STEPS - 1, 2, nvx, NZ, LANES), f32),
            pltpu.VMEM((STEPS - 1, 2, nvx, NZ, LANES), f32),
            pltpu.VMEM((nvx // 2, NZ, 2 * PLANE), f32),
            pltpu.VMEM((nvx, NZ, LANES), f32),
            pltpu.VMEM((2, nvx, NZ, LANES), f32),
            pltpu.VMEM((KERNELS, nvx * NZ, 2 * LANES), f32),
            pltpu.VMEM((NZ, LANES), f32),
            pltpu.VMEM((NZ, LANES), f32),
            pltpu.VMEM((NZ, LANES), f32),
            pltpu.VMEM((cells, NZ, LANES), f32),
            dma((11,)),
            dma((4, STEPS - 1)),
            dma((4, STEPS - 1)),
            dma((2,)),
            dma((2,)),
            dma,
            dma((2,)),
            dma,
            dma,
            dma,
            dma,
        ],
        compiler_params=pltpu.CompilerParams(
            collective_id=0, has_side_effects=True, vmem_limit_bytes=VMEM_LIMIT
        ),
        cost_estimate=pl.CostEstimate(flops=1_000_000_000, bytes_accessed=2_000_000, transcendentals=0),
        name="collide",
    )(distribution, wall_cell, wall_count, wall_panel, gain_left, gain_right, loss, picks, mats, tables, rows)
    return out, loads


def solution(mesh):
    placed = (
        P("vel", "cell", None),
        P(),
        P(),
        P(),
        P("cell", "vel", None),
        P("cell", "vel"),
        P("cell", "vel", None),
    )
    return jax.shard_map(
        functools.partial(per_device, mesh.shape["cell"], mesh.shape["vel"]),
        mesh=mesh,
        in_specs=placed,
        out_specs=(P("vel", "cell", None), P(None, ("cell", "vel"))),
        check_vma=False,
    )
```

```python
import functools
import math

import jax
import jax.numpy as jnp
import ml_dtypes
import numpy as np
from jax import lax
from jax.experimental import pallas as pl
from jax.experimental.pallas import tpu as pltpu
from jax.sharding import PartitionSpec as P

NVY = 16
NVZ = 12
PLANE = NVY * NVZ
HALF = PLANE // 2
KEPT = NVZ // 2 + 1
KERNELS = 5
DIRS = 2
MOMENTS = 4
STEPS = 3
NZ = 8
WALL_SLOTS = 8
PANEL_DEV = 4
LOCAL_V = 64
PARTS = PLANE // LOCAL_V
LANES = 128
VMEM_LIMIT = 60 * 1024 * 1024

SPACING = 0.5
COURANT = 0.09
COLLISION_STEP = 0.3

MESH = pl.DeviceIdType.MESH


def split(values):
    high = values.astype(ml_dtypes.bfloat16)
    low = (values - high.astype(np.float64)).astype(ml_dtypes.bfloat16)
    return high, low


def plane_matrices():
    table = np.zeros((2 * LANES, 2 * LANES))
    for point in range(PLANE):
        b, c = divmod(point, NVZ)
        row = b // (NVY // 2) * LANES + point % HALF
        for kb in range(NVY):
            for kc in range(KEPT):
                angle = 2.0 * math.pi * ((b * kb % NVY) / NVY + (c * kc % NVZ) / NVZ)
                table[row, kb * KEPT + kc] = math.cos(angle)
                table[row, LANES + kb * KEPT + kc] = -math.sin(angle)
    high, low = split(table)
    return np.concatenate([high, high, low, high.T, high.T, low.T], axis=0)


def weight_selectors():
    table = np.zeros((2 * PLANE, 4 * LANES))
    for kb in range(NVY):
        for kc in range(KEPT):
            share = 0.5 if kc in (0, KEPT - 1) else 1.0
            column = kb * KEPT + kc
            there = kb * NVZ + kc
            mirror = -kb % NVY * NVZ + -kc % NVZ
            for half in (0, 1):
                table[half * PLANE + there, half * LANES + column] = share
                table[half * PLANE + mirror, (2 + half) * LANES + column] = share
    return table.astype(ml_dtypes.bfloat16)


def lane_tables():
    lane = np.arange(LANES)
    used = (lane < HALF).astype(np.float64)
    vz = (2 * (lane % NVZ) - (NVZ - 1)) * 0.5 * SPACING * used
    vy = [(2 * (lane // NVZ + h * NVY // 2) - (NVY - 1)) * 0.5 * SPACING * used for h in (0, 1)]
    z = np.arange(NZ)[:, None]
    rows = []
    for h in (0, 1):
        rows.append(1.0 - COURANT * (np.abs(vy[h]) + np.abs(vz)) + 0.0 * z)
    for h in (0, 1):
        rows.append(COURANT * np.abs(vy[h]) + 0.0 * z)
    rows.append(COURANT * np.maximum(vz, 0.0) * (z > 0))
    rows.append(COURANT * np.maximum(-vz, 0.0) * (z < NZ - 1))
    cube = SPACING**3
    rows.append(cube * vy[0] + 0.0 * z)
    rows.append(cube * vy[1] + 0.0 * z)
    rows.append(cube * vz + 0.0 * z)
    rows.append(cube * (vy[0] ** 2 + vz**2) + 0.0 * z)
    rows.append(cube * (vy[1] ** 2 + vz**2) + 0.0 * z)
    return np.stack(rows).astype(np.float32)


def row_tables():
    lane = np.arange(LANES)
    z = (np.arange(NZ)[:, None] + lane // LOCAL_V * (NZ // 2)) % NZ
    parts = []
    for part in range(PARTS):
        point = part * LOCAL_V + lane % LOCAL_V
        vy = (2 * (point // NVZ) - (NVY - 1)) * 0.5 * SPACING
        vz = (2 * (point % NVZ) - (NVZ - 1)) * 0.5 * SPACING
        parts.append([
            1.0 - COURANT * (np.abs(vy) + np.abs(vz)) + 0.0 * z,
            COURANT * np.maximum(vy, 0.0) + 0.0 * z,
            COURANT * np.maximum(-vy, 0.0) + 0.0 * z,
            COURANT * np.maximum(vz, 0.0) * (z > 0),
            COURANT * np.maximum(-vz, 0.0) * (z < NZ - 1),
        ])
    return np.array(parts).astype(np.float32)


def fourier(real, imag, sign):
    count = len(real)
    if count == 1:
        return real, imag
    even_r, even_i = fourier(real[::2], imag[::2], sign)
    odd_r, odd_i = fourier(real[1::2], imag[1::2], sign)
    out_r, out_i = [None] * count, [None] * count
    half = count // 2
    for k in range(half):
        r, i = odd_r[k], odd_i[k]
        if k == 0:
            pass
        elif 4 * k == count:
            r, i = (-i, r) if sign > 0 else (i, -r)
        else:
            cos = math.cos(2.0 * math.pi * k / count)
            sin = sign * math.sin(2.0 * math.pi * k / count)
            if 8 * k == count or 8 * k == 3 * count:
                size = math.sqrt(0.5)
                up, across = cos / abs(cos), sin / abs(sin)
                first = r - i if up == across else r + i
                second = r + i if up == across else (i - r)
                if up > 0:
                    r, i = (first * size, second * size)
                else:
                    r, i = (first * -size, second * -size)
            else:
                r, i = r * cos - i * sin, r * sin + i * cos
        out_r[k], out_i[k] = even_r[k] + r, even_i[k] + i
        out_r[k + half], out_i[k + half] = even_r[k] - r, even_i[k] - i
    return out_r, out_i


def three_parts(values):
    top = values.astype(jnp.bfloat16)
    rest = (values - top.astype(jnp.float32)).astype(jnp.bfloat16)
    return jnp.concatenate([top, rest, top], axis=1)


def kernel(
    cells, columns,
    x_in, wall_cell_in, wall_count_in, wall_panel_in, left_in, right_in, loss_in, picks_in, mats_in, lanes_in, own_in,
    out, loads,
    x_v, wall_cell, wall_count, wall_panel, left, right, loss, picks, mats, lanes, own_rows,
    field, packed, packed_on, arrived, arrived_on, moved, packed_back, arrived_back, state, halo_x, halo_y,
    planes, sym, spec, back, my_uses, uses, mine, others,
    in_sems, halo_send, halo_recv, swap_send, swap_recv, on_send, on_recv, load_send, load_recv, uses_send, uses_recv,
):
    nvx = columns // PARTS
    mid = nvx // 2
    me_c = lax.axis_index("cell")
    me_v = lax.axis_index("vel")

    lines = 4 if columns % 4 == 0 else 2
    ring = columns // lines

    def owner_of(column):
        line, place = column // ring, lax.rem(column, ring)
        return line * ring + lax.rem(place + 1 - line + ring, ring)

    def column_of(device):
        line, place = device // ring, lax.rem(device, ring)
        return line * ring + lax.rem(place - 1 + line + ring, ring)

    half = columns // 2
    goes_up = me_v >= half
    next_c = me_c + jnp.where(goes_up, 1, -1)
    has_next = jnp.logical_and(next_c >= 0, next_c < cells)
    me_y = column_of(me_v)
    my_owner = owner_of(me_v)
    line, place = me_v // ring, lax.rem(me_v, ring)

    def wrapped(value, count):
        return jnp.where(value >= count, value - count, value)

    across = [lines // 2 + (m + 1) // 2 * (1 if m % 2 else -1) for m in range(lines)]
    to_lines = [wrapped(line + shift % lines, lines) for shift in across]

    def visit_line(visit, there, m):
        column = there + to_lines[m] - 1
        column = wrapped(jnp.where(column < 0, column + ring, column), ring)
        visit(to_lines[m] * ring + there, to_lines[m] * ring + column)

    def farthest_first(visit):
        def one_round(n, carry):
            away = (n + 1) // 2
            there = wrapped(place + ring // 2 + jnp.where(lax.rem(n, 2) == 1, away, -away), ring)
            for m in range(lines):
                visit_line(visit, there, m)
            return carry

        lax.fori_loop(0, ring - 1, one_round, 0)
        for m in range(lines - 1):
            visit_line(visit, place, m)

    def in_place_order(visit, start, stop):
        def one_round(there, carry):
            for m in range(lines - 1):
                visit_line(visit, there, m)
            pl.when(there != place)(lambda: visit_line(visit, there, lines - 1))
            return carry

        lax.fori_loop(start, stop, one_round, 0)

    pairs = [
        (x_in, x_v), (wall_cell_in, wall_cell), (wall_count_in, wall_count), (wall_panel_in, wall_panel),
        (left_in, left), (right_in, right), (loss_in, loss), (picks_in, picks), (mats_in, mats), (lanes_in, lanes), (own_in, own_rows),
    ]
    loads_in = [pltpu.make_async_copy(src, dst, in_sems.at[n]) for n, (src, dst) in enumerate(pairs)]
    for copy in loads_in:
        copy.start()

    barrier = pltpu.get_barrier_semaphore()

    def greet_column(to, column):
        pl.semaphore_signal(barrier, inc=1, device_id=(me_c, to), device_id_type=MESH)
        greet_sender(to)

    def greet_sender(to):
        upward = to >= half
        present = jnp.logical_or(jnp.logical_and(upward, has_low_x), jnp.logical_and(to < half, has_high_x))

        @pl.when(present)
        def _():
            neighbour = me_c + jnp.where(upward, -1, 1)
            pl.semaphore_signal(barrier, inc=1, device_id=(neighbour, to), device_id_type=MESH)

    def greet_row(j, carry):
        to = lax.rem(me_c + j, cells)
        pl.semaphore_signal(barrier, inc=1, device_id=(to, my_owner), device_id_type=MESH)
        return carry

    has_low_x, has_high_x = me_c > 0, me_c < cells - 1
    has_low_y, has_high_y = me_y > 0, me_y < columns - 1
    moved_home = my_owner != me_v
    greetings = [(jnp.logical_and(moved_home, has_low_x), -1), (jnp.logical_and(moved_home, has_high_x), 1)]

    farthest_first(greet_column)
    greet_sender(me_v)
    lax.fori_loop(1, cells, greet_row, 0)
    greeted = columns - 1 + cells - 1 + jnp.where(has_next, columns, 0)
    for present, way in greetings:
        greeted = greeted + jnp.where(present, 1, 0)

        @pl.when(present)
        def _():
            pl.semaphore_signal(barrier, inc=1, device_id=(me_c + way, me_v), device_id_type=MESH)

    loads_in[0].wait()
    width = NZ * columns
    for start in range(0, width, LANES):
        stop = min(start + LANES, width)
        tile = x_v[:, 0, start:stop]
        back_by_half = jnp.concatenate([tile[:, NZ // 2 :], tile[:, : NZ // 2]], axis=1)
        on_by_half = jnp.concatenate([tile[:, -(NZ // 2) :], tile[:, : -(NZ // 2)]], axis=1)
        place_z = lax.rem(lax.broadcasted_iota(jnp.int32, tile.shape, 1), NZ)
        shifted = jnp.where(place_z < NZ // 2, back_by_half, on_by_half)
        turned = jnp.transpose(jnp.concatenate([tile, shifted], axis=0))
        turned = turned.reshape((stop - start) // NZ, NZ, LANES)
        field[1 + start // NZ : 1 + stop // NZ] = turned
    field[0] = jnp.zeros((NZ, LANES), jnp.float32)
    field[columns + 1] = jnp.zeros((NZ, LANES), jnp.float32)

    loads_in[10].wait()
    part = lax.rem(me_v, PARTS)
    weight_x = COURANT * 0.5 * SPACING * jnp.abs(2 * (me_v // PARTS) - (nvx - 1)).astype(jnp.float32)
    here = field[1 : columns + 1]
    stays = (
        here * (own_rows[part, 0] - weight_x)
        + field[:columns] * own_rows[part, 1]
        + field[2:] * own_rows[part, 2]
        + pltpu.roll(here, 1, 1) * own_rows[part, 3]
        + pltpu.roll(here, NZ - 1, 1) * own_rows[part, 4]
    )
    packed[...] = stays[:, : NZ // 2]
    packed_on[...] = here[:, : NZ // 2] * weight_x
    arrived[pl.ds(me_v, 1)] = packed[pl.ds(me_y, 1)]

    @pl.when(jnp.logical_not(has_low_x))
    def _():
        arrived_on[half:] = jnp.zeros((half, NZ // 2, LANES), jnp.float32)

    @pl.when(jnp.logical_not(has_high_x))
    def _():
        arrived_on[:half] = jnp.zeros((half, NZ // 2, LANES), jnp.float32)

    depth = lax.broadcasted_iota(jnp.int32, (NZ, LANES), 0)
    slot = lax.broadcasted_iota(jnp.int32, (NZ, LANES), 1)
    for copy in loads_in[1:4]:
        copy.wait()
    counted = jnp.zeros((NZ, LANES), jnp.float32)
    per_owner = PANEL_DEV * columns
    for n in range(WALL_SLOTS):
        panel = wall_panel[0, 0, n]
        target = panel // per_owner * PANEL_DEV + lax.rem(panel, PANEL_DEV)
        target = jnp.where(n < wall_count[0, 0], target, -1)
        hit = jnp.logical_and(depth == wall_cell[0, 0, n], slot == target)
        counted = counted + jnp.where(hit, 1.0, 0.0)
    my_uses[...] = counted

    @pl.when(jnp.logical_not(moved_home))
    def _():
        uses[...] = counted

    pl.semaphore_wait(barrier, greeted)

    def send_block(source, target, which, to, source_slot, target_slot):
        pltpu.make_async_remote_copy(
            src_ref=source.at[source_slot],
            dst_ref=target.at[target_slot],
            send_sem=swap_send.at[which],
            recv_sem=swap_recv.at[which],
            device_id=(me_c, to),
            device_id_type=MESH,
        ).start()

    def arrivals(target, which):
        rest = target.at[pl.ds(0, columns - 1)]
        pltpu.make_async_copy(rest, rest, swap_recv.at[which]).wait()

    def departures(source, which):
        rest = source.at[pl.ds(0, columns - 1)]
        pltpu.make_async_copy(rest, rest, swap_send.at[which]).wait()

    on_way = jnp.where(goes_up, 0, 1)

    def send_on(to, column):
        pltpu.make_async_remote_copy(
            src_ref=packed_on.at[column],
            dst_ref=arrived_on.at[me_v],
            send_sem=on_send,
            recv_sem=on_recv.at[on_way],
            device_id=(next_c, to),
            device_id_type=MESH,
        ).start()

    def send_one(to, column):
        send_block(packed, arrived, 0, to, column, me_v)

    def send_both(to, column):
        send_one(to, column)
        send_on(to, column)

    @pl.when(has_next)
    def _():
        farthest_first(send_both)
        send_on(me_v, me_y)

    pl.when(jnp.logical_not(has_next))(lambda: farthest_first(send_one))

    uses_copy = pltpu.make_async_remote_copy(
        src_ref=my_uses,
        dst_ref=uses,
        send_sem=uses_send,
        recv_sem=uses_recv,
        device_id=(me_c, my_owner),
        device_id_type=MESH,
    )
    pl.when(moved_home)(uses_copy.start)

    @pl.when(jnp.logical_not(has_low_x))
    def _():
        halo_x[:, :, mid:] = jnp.zeros((STEPS - 1, 2, mid, NZ, LANES), jnp.float32)

    @pl.when(jnp.logical_not(has_high_x))
    def _():
        halo_x[:, :, :mid] = jnp.zeros((STEPS - 1, 2, mid, NZ, LANES), jnp.float32)

    @pl.when(jnp.logical_not(has_low_y))
    def _():
        halo_y[:, 1] = jnp.zeros((STEPS - 1, nvx, NZ, LANES), jnp.float32)

    @pl.when(jnp.logical_not(has_high_y))
    def _():
        halo_y[:, 0] = jnp.zeros((STEPS - 1, nvx, NZ, LANES), jnp.float32)

    for copy in loads_in[4:10]:
        copy.wait()
    for pair in range(nvx // 2):
        span = slice(pair * 2 * PLANE, (pair + 1) * 2 * PLANE)
        planes[pair, :DIRS] = left[:, span]
        planes[pair, DIRS : 2 * DIRS] = right[:, span]
        planes[pair, 2 * DIRS : KERNELS] = loss[:, span]
        planes[pair, KERNELS:] = jnp.zeros((NZ - KERNELS, 2 * PLANE), jnp.float32)
    remaining = planes[...].reshape(nvx // 2 * NZ, 2 * PLANE)
    chosen = 0.0
    for _ in range(3):
        top = remaining.astype(jnp.bfloat16)
        chosen = chosen + jnp.dot(top, picks[...], preferred_element_type=jnp.float32)
        remaining = remaining - top.astype(jnp.float32)
    chosen = (chosen * (1.0 / (nvx * PLANE))).reshape(nvx // 2, NZ, 4 * LANES)
    for a in range(nvx):
        b = -a % nvx
        near, far = a % 2 * LANES, (2 + b % 2) * LANES
        sym[a] = chosen[a // 2, :, near : near + LANES] + chosen[b // 2, :, far : far + LANES]

    arrivals(arrived, 0)
    from_low, from_high = arrived_on.at[pl.ds(half, half)], arrived_on.at[pl.ds(0, half)]
    pl.when(has_low_x)(pltpu.make_async_copy(from_low, from_low, on_recv.at[0]).wait)
    pl.when(has_high_x)(pltpu.make_async_copy(from_high, from_high, on_recv.at[1]).wait)

    lane = lax.broadcasted_iota(jnp.int32, (1, 1, LANES), 2)
    used = lane < HALF
    quarter = LOCAL_V // 2

    def turn(values, by):
        return pltpu.roll(values, by, values.ndim - 1)

    blocks = (arrived[...] + arrived_on[...]).reshape(nvx, PARTS, NZ // 2, LANES)
    wide = []
    for part in range(PARTS):
        block = blocks[:, part]
        wide.append(jnp.concatenate([block, turn(block, LOCAL_V)], axis=1))
    moved[0] = jnp.where(lane < LOCAL_V, wide[0], jnp.where(used, turn(wide[1], LOCAL_V), 0.0))
    moved[1] = jnp.where(
        lane < quarter, turn(wide[1], LANES - quarter), jnp.where(used, turn(wide[2], quarter), 0.0)
    )

    def halo_copies(step):
        routes = [
            (state.at[step, :, pl.ds(mid, mid)], halo_x.at[step, :, pl.ds(mid, mid)], (me_c + 1, me_v)),
            (state.at[step, :, pl.ds(0, mid)], halo_x.at[step, :, pl.ds(0, mid)], (me_c - 1, me_v)),
            (state.at[step, 1], halo_y.at[step, 1], (me_c, owner_of(me_y + 1))),
            (state.at[step, 0], halo_y.at[step, 0], (me_c, owner_of(me_y - 1))),
        ]
        return [
            pltpu.make_async_remote_copy(
                src_ref=src,
                dst_ref=dst,
                send_sem=halo_send.at[n, step],
                recv_sem=halo_recv.at[n, step],
                device_id=to,
                device_id_type=MESH,
            )
            for n, (src, dst, to) in enumerate(routes)
        ]

    sends = [has_high_x, has_low_x, has_high_y, has_low_y]
    receives = [has_low_x, has_high_x, has_low_y, has_high_y]

    def speed_x(a):
        return (2 * a - (nvx - 1)) * 0.5 * SPACING

    def transport(step):
        copies = halo_copies(step)
        for copy, present in zip(copies, sends):
            pl.when(present)(copy.start)

        own = []
        for h in (0, 1):
            here = state[step, h]
            own.append(
                here * lanes[h]
                + pltpu.roll(here, 1, 1) * lanes[4]
                + pltpu.roll(here, NZ - 1, 1) * lanes[5]
            )

        for copy, present in zip(copies, receives):
            pl.when(present)(copy.wait_recv)

        for h in (0, 1):
            side = []
            for a in range(nvx):
                weight = COURANT * abs(speed_x(a))
                side.append(own[h][a] + (halo_x[step, h, a] - state[step, h, a]) * weight)
            moved[h] = jnp.stack(side) + halo_y[step, h] * lanes[2 + h]

    def advance(step, carry):
        rows = jnp.concatenate([moved[h].reshape(nvx * NZ, LANES) for h in (0, 1)], axis=1)

        span = 2 * LANES
        plane = jnp.dot(three_parts(rows), mats[: 3 * span], preferred_element_type=jnp.float32)
        plane = plane.reshape(nvx, NZ, span)
        real, imag = fourier(
            [plane[a, :, :LANES] for a in range(nvx)], [plane[a, :, LANES:] for a in range(nvx)], -1
        )
        spec[0] = jnp.stack(real)
        spec[1] = jnp.stack(imag)

        def weigh(w, carry):
            gains = [sym[a, pl.ds(w, 1), :] for a in range(nvx)]
            real, imag = fourier(
                [spec[0, a] * gains[a] for a in range(nvx)], [spec[1, a] * gains[a] for a in range(nvx)], 1
            )
            line = jnp.concatenate(
                [jnp.concatenate(real, axis=0), jnp.concatenate(imag, axis=0)], axis=1
            )
            tall = nvx * NZ
            back[pl.ds(pl.multiple_of(w * tall, tall), tall)] = three_parts(line)
            return carry

        lax.fori_loop(0, KERNELS, weigh, 0, unroll=True)
        found = jnp.dot(back[...], mats[3 * span :], preferred_element_type=jnp.float32)
        found = found.reshape(KERNELS, nvx * NZ, span)
        change = found[0] * found[2] + found[1] * found[3] - rows * found[4]
        after = rows + COLLISION_STEP * change
        for h in (0, 1):
            state[step, h] = after[:, h * LANES : (h + 1) * LANES].reshape(nvx, NZ, LANES)
        pl.when(step < STEPS - 1)(lambda: transport(step))
        return carry

    lax.fori_loop(0, STEPS, advance, 0)

    low, high = state[STEPS - 1, 0], state[STEPS - 1, 1]
    parts = [
        low,
        jnp.where(lane < quarter, turn(low, LOCAL_V), turn(high, quarter)),
        turn(high, LANES - quarter),
    ]
    stacked = [
        jnp.where(lane < LOCAL_V, part[:, : NZ // 2], turn(part, LOCAL_V)[:, NZ // 2 :]) for part in parts
    ]
    packed_back[...] = jnp.stack(stacked, axis=1).reshape(columns, NZ // 2, LANES)
    def send_home(to, column):
        send_block(packed_back, arrived_back, 1, to, to, me_y)

    in_place_order(send_home, 0, ring // 4)

    both = low + high
    sums_low, sums_high = jnp.sum(low, axis=0), jnp.sum(high, axis=0)
    along, squared = 0.0, 0.0
    for a in range(nvx):
        along = along + both[a] * (SPACING**3 * speed_x(a))
        squared = squared + both[a] * (SPACING**3 * speed_x(a) ** 2)
    totals = [
        along,
        sums_low * lanes[6] + sums_high * lanes[7],
        (sums_low + sums_high) * lanes[8],
        squared + sums_low * lanes[9] + sums_high * lanes[10],
    ]
    pl.when(moved_home)(uses_copy.wait_recv)
    counted = uses[...]
    shares = [
        jnp.sum(jnp.sum(total, axis=1, keepdims=True) * counted, axis=0, keepdims=True) for total in totals
    ]
    shares.append(jnp.zeros((NZ - MOMENTS, LANES), jnp.float32))
    share = jnp.concatenate(shares, axis=0)
    mine[...] = share
    all_others, rest = others.at[pl.ds(0, cells)], others.at[pl.ds(0, cells - 1)]

    def give(j, carry):
        to = lax.rem(me_c + j, cells)
        pltpu.make_async_remote_copy(
            src_ref=mine,
            dst_ref=others.at[me_c],
            send_sem=load_send,
            recv_sem=load_recv,
            device_id=(to, me_y),
            device_id_type=MESH,
        ).start()
        return carry

    lax.fori_loop(1, cells, give, 0)
    pl.when(moved_home)(lambda: give(0, None))

    in_place_order(send_home, ring // 4, ring)
    arrived_back[pl.ds(me_y, 1)] = packed_back[pl.ds(me_v, 1)]

    @pl.when(moved_home)
    def _():
        pltpu.make_async_copy(all_others, all_others, load_recv).wait()

    @pl.when(jnp.logical_not(moved_home))
    def _():
        others[pl.ds(me_c, 1)] = share[None]
        pltpu.make_async_copy(rest, rest, load_recv).wait()

    summed = jnp.sum(others[...], axis=0)
    picked = slot - PANEL_DEV * me_c
    columns_out = [
        jnp.sum(jnp.where(picked == k, summed, 0.0), axis=1, keepdims=True) for k in range(PANEL_DEV)
    ]
    loads[...] = jnp.concatenate(columns_out, axis=1)[:MOMENTS]

    arrivals(arrived_back, 1)
    for start in range(0, columns, LANES // NZ):
        stop = min(start + LANES // NZ, columns)
        block = arrived_back[start:stop]
        tall = jnp.concatenate([block, turn(block, LOCAL_V)], axis=1).reshape((stop - start) * NZ, LANES)
        out[:, 0, start * NZ : stop * NZ] = jnp.transpose(tall)[:LOCAL_V]

    departures(packed, 0)
    pl.when(has_next)(pltpu.make_async_copy(packed_on, packed_on, on_send).wait)
    departures(packed_back, 1)
    pl.when(moved_home)(uses_copy.wait_send)
    pl.when(moved_home)(pltpu.make_async_copy(all_others, all_others, load_send).wait)
    pl.when(jnp.logical_not(moved_home))(pltpu.make_async_copy(rest, rest, load_send).wait)

    def finish(step, carry):
        for copy, present in zip(halo_copies(step), sends):
            pl.when(present)(copy.wait_send)
        return carry

    lax.fori_loop(0, STEPS - 1, finish, 0)


def per_device(cells, columns, distribution, gain_left, gain_right, loss_kernel, wall_cell, wall_count, wall_panel):
    nvx = columns // PARTS
    local, _, width = distribution.shape
    f32 = jnp.float32
    loss = loss_kernel.reshape(1, -1)
    picks = jnp.asarray(weight_selectors())
    mats = jnp.asarray(plane_matrices())
    tables = jnp.asarray(lane_tables())
    rows = jnp.asarray(row_tables())
    anywhere = pl.BlockSpec(memory_space=pl.ANY)
    in_vmem = pl.BlockSpec(memory_space=pltpu.VMEM)
    dma = pltpu.SemaphoreType.DMA
    out, loads = pl.pallas_call(
        functools.partial(kernel, cells, columns),
        out_shape=(
            pltpu.VMEM((local, 1, width), f32),
            pltpu.VMEM((MOMENTS, PANEL_DEV), f32),
        ),
        in_specs=[anywhere] * 11,
        out_specs=(in_vmem, in_vmem),
        scratch_shapes=[
            pltpu.VMEM(distribution.shape, f32),
            pltpu.SMEM(wall_cell.shape, jnp.int32),
            pltpu.SMEM(wall_count.shape, jnp.int32),
            pltpu.SMEM(wall_panel.shape, jnp.int32),
            pltpu.VMEM(gain_left.shape, f32),
            pltpu.VMEM(gain_right.shape, f32),
            pltpu.VMEM(loss.shape, f32),
            pltpu.VMEM(picks.shape, jnp.bfloat16),
            pltpu.VMEM(mats.shape, jnp.bfloat16),
            pltpu.VMEM(tables.shape, f32),
            pltpu.VMEM(rows.shape, f32),
            pltpu.VMEM((columns + 2, NZ, LANES), f32),
            pltpu.VMEM((columns, NZ // 2, LANES), f32),
            pltpu.VMEM((columns, NZ // 2, LANES), f32),
            pltpu.VMEM((columns, NZ // 2, LANES), f32),
            pltpu.VMEM((columns, NZ // 2, LANES), f32),
            pltpu.VMEM((2, nvx, NZ, LANES), f32),
            pltpu.VMEM((columns, NZ // 2, LANES), f32),
            pltpu.VMEM((columns, NZ // 2, LANES), f32),
            pltpu.VMEM((STEPS, 2, nvx, NZ, LANES), f32),
            pltpu.VMEM((STEPS - 1, 2, nvx, NZ, LANES), f32),
            pltpu.VMEM((STEPS - 1, 2, nvx, NZ, LANES), f32),
            pltpu.VMEM((nvx // 2, NZ, 2 * PLANE), f32),
            pltpu.VMEM((nvx, NZ, LANES), f32),
            pltpu.VMEM((2, nvx, NZ, LANES), f32),
            pltpu.VMEM((KERNELS * nvx * NZ, 6 * LANES), jnp.bfloat16),
            pltpu.VMEM((NZ, LANES), f32),
            pltpu.VMEM((NZ, LANES), f32),
            pltpu.VMEM((NZ, LANES), f32),
            pltpu.VMEM((cells, NZ, LANES), f32),
            dma((11,)),
            dma((4, STEPS - 1)),
            dma((4, STEPS - 1)),
            dma((2,)),
            dma((2,)),
            dma,
            dma((2,)),
            dma,
            dma,
            dma,
            dma,
        ],
        compiler_params=pltpu.CompilerParams(
            collective_id=0, has_side_effects=True, vmem_limit_bytes=VMEM_LIMIT
        ),
        cost_estimate=pl.CostEstimate(flops=1_000_000_000, bytes_accessed=2_000_000, transcendentals=0),
        name="collide",
    )(distribution, wall_cell, wall_count, wall_panel, gain_left, gain_right, loss, picks, mats, tables, rows)
    return out, loads


def solution(mesh):
    placed = (
        P("vel", "cell", None),
        P(),
        P(),
        P(),
        P("cell", "vel", None),
        P("cell", "vel"),
        P("cell", "vel", None),
    )
    return jax.shard_map(
        functools.partial(per_device, mesh.shape["cell"], mesh.shape["vel"]),
        mesh=mesh,
        in_specs=placed,
        out_specs=(P("vel", "cell", None), P(None, ("cell", "vel"))),
        check_vma=False,
    )
```

```python
import functools
import math

import jax
import jax.numpy as jnp
import ml_dtypes
import numpy as np
from jax import lax
from jax.experimental import pallas as pl
from jax.experimental.pallas import tpu as pltpu
from jax.sharding import PartitionSpec as P

NVY = 16
NVZ = 12
PLANE = NVY * NVZ
HALF = PLANE // 2
KEPT = NVZ // 2 + 1
KERNELS = 5
DIRS = 2
MOMENTS = 4
STEPS = 3
NZ = 8
WALL_SLOTS = 8
PANEL_DEV = 4
LOCAL_V = 64
PARTS = PLANE // LOCAL_V
LANES = 128
VMEM_LIMIT = 60 * 1024 * 1024

SPACING = 0.5
COURANT = 0.09
COLLISION_STEP = 0.3

MESH = pl.DeviceIdType.MESH


def split(values):
    high = values.astype(ml_dtypes.bfloat16)
    low = (values - high.astype(np.float64)).astype(ml_dtypes.bfloat16)
    return high, low


def plane_matrices():
    table = np.zeros((2 * LANES, 2 * LANES))
    for point in range(PLANE):
        b, c = divmod(point, NVZ)
        row = b // (NVY // 2) * LANES + point % HALF
        for kb in range(NVY):
            for kc in range(KEPT):
                angle = 2.0 * math.pi * ((b * kb % NVY) / NVY + (c * kc % NVZ) / NVZ)
                table[row, kb * KEPT + kc] = math.cos(angle)
                table[row, LANES + kb * KEPT + kc] = -math.sin(angle)
    high, low = split(table)
    return np.concatenate([high, high, low, high.T, high.T, low.T], axis=0)


def weight_selectors():
    table = np.zeros((2 * PLANE, 4 * LANES))
    for kb in range(NVY):
        for kc in range(KEPT):
            share = 0.5 if kc in (0, KEPT - 1) else 1.0
            column = kb * KEPT + kc
            there = kb * NVZ + kc
            mirror = -kb % NVY * NVZ + -kc % NVZ
            for half in (0, 1):
                table[half * PLANE + there, half * LANES + column] = share
                table[half * PLANE + mirror, (2 + half) * LANES + column] = share
    return table.astype(ml_dtypes.bfloat16)


def lane_tables():
    lane = np.arange(LANES)
    used = (lane < HALF).astype(np.float64)
    vz = (2 * (lane % NVZ) - (NVZ - 1)) * 0.5 * SPACING * used
    vy = [(2 * (lane // NVZ + h * NVY // 2) - (NVY - 1)) * 0.5 * SPACING * used for h in (0, 1)]
    z = np.arange(NZ)[:, None]
    rows = []
    for h in (0, 1):
        rows.append(1.0 - COURANT * (np.abs(vy[h]) + np.abs(vz)) + 0.0 * z)
    for h in (0, 1):
        rows.append(COURANT * np.abs(vy[h]) + 0.0 * z)
    rows.append(COURANT * np.maximum(vz, 0.0) * (z > 0))
    rows.append(COURANT * np.maximum(-vz, 0.0) * (z < NZ - 1))
    cube = SPACING**3
    rows.append(cube * vy[0] + 0.0 * z)
    rows.append(cube * vy[1] + 0.0 * z)
    rows.append(cube * vz + 0.0 * z)
    rows.append(cube * (vy[0] ** 2 + vz**2) + 0.0 * z)
    rows.append(cube * (vy[1] ** 2 + vz**2) + 0.0 * z)
    return np.stack(rows).astype(np.float32)


def row_tables():
    lane = np.arange(LANES)
    z = (np.arange(NZ)[:, None] + lane // LOCAL_V * (NZ // 2)) % NZ
    parts = []
    for part in range(PARTS):
        point = part * LOCAL_V + lane % LOCAL_V
        vy = (2 * (point // NVZ) - (NVY - 1)) * 0.5 * SPACING
        vz = (2 * (point % NVZ) - (NVZ - 1)) * 0.5 * SPACING
        parts.append([
            1.0 - COURANT * (np.abs(vy) + np.abs(vz)) + 0.0 * z,
            COURANT * np.maximum(vy, 0.0) + 0.0 * z,
            COURANT * np.maximum(-vy, 0.0) + 0.0 * z,
            COURANT * np.maximum(vz, 0.0) * (z > 0),
            COURANT * np.maximum(-vz, 0.0) * (z < NZ - 1),
        ])
    return np.array(parts).astype(np.float32)


def fourier(real, imag, sign):
    count = len(real)
    if count == 1:
        return real, imag
    even_r, even_i = fourier(real[::2], imag[::2], sign)
    odd_r, odd_i = fourier(real[1::2], imag[1::2], sign)
    out_r, out_i = [None] * count, [None] * count
    half = count // 2
    for k in range(half):
        r, i = odd_r[k], odd_i[k]
        if k == 0:
            pass
        elif 4 * k == count:
            r, i = (-i, r) if sign > 0 else (i, -r)
        else:
            cos = math.cos(2.0 * math.pi * k / count)
            sin = sign * math.sin(2.0 * math.pi * k / count)
            if 8 * k == count or 8 * k == 3 * count:
                size = math.sqrt(0.5)
                up, across = cos / abs(cos), sin / abs(sin)
                first = r - i if up == across else r + i
                second = r + i if up == across else (i - r)
                if up > 0:
                    r, i = (first * size, second * size)
                else:
                    r, i = (first * -size, second * -size)
            else:
                r, i = r * cos - i * sin, r * sin + i * cos
        out_r[k], out_i[k] = even_r[k] + r, even_i[k] + i
        out_r[k + half], out_i[k + half] = even_r[k] - r, even_i[k] - i
    return out_r, out_i


def three_parts(values):
    top = values.astype(jnp.bfloat16)
    rest = (values - top.astype(jnp.float32)).astype(jnp.bfloat16)
    return jnp.concatenate([top, rest, top], axis=1)


def kernel(
    cells, columns,
    x_in, wall_cell_in, wall_count_in, wall_panel_in, left_in, right_in, loss_in, picks_in, mats_in, lanes_in, own_in,
    out, loads,
    x_v, wall_cell, wall_count, wall_panel, left, right, loss, picks, mats, lanes, own_rows,
    field, packed, packed_on, arrived, arrived_on, moved, packed_back, arrived_back, state, halo_x, halo_y,
    planes, sym, spec, back, my_uses, uses, mine, others,
    in_sems, halo_send, halo_recv, swap_send, swap_recv, on_send, on_recv, load_send, load_recv, uses_send, uses_recv,
):
    nvx = columns // PARTS
    mid = nvx // 2
    me_c = lax.axis_index("cell")
    me_v = lax.axis_index("vel")

    lines = 4 if columns % 4 == 0 else 2
    ring = columns // lines

    def owner_of(column):
        line, place = column // ring, lax.rem(column, ring)
        return line * ring + lax.rem(place + 1 - line + ring, ring)

    def column_of(device):
        line, place = device // ring, lax.rem(device, ring)
        return line * ring + lax.rem(place - 1 + line + ring, ring)

    half = columns // 2
    goes_up = me_v >= half
    next_c = me_c + jnp.where(goes_up, 1, -1)
    has_next = jnp.logical_and(next_c >= 0, next_c < cells)
    me_y = column_of(me_v)
    my_owner = owner_of(me_v)
    line, place = me_v // ring, lax.rem(me_v, ring)

    def wrapped(value, count):
        return jnp.where(value >= count, value - count, value)

    across = [lines // 2 + (m + 1) // 2 * (1 if m % 2 else -1) for m in range(lines)]
    to_lines = [wrapped(line + shift % lines, lines) for shift in across]

    def visit_line(visit, there, m):
        column = there + to_lines[m] - 1
        column = wrapped(jnp.where(column < 0, column + ring, column), ring)
        visit(to_lines[m] * ring + there, to_lines[m] * ring + column)

    def farthest_first(visit, start, stop):
        def one_round(n, carry):
            away = (n + 1) // 2
            there = wrapped(place + ring // 2 + jnp.where(lax.rem(n, 2) == 1, away, -away), ring)
            for m in range(lines):
                visit_line(visit, there, m)
            return carry

        lax.fori_loop(start, min(stop, ring - 1), one_round, 0)
        if stop == ring:
            for m in range(lines - 1):
                visit_line(visit, place, m)

    def in_place_order(visit, start, stop):
        def one_round(there, carry):
            for m in range(lines - 1):
                visit_line(visit, there, m)
            pl.when(there != place)(lambda: visit_line(visit, there, lines - 1))
            return carry

        lax.fori_loop(start, stop, one_round, 0)

    pairs = [
        (x_in, x_v), (wall_cell_in, wall_cell), (wall_count_in, wall_count), (wall_panel_in, wall_panel),
        (left_in, left), (right_in, right), (loss_in, loss), (picks_in, picks), (mats_in, mats), (lanes_in, lanes), (own_in, own_rows),
    ]
    loads_in = [pltpu.make_async_copy(src, dst, in_sems.at[n]) for n, (src, dst) in enumerate(pairs)]
    loads_in[0].start()

    barrier = pltpu.get_barrier_semaphore()

    def greet_column(to, column):
        pl.semaphore_signal(barrier, inc=1, device_id=(me_c, to), device_id_type=MESH)
        greet_sender(to)

    def greet_sender(to):
        upward = to >= half
        present = jnp.logical_or(jnp.logical_and(upward, has_low_x), jnp.logical_and(to < half, has_high_x))

        @pl.when(present)
        def _():
            neighbour = me_c + jnp.where(upward, -1, 1)
            pl.semaphore_signal(barrier, inc=1, device_id=(neighbour, to), device_id_type=MESH)

    def greet_row(j, carry):
        to = lax.rem(me_c + j, cells)
        pl.semaphore_signal(barrier, inc=1, device_id=(to, my_owner), device_id_type=MESH)
        return carry

    has_low_x, has_high_x = me_c > 0, me_c < cells - 1
    has_low_y, has_high_y = me_y > 0, me_y < columns - 1
    moved_home = my_owner != me_v
    greetings = [(jnp.logical_and(moved_home, has_low_x), -1), (jnp.logical_and(moved_home, has_high_x), 1)]

    farthest_first(greet_column, 0, ring // 4)
    lax.fori_loop(1, cells, greet_row, 0)
    farthest_first(greet_column, ring // 4, ring)
    greet_sender(me_v)
    greeted = columns - 1 + cells - 1 + jnp.where(has_next, columns, 0)
    for present, way in greetings:
        greeted = greeted + jnp.where(present, 1, 0)

        @pl.when(present)
        def _():
            pl.semaphore_signal(barrier, inc=1, device_id=(me_c + way, me_v), device_id_type=MESH)

    for copy in loads_in[1:]:
        copy.start()

    loads_in[0].wait()
    width = NZ * columns
    for start in range(0, width, LANES):
        stop = min(start + LANES, width)
        tile = x_v[:, 0, start:stop]
        back_by_half = jnp.concatenate([tile[:, NZ // 2 :], tile[:, : NZ // 2]], axis=1)
        on_by_half = jnp.concatenate([tile[:, -(NZ // 2) :], tile[:, : -(NZ // 2)]], axis=1)
        place_z = lax.rem(lax.broadcasted_iota(jnp.int32, tile.shape, 1), NZ)
        shifted = jnp.where(place_z < NZ // 2, back_by_half, on_by_half)
        turned = jnp.transpose(jnp.concatenate([tile, shifted], axis=0))
        turned = turned.reshape((stop - start) // NZ, NZ, LANES)
        field[1 + start // NZ : 1 + stop // NZ] = turned
    field[0] = jnp.zeros((NZ, LANES), jnp.float32)
    field[columns + 1] = jnp.zeros((NZ, LANES), jnp.float32)

    loads_in[10].wait()
    part = lax.rem(me_v, PARTS)
    weight_x = COURANT * 0.5 * SPACING * jnp.abs(2 * (me_v // PARTS) - (nvx - 1)).astype(jnp.float32)
    here = field[1 : columns + 1]
    stays = (
        here * (own_rows[part, 0] - weight_x)
        + field[:columns] * own_rows[part, 1]
        + field[2:] * own_rows[part, 2]
        + pltpu.roll(here, 1, 1) * own_rows[part, 3]
        + pltpu.roll(here, NZ - 1, 1) * own_rows[part, 4]
    )
    packed[...] = stays[:, : NZ // 2]
    packed_on[...] = here[:, : NZ // 2] * weight_x
    arrived[pl.ds(me_v, 1)] = packed[pl.ds(me_y, 1)]

    @pl.when(jnp.logical_not(has_low_x))
    def _():
        arrived_on[half:] = jnp.zeros((half, NZ // 2, LANES), jnp.float32)

    @pl.when(jnp.logical_not(has_high_x))
    def _():
        arrived_on[:half] = jnp.zeros((half, NZ // 2, LANES), jnp.float32)

    depth = lax.broadcasted_iota(jnp.int32, (NZ, LANES), 0)
    slot = lax.broadcasted_iota(jnp.int32, (NZ, LANES), 1)
    for copy in loads_in[1:4]:
        copy.wait()
    counted = jnp.zeros((NZ, LANES), jnp.float32)
    per_owner = PANEL_DEV * columns
    for n in range(WALL_SLOTS):
        panel = wall_panel[0, 0, n]
        target = panel // per_owner * PANEL_DEV + lax.rem(panel, PANEL_DEV)
        target = jnp.where(n < wall_count[0, 0], target, -1)
        hit = jnp.logical_and(depth == wall_cell[0, 0, n], slot == target)
        counted = counted + jnp.where(hit, 1.0, 0.0)
    my_uses[...] = counted

    @pl.when(jnp.logical_not(moved_home))
    def _():
        uses[...] = counted

    pl.semaphore_wait(barrier, greeted)

    def send_block(source, target, which, to, source_slot, target_slot):
        pltpu.make_async_remote_copy(
            src_ref=source.at[source_slot],
            dst_ref=target.at[target_slot],
            send_sem=swap_send.at[which],
            recv_sem=swap_recv.at[which],
            device_id=(me_c, to),
            device_id_type=MESH,
        ).start()

    def arrivals(target, which):
        rest = target.at[pl.ds(0, columns - 1)]
        pltpu.make_async_copy(rest, rest, swap_recv.at[which]).wait()

    def departures(source, which):
        rest = source.at[pl.ds(0, columns - 1)]
        pltpu.make_async_copy(rest, rest, swap_send.at[which]).wait()

    on_way = jnp.where(goes_up, 0, 1)

    def send_on(to, column):
        pltpu.make_async_remote_copy(
            src_ref=packed_on.at[column],
            dst_ref=arrived_on.at[me_v],
            send_sem=on_send,
            recv_sem=on_recv.at[on_way],
            device_id=(next_c, to),
            device_id_type=MESH,
        ).start()

    def send_one(to, column):
        send_block(packed, arrived, 0, to, column, me_v)

    def send_both(to, column):
        send_one(to, column)
        send_on(to, column)

    @pl.when(has_next)
    def _():
        farthest_first(send_both, 0, ring)
        send_on(me_v, me_y)

    pl.when(jnp.logical_not(has_next))(lambda: farthest_first(send_one, 0, ring))

    uses_copy = pltpu.make_async_remote_copy(
        src_ref=my_uses,
        dst_ref=uses,
        send_sem=uses_send,
        recv_sem=uses_recv,
        device_id=(me_c, my_owner),
        device_id_type=MESH,
    )
    pl.when(moved_home)(uses_copy.start)

    @pl.when(jnp.logical_not(has_low_x))
    def _():
        halo_x[:, :, mid:] = jnp.zeros((STEPS - 1, 2, mid, NZ, LANES), jnp.float32)

    @pl.when(jnp.logical_not(has_high_x))
    def _():
        halo_x[:, :, :mid] = jnp.zeros((STEPS - 1, 2, mid, NZ, LANES), jnp.float32)

    @pl.when(jnp.logical_not(has_low_y))
    def _():
        halo_y[:, 1] = jnp.zeros((STEPS - 1, nvx, NZ, LANES), jnp.float32)

    @pl.when(jnp.logical_not(has_high_y))
    def _():
        halo_y[:, 0] = jnp.zeros((STEPS - 1, nvx, NZ, LANES), jnp.float32)

    for copy in loads_in[4:10]:
        copy.wait()
    for pair in range(nvx // 2):
        span = slice(pair * 2 * PLANE, (pair + 1) * 2 * PLANE)
        planes[pair, :DIRS] = left[:, span]
        planes[pair, DIRS : 2 * DIRS] = right[:, span]
        planes[pair, 2 * DIRS : KERNELS] = loss[:, span]
        planes[pair, KERNELS:] = jnp.zeros((NZ - KERNELS, 2 * PLANE), jnp.float32)
    remaining = planes[...].reshape(nvx // 2 * NZ, 2 * PLANE)
    chosen = 0.0
    for _ in range(3):
        top = remaining.astype(jnp.bfloat16)
        chosen = chosen + jnp.dot(top, picks[...], preferred_element_type=jnp.float32)
        remaining = remaining - top.astype(jnp.float32)
    chosen = (chosen * (1.0 / (nvx * PLANE))).reshape(nvx // 2, NZ, 4 * LANES)
    for a in range(nvx):
        b = -a % nvx
        near, far = a % 2 * LANES, (2 + b % 2) * LANES
        sym[a] = chosen[a // 2, :, near : near + LANES] + chosen[b // 2, :, far : far + LANES]

    arrivals(arrived, 0)
    from_low, from_high = arrived_on.at[pl.ds(half, half)], arrived_on.at[pl.ds(0, half)]
    pl.when(has_low_x)(pltpu.make_async_copy(from_low, from_low, on_recv.at[0]).wait)
    pl.when(has_high_x)(pltpu.make_async_copy(from_high, from_high, on_recv.at[1]).wait)

    lane = lax.broadcasted_iota(jnp.int32, (1, 1, LANES), 2)
    used = lane < HALF
    quarter = LOCAL_V // 2

    def turn(values, by):
        return pltpu.roll(values, by, values.ndim - 1)

    blocks = (arrived[...] + arrived_on[...]).reshape(nvx, PARTS, NZ // 2, LANES)
    wide = []
    for part in range(PARTS):
        block = blocks[:, part]
        wide.append(jnp.concatenate([block, turn(block, LOCAL_V)], axis=1))
    moved[0] = jnp.where(lane < LOCAL_V, wide[0], jnp.where(used, turn(wide[1], LOCAL_V), 0.0))
    moved[1] = jnp.where(
        lane < quarter, turn(wide[1], LANES - quarter), jnp.where(used, turn(wide[2], quarter), 0.0)
    )

    def halo_copies(step):
        routes = [
            (state.at[step, 1], halo_y.at[step, 1], (me_c, owner_of(me_y + 1))),
            (state.at[step, 0], halo_y.at[step, 0], (me_c, owner_of(me_y - 1))),
            (state.at[step, :, pl.ds(mid, mid)], halo_x.at[step, :, pl.ds(mid, mid)], (me_c + 1, me_v)),
            (state.at[step, :, pl.ds(0, mid)], halo_x.at[step, :, pl.ds(0, mid)], (me_c - 1, me_v)),
        ]
        return [
            pltpu.make_async_remote_copy(
                src_ref=src,
                dst_ref=dst,
                send_sem=halo_send.at[n, step],
                recv_sem=halo_recv.at[n, step],
                device_id=to,
                device_id_type=MESH,
            )
            for n, (src, dst, to) in enumerate(routes)
        ]

    sends = [has_high_y, has_low_y, has_high_x, has_low_x]
    receives = [has_low_y, has_high_y, has_low_x, has_high_x]

    def speed_x(a):
        return (2 * a - (nvx - 1)) * 0.5 * SPACING

    def transport(step):
        copies = halo_copies(step)
        for copy, present in zip(copies, sends):
            pl.when(present)(copy.start)

        own = []
        for h in (0, 1):
            here = state[step, h]
            own.append(
                here * lanes[h]
                + pltpu.roll(here, 1, 1) * lanes[4]
                + pltpu.roll(here, NZ - 1, 1) * lanes[5]
            )

        for copy, present in zip(copies, receives):
            pl.when(present)(copy.wait_recv)

        for h in (0, 1):
            side = []
            for a in range(nvx):
                weight = COURANT * abs(speed_x(a))
                side.append(own[h][a] + (halo_x[step, h, a] - state[step, h, a]) * weight)
            moved[h] = jnp.stack(side) + halo_y[step, h] * lanes[2 + h]

    def advance(step, carry):
        rows = jnp.concatenate([moved[h].reshape(nvx * NZ, LANES) for h in (0, 1)], axis=1)

        span = 2 * LANES
        plane = jnp.dot(three_parts(rows), mats[: 3 * span], preferred_element_type=jnp.float32)
        plane = plane.reshape(nvx, NZ, span)
        real, imag = fourier(
            [plane[a, :, :LANES] for a in range(nvx)], [plane[a, :, LANES:] for a in range(nvx)], -1
        )
        spec[0] = jnp.stack(real)
        spec[1] = jnp.stack(imag)

        def weigh(w, carry):
            gains = [sym[a, pl.ds(w, 1), :] for a in range(nvx)]
            real, imag = fourier(
                [spec[0, a] * gains[a] for a in range(nvx)], [spec[1, a] * gains[a] for a in range(nvx)], 1
            )
            line = jnp.concatenate(
                [jnp.concatenate(real, axis=0), jnp.concatenate(imag, axis=0)], axis=1
            )
            tall = nvx * NZ
            back[pl.ds(pl.multiple_of(w * tall, tall), tall)] = three_parts(line)
            return carry

        lax.fori_loop(0, KERNELS, weigh, 0, unroll=True)
        found = jnp.dot(back[...], mats[3 * span :], preferred_element_type=jnp.float32)
        found = found.reshape(KERNELS, nvx * NZ, span)
        change = found[0] * found[2] + found[1] * found[3] - rows * found[4]
        after = rows + COLLISION_STEP * change
        for h in (0, 1):
            state[step, h] = after[:, h * LANES : (h + 1) * LANES].reshape(nvx, NZ, LANES)
        pl.when(step < STEPS - 1)(lambda: transport(step))
        return carry

    lax.fori_loop(0, STEPS, advance, 0)

    low, high = state[STEPS - 1, 0], state[STEPS - 1, 1]
    parts = [
        low,
        jnp.where(lane < quarter, turn(low, LOCAL_V), turn(high, quarter)),
        turn(high, LANES - quarter),
    ]
    stacked = [
        jnp.where(lane < LOCAL_V, part[:, : NZ // 2], turn(part, LOCAL_V)[:, NZ // 2 :]) for part in parts
    ]
    packed_back[...] = jnp.stack(stacked, axis=1).reshape(columns, NZ // 2, LANES)
    def send_home(to, column):
        send_block(packed_back, arrived_back, 1, to, to, me_y)

    in_place_order(send_home, 0, ring // 4)

    both = low + high
    sums_low, sums_high = jnp.sum(low, axis=0), jnp.sum(high, axis=0)
    along, squared = 0.0, 0.0
    for a in range(nvx):
        along = along + both[a] * (SPACING**3 * speed_x(a))
        squared = squared + both[a] * (SPACING**3 * speed_x(a) ** 2)
    totals = [
        along,
        sums_low * lanes[6] + sums_high * lanes[7],
        (sums_low + sums_high) * lanes[8],
        squared + sums_low * lanes[9] + sums_high * lanes[10],
    ]
    pl.when(moved_home)(uses_copy.wait_recv)
    counted = uses[...]
    shares = [
        jnp.sum(jnp.sum(total, axis=1, keepdims=True) * counted, axis=0, keepdims=True) for total in totals
    ]
    shares.append(jnp.zeros((NZ - MOMENTS, LANES), jnp.float32))
    share = jnp.concatenate(shares, axis=0)
    mine[...] = share
    all_others, rest = others.at[pl.ds(0, cells)], others.at[pl.ds(0, cells - 1)]

    def give(j, carry):
        to = lax.rem(me_c + j, cells)
        pltpu.make_async_remote_copy(
            src_ref=mine,
            dst_ref=others.at[me_c],
            send_sem=load_send,
            recv_sem=load_recv,
            device_id=(to, me_y),
            device_id_type=MESH,
        ).start()
        return carry

    lax.fori_loop(1, cells, give, 0)
    pl.when(moved_home)(lambda: give(0, None))

    in_place_order(send_home, ring // 4, ring)
    arrived_back[pl.ds(me_y, 1)] = packed_back[pl.ds(me_v, 1)]

    @pl.when(moved_home)
    def _():
        pltpu.make_async_copy(all_others, all_others, load_recv).wait()

    @pl.when(jnp.logical_not(moved_home))
    def _():
        others[pl.ds(me_c, 1)] = share[None]
        pltpu.make_async_copy(rest, rest, load_recv).wait()

    summed = jnp.sum(others[...], axis=0)
    picked = slot - PANEL_DEV * me_c
    columns_out = [
        jnp.sum(jnp.where(picked == k, summed, 0.0), axis=1, keepdims=True) for k in range(PANEL_DEV)
    ]
    loads[...] = jnp.concatenate(columns_out, axis=1)[:MOMENTS]

    arrivals(arrived_back, 1)
    for start in range(0, columns, LANES // NZ):
        stop = min(start + LANES // NZ, columns)
        block = arrived_back[start:stop]
        tall = jnp.concatenate([block, turn(block, LOCAL_V)], axis=1).reshape((stop - start) * NZ, LANES)
        out[:, 0, start * NZ : stop * NZ] = jnp.transpose(tall)[:LOCAL_V]

    departures(packed, 0)
    pl.when(has_next)(pltpu.make_async_copy(packed_on, packed_on, on_send).wait)
    departures(packed_back, 1)
    pl.when(moved_home)(uses_copy.wait_send)
    pl.when(moved_home)(pltpu.make_async_copy(all_others, all_others, load_send).wait)
    pl.when(jnp.logical_not(moved_home))(pltpu.make_async_copy(rest, rest, load_send).wait)

    def finish(step, carry):
        for copy, present in zip(halo_copies(step), sends):
            pl.when(present)(copy.wait_send)
        return carry

    lax.fori_loop(0, STEPS - 1, finish, 0)


def per_device(cells, columns, distribution, gain_left, gain_right, loss_kernel, wall_cell, wall_count, wall_panel):
    nvx = columns // PARTS
    local, _, width = distribution.shape
    f32 = jnp.float32
    loss = loss_kernel.reshape(1, -1)
    picks = jnp.asarray(weight_selectors())
    mats = jnp.asarray(plane_matrices())
    tables = jnp.asarray(lane_tables())
    rows = jnp.asarray(row_tables())
    anywhere = pl.BlockSpec(memory_space=pl.ANY)
    in_vmem = pl.BlockSpec(memory_space=pltpu.VMEM)
    dma = pltpu.SemaphoreType.DMA
    out, loads = pl.pallas_call(
        functools.partial(kernel, cells, columns),
        out_shape=(
            pltpu.VMEM((local, 1, width), f32),
            pltpu.VMEM((MOMENTS, PANEL_DEV), f32),
        ),
        in_specs=[anywhere] * 11,
        out_specs=(in_vmem, in_vmem),
        scratch_shapes=[
            pltpu.VMEM(distribution.shape, f32),
            pltpu.SMEM(wall_cell.shape, jnp.int32),
            pltpu.SMEM(wall_count.shape, jnp.int32),
            pltpu.SMEM(wall_panel.shape, jnp.int32),
            pltpu.VMEM(gain_left.shape, f32),
            pltpu.VMEM(gain_right.shape, f32),
            pltpu.VMEM(loss.shape, f32),
            pltpu.VMEM(picks.shape, jnp.bfloat16),
            pltpu.VMEM(mats.shape, jnp.bfloat16),
            pltpu.VMEM(tables.shape, f32),
            pltpu.VMEM(rows.shape, f32),
            pltpu.VMEM((columns + 2, NZ, LANES), f32),
            pltpu.VMEM((columns, NZ // 2, LANES), f32),
            pltpu.VMEM((columns, NZ // 2, LANES), f32),
            pltpu.VMEM((columns, NZ // 2, LANES), f32),
            pltpu.VMEM((columns, NZ // 2, LANES), f32),
            pltpu.VMEM((2, nvx, NZ, LANES), f32),
            pltpu.VMEM((columns, NZ // 2, LANES), f32),
            pltpu.VMEM((columns, NZ // 2, LANES), f32),
            pltpu.VMEM((STEPS, 2, nvx, NZ, LANES), f32),
            pltpu.VMEM((STEPS - 1, 2, nvx, NZ, LANES), f32),
            pltpu.VMEM((STEPS - 1, 2, nvx, NZ, LANES), f32),
            pltpu.VMEM((nvx // 2, NZ, 2 * PLANE), f32),
            pltpu.VMEM((nvx, NZ, LANES), f32),
            pltpu.VMEM((2, nvx, NZ, LANES), f32),
            pltpu.VMEM((KERNELS * nvx * NZ, 6 * LANES), jnp.bfloat16),
            pltpu.VMEM((NZ, LANES), f32),
            pltpu.VMEM((NZ, LANES), f32),
            pltpu.VMEM((NZ, LANES), f32),
            pltpu.VMEM((cells, NZ, LANES), f32),
            dma((11,)),
            dma((4, STEPS - 1)),
            dma((4, STEPS - 1)),
            dma((2,)),
            dma((2,)),
            dma,
            dma((2,)),
            dma,
            dma,
            dma,
            dma,
        ],
        compiler_params=pltpu.CompilerParams(
            collective_id=0, has_side_effects=True, vmem_limit_bytes=VMEM_LIMIT
        ),
        cost_estimate=pl.CostEstimate(flops=1_000_000_000, bytes_accessed=2_000_000, transcendentals=0),
        name="collide",
    )(distribution, wall_cell, wall_count, wall_panel, gain_left, gain_right, loss, picks, mats, tables, rows)
    return out, loads


def solution(mesh):
    placed = (
        P("vel", "cell", None),
        P(),
        P(),
        P(),
        P("cell", "vel", None),
        P("cell", "vel"),
        P("cell", "vel", None),
    )
    return jax.shard_map(
        functools.partial(per_device, mesh.shape["cell"], mesh.shape["vel"]),
        mesh=mesh,
        in_specs=placed,
        out_specs=(P("vel", "cell", None), P(None, ("cell", "vel"))),
        check_vma=False,
    )
```

```python
import functools
import math

import jax
import jax.numpy as jnp
import ml_dtypes
import numpy as np
from jax import lax
from jax.experimental import pallas as pl
from jax.experimental.pallas import tpu as pltpu
from jax.sharding import PartitionSpec as P

NVY = 16
NVZ = 12
PLANE = NVY * NVZ
HALF = PLANE // 2
KEPT = NVZ // 2 + 1
KERNELS = 5
DIRS = 2
MOMENTS = 4
STEPS = 3
NZ = 8
WALL_SLOTS = 8
PANEL_DEV = 4
LOCAL_V = 64
PARTS = PLANE // LOCAL_V
LANES = 128
VMEM_LIMIT = 60 * 1024 * 1024

SPACING = 0.5
COURANT = 0.09
COLLISION_STEP = 0.3

MESH = pl.DeviceIdType.MESH


def split(values):
    high = values.astype(ml_dtypes.bfloat16)
    low = (values - high.astype(np.float64)).astype(ml_dtypes.bfloat16)
    return high, low


def plane_matrices():
    table = np.zeros((2 * LANES, 2 * LANES))
    for point in range(PLANE):
        b, c = divmod(point, NVZ)
        row = b // (NVY // 2) * LANES + point % HALF
        for kb in range(NVY):
            for kc in range(KEPT):
                angle = 2.0 * math.pi * ((b * kb % NVY) / NVY + (c * kc % NVZ) / NVZ)
                table[row, kb * KEPT + kc] = math.cos(angle)
                table[row, LANES + kb * KEPT + kc] = -math.sin(angle)
    high, low = split(table)
    return np.concatenate([high, high, low, high.T, high.T, low.T], axis=0)


def weight_selectors():
    table = np.zeros((2 * PLANE, 4 * LANES))
    for kb in range(NVY):
        for kc in range(KEPT):
            share = 0.5 if kc in (0, KEPT - 1) else 1.0
            column = kb * KEPT + kc
            there = kb * NVZ + kc
            mirror = -kb % NVY * NVZ + -kc % NVZ
            for half in (0, 1):
                table[half * PLANE + there, half * LANES + column] = share
                table[half * PLANE + mirror, (2 + half) * LANES + column] = share
    return table.astype(ml_dtypes.bfloat16)


def lane_tables():
    lane = np.arange(LANES)
    used = (lane < HALF).astype(np.float64)
    vz = (2 * (lane % NVZ) - (NVZ - 1)) * 0.5 * SPACING * used
    vy = [(2 * (lane // NVZ + h * NVY // 2) - (NVY - 1)) * 0.5 * SPACING * used for h in (0, 1)]
    z = np.arange(NZ)[:, None]
    rows = []
    for h in (0, 1):
        rows.append(1.0 - COURANT * (np.abs(vy[h]) + np.abs(vz)) + 0.0 * z)
    for h in (0, 1):
        rows.append(COURANT * np.abs(vy[h]) + 0.0 * z)
    rows.append(COURANT * np.maximum(vz, 0.0) * (z > 0))
    rows.append(COURANT * np.maximum(-vz, 0.0) * (z < NZ - 1))
    cube = SPACING**3
    rows.append(cube * vy[0] + 0.0 * z)
    rows.append(cube * vy[1] + 0.0 * z)
    rows.append(cube * vz + 0.0 * z)
    rows.append(cube * (vy[0] ** 2 + vz**2) + 0.0 * z)
    rows.append(cube * (vy[1] ** 2 + vz**2) + 0.0 * z)
    return np.stack(rows).astype(np.float32)


def row_tables():
    lane = np.arange(LANES)
    z = (np.arange(NZ)[:, None] + lane // LOCAL_V * (NZ // 2)) % NZ
    parts = []
    for part in range(PARTS):
        point = part * LOCAL_V + lane % LOCAL_V
        vy = (2 * (point // NVZ) - (NVY - 1)) * 0.5 * SPACING
        vz = (2 * (point % NVZ) - (NVZ - 1)) * 0.5 * SPACING
        parts.append([
            1.0 - COURANT * (np.abs(vy) + np.abs(vz)) + 0.0 * z,
            COURANT * np.maximum(vy, 0.0) + 0.0 * z,
            COURANT * np.maximum(-vy, 0.0) + 0.0 * z,
            COURANT * np.maximum(vz, 0.0) * (z > 0),
            COURANT * np.maximum(-vz, 0.0) * (z < NZ - 1),
        ])
    return np.array(parts).astype(np.float32)


def fourier(real, imag, sign):
    count = len(real)
    if count == 1:
        return real, imag
    even_r, even_i = fourier(real[::2], imag[::2], sign)
    odd_r, odd_i = fourier(real[1::2], imag[1::2], sign)
    out_r, out_i = [None] * count, [None] * count
    half = count // 2
    for k in range(half):
        r, i = odd_r[k], odd_i[k]
        if k == 0:
            pass
        elif 4 * k == count:
            r, i = (-i, r) if sign > 0 else (i, -r)
        else:
            cos = math.cos(2.0 * math.pi * k / count)
            sin = sign * math.sin(2.0 * math.pi * k / count)
            if 8 * k == count or 8 * k == 3 * count:
                size = math.sqrt(0.5)
                up, across = cos / abs(cos), sin / abs(sin)
                first = r - i if up == across else r + i
                second = r + i if up == across else (i - r)
                if up > 0:
                    r, i = (first * size, second * size)
                else:
                    r, i = (first * -size, second * -size)
            else:
                r, i = r * cos - i * sin, r * sin + i * cos
        out_r[k], out_i[k] = even_r[k] + r, even_i[k] + i
        out_r[k + half], out_i[k + half] = even_r[k] - r, even_i[k] - i
    return out_r, out_i


def three_parts(values):
    top = values.astype(jnp.bfloat16)
    rest = (values - top.astype(jnp.float32)).astype(jnp.bfloat16)
    return jnp.concatenate([top, rest, top], axis=1)


def kernel(
    cells, columns,
    x_in, wall_cell_in, wall_count_in, wall_panel_in, left_in, right_in, loss_in, picks_in, mats_in, lanes_in, own_in,
    out, loads,
    x_v, wall_cell, wall_count, wall_panel, left, right, loss, picks, mats, lanes, own_rows,
    field, packed, packed_on, from_mate, arrived, arrived_on, moved, packed_back, arrived_back, state, halo_x, halo_y,
    planes, sym, spec, back, my_uses, uses, mine, others,
    in_sems, halo_send, halo_recv, swap_send, swap_recv, on_send, on_recv, give_send, give_recv, load_send, load_recv, uses_send, uses_recv,
):
    nvx = columns // PARTS
    mid = nvx // 2
    me_c = lax.axis_index("cell")
    me_v = lax.axis_index("vel")

    lines = 4 if columns % 4 == 0 else 2
    ring = columns // lines

    def owner_of(column):
        line, place = column // ring, lax.rem(column, ring)
        return line * ring + lax.rem(place + 1 - line + ring, ring)

    def column_of(device):
        line, place = device // ring, lax.rem(device, ring)
        return line * ring + lax.rem(place - 1 + line + ring, ring)

    half = columns // 2
    goes_up = me_v >= half
    next_c = me_c + jnp.where(goes_up, 1, -1)
    has_next = jnp.logical_and(next_c >= 0, next_c < cells)
    even = lax.rem(me_c, 2) == 0
    mate = me_c + jnp.where(even, 1, -1)
    gives = next_c == mate
    sends_on = jnp.logical_and(has_next, jnp.logical_not(gives))
    low_sends = jnp.logical_and(even, me_c > 0)
    high_sends = jnp.logical_and(jnp.logical_not(even), me_c < cells - 1)
    me_y = column_of(me_v)
    my_owner = owner_of(me_v)
    line, place = me_v // ring, lax.rem(me_v, ring)

    def wrapped(value, count):
        return jnp.where(value >= count, value - count, value)

    across = [lines // 2 + (m + 1) // 2 * (1 if m % 2 else -1) for m in range(lines)]
    to_lines = [wrapped(line + shift % lines, lines) for shift in across]

    def visit_line(visit, there, m):
        column = there + to_lines[m] - 1
        column = wrapped(jnp.where(column < 0, column + ring, column), ring)
        visit(to_lines[m] * ring + there, to_lines[m] * ring + column)

    def farthest_first(visit, start, stop):
        def one_round(n, carry):
            away = (n + 1) // 2
            there = wrapped(place + ring // 2 + jnp.where(lax.rem(n, 2) == 1, away, -away), ring)
            for m in range(lines):
                visit_line(visit, there, m)
            return carry

        lax.fori_loop(start, min(stop, ring - 1), one_round, 0)
        if stop == ring:
            for m in range(lines - 1):
                visit_line(visit, place, m)

    def in_place_order(visit, start, stop):
        def one_round(there, carry):
            for m in range(lines - 1):
                visit_line(visit, there, m)
            pl.when(there != place)(lambda: visit_line(visit, there, lines - 1))
            return carry

        lax.fori_loop(start, stop, one_round, 0)

    pairs = [
        (x_in, x_v), (wall_cell_in, wall_cell), (wall_count_in, wall_count), (wall_panel_in, wall_panel),
        (left_in, left), (right_in, right), (loss_in, loss), (picks_in, picks), (mats_in, mats), (lanes_in, lanes), (own_in, own_rows),
    ]
    loads_in = [pltpu.make_async_copy(src, dst, in_sems.at[n]) for n, (src, dst) in enumerate(pairs)]
    loads_in[0].start()

    barrier = pltpu.get_barrier_semaphore()

    def greet_column(to, column):
        pl.semaphore_signal(barrier, inc=1, device_id=(me_c, to), device_id_type=MESH)
        greet_sender(to)

    def greet_sender(to):
        upward = to >= half
        present = jnp.logical_or(jnp.logical_and(upward, low_sends), jnp.logical_and(to < half, high_sends))

        @pl.when(present)
        def _():
            neighbour = me_c + jnp.where(upward, -1, 1)
            pl.semaphore_signal(barrier, inc=1, device_id=(neighbour, to), device_id_type=MESH)

    def greet_row(j, carry):
        to = lax.rem(me_c + j, cells)
        pl.semaphore_signal(barrier, inc=1, device_id=(to, my_owner), device_id_type=MESH)
        return carry

    has_low_x, has_high_x = me_c > 0, me_c < cells - 1
    has_low_y, has_high_y = me_y > 0, me_y < columns - 1
    moved_home = my_owner != me_v
    greetings = [(jnp.logical_and(moved_home, has_low_x), -1), (jnp.logical_and(moved_home, has_high_x), 1)]

    farthest_first(greet_column, 0, ring // 4)
    lax.fori_loop(1, cells, greet_row, 0)
    farthest_first(greet_column, ring // 4, ring)
    greet_sender(me_v)

    @pl.when(jnp.logical_not(gives))
    def _():
        pl.semaphore_signal(barrier, inc=1, device_id=(mate, me_v), device_id_type=MESH)

    greeted = columns - 1 + cells - 1 + jnp.where(gives, 1, jnp.where(sends_on, columns, 0))
    for present, way in greetings:
        greeted = greeted + jnp.where(present, 1, 0)

        @pl.when(present)
        def _():
            pl.semaphore_signal(barrier, inc=1, device_id=(me_c + way, me_v), device_id_type=MESH)

    for copy in loads_in[1:]:
        copy.start()

    loads_in[0].wait()
    width = NZ * columns
    for start in range(0, width, LANES):
        stop = min(start + LANES, width)
        tile = x_v[:, 0, start:stop]
        back_by_half = jnp.concatenate([tile[:, NZ // 2 :], tile[:, : NZ // 2]], axis=1)
        on_by_half = jnp.concatenate([tile[:, -(NZ // 2) :], tile[:, : -(NZ // 2)]], axis=1)
        place_z = lax.rem(lax.broadcasted_iota(jnp.int32, tile.shape, 1), NZ)
        shifted = jnp.where(place_z < NZ // 2, back_by_half, on_by_half)
        turned = jnp.transpose(jnp.concatenate([tile, shifted], axis=0))
        turned = turned.reshape((stop - start) // NZ, NZ, LANES)
        field[1 + start // NZ : 1 + stop // NZ] = turned
    field[0] = jnp.zeros((NZ, LANES), jnp.float32)
    field[columns + 1] = jnp.zeros((NZ, LANES), jnp.float32)

    loads_in[10].wait()
    part = lax.rem(me_v, PARTS)
    weight_x = COURANT * 0.5 * SPACING * jnp.abs(2 * (me_v // PARTS) - (nvx - 1)).astype(jnp.float32)
    here = field[1 : columns + 1]
    stays = (
        here * (own_rows[part, 0] - weight_x)
        + field[:columns] * own_rows[part, 1]
        + field[2:] * own_rows[part, 2]
        + pltpu.roll(here, 1, 1) * own_rows[part, 3]
        + pltpu.roll(here, NZ - 1, 1) * own_rows[part, 4]
    )
    packed[...] = stays[:, : NZ // 2]
    packed_on[...] = here[:, : NZ // 2] * weight_x

    @pl.when(jnp.logical_not(low_sends))
    def _():
        arrived_on[half:] = jnp.zeros((half, NZ // 2, LANES), jnp.float32)

    @pl.when(jnp.logical_not(high_sends))
    def _():
        arrived_on[:half] = jnp.zeros((half, NZ // 2, LANES), jnp.float32)

    depth = lax.broadcasted_iota(jnp.int32, (NZ, LANES), 0)
    slot = lax.broadcasted_iota(jnp.int32, (NZ, LANES), 1)
    for copy in loads_in[1:4]:
        copy.wait()
    counted = jnp.zeros((NZ, LANES), jnp.float32)
    per_owner = PANEL_DEV * columns
    for n in range(WALL_SLOTS):
        panel = wall_panel[0, 0, n]
        target = panel // per_owner * PANEL_DEV + lax.rem(panel, PANEL_DEV)
        target = jnp.where(n < wall_count[0, 0], target, -1)
        hit = jnp.logical_and(depth == wall_cell[0, 0, n], slot == target)
        counted = counted + jnp.where(hit, 1.0, 0.0)
    my_uses[...] = counted

    @pl.when(jnp.logical_not(moved_home))
    def _():
        uses[...] = counted

    pl.semaphore_wait(barrier, greeted)

    def send_block(source, target, which, to, source_slot, target_slot):
        pltpu.make_async_remote_copy(
            src_ref=source.at[source_slot],
            dst_ref=target.at[target_slot],
            send_sem=swap_send.at[which],
            recv_sem=swap_recv.at[which],
            device_id=(me_c, to),
            device_id_type=MESH,
        ).start()

    def arrivals(target, which):
        rest = target.at[pl.ds(0, columns - 1)]
        pltpu.make_async_copy(rest, rest, swap_recv.at[which]).wait()

    def departures(source, which):
        rest = source.at[pl.ds(0, columns - 1)]
        pltpu.make_async_copy(rest, rest, swap_send.at[which]).wait()

    on_way = jnp.where(goes_up, 0, 1)

    def send_on(to, column):
        pltpu.make_async_remote_copy(
            src_ref=packed_on.at[column],
            dst_ref=arrived_on.at[me_v],
            send_sem=on_send,
            recv_sem=on_recv.at[on_way],
            device_id=(next_c, to),
            device_id_type=MESH,
        ).start()

    def send_one(to, column):
        send_block(packed, arrived, 0, to, column, me_v)

    give_copy = pltpu.make_async_remote_copy(
        src_ref=packed_on,
        dst_ref=from_mate,
        send_sem=give_send,
        recv_sem=give_recv,
        device_id=(mate, me_v),
        device_id_type=MESH,
    )
    pl.when(gives)(give_copy.start)

    @pl.when(jnp.logical_not(gives))
    def _():
        pl.when(sends_on)(lambda: farthest_first(send_on, 0, ring // 4))
        give_copy.wait_recv()
        packed[...] = packed[...] + from_mate[...]

    farthest_first(send_one, 0, ring)
    arrived[pl.ds(me_v, 1)] = packed[pl.ds(me_y, 1)]

    @pl.when(sends_on)
    def _():
        farthest_first(send_on, ring // 4, ring)
        send_on(me_v, me_y)

    uses_copy = pltpu.make_async_remote_copy(
        src_ref=my_uses,
        dst_ref=uses,
        send_sem=uses_send,
        recv_sem=uses_recv,
        device_id=(me_c, my_owner),
        device_id_type=MESH,
    )
    pl.when(moved_home)(uses_copy.start)

    @pl.when(jnp.logical_not(has_low_x))
    def _():
        halo_x[:, :, mid:] = jnp.zeros((STEPS - 1, 2, mid, NZ, LANES), jnp.float32)

    @pl.when(jnp.logical_not(has_high_x))
    def _():
        halo_x[:, :, :mid] = jnp.zeros((STEPS - 1, 2, mid, NZ, LANES), jnp.float32)

    @pl.when(jnp.logical_not(has_low_y))
    def _():
        halo_y[:, 1] = jnp.zeros((STEPS - 1, nvx, NZ, LANES), jnp.float32)

    @pl.when(jnp.logical_not(has_high_y))
    def _():
        halo_y[:, 0] = jnp.zeros((STEPS - 1, nvx, NZ, LANES), jnp.float32)

    for copy in loads_in[4:10]:
        copy.wait()
    for pair in range(nvx // 2):
        span = slice(pair * 2 * PLANE, (pair + 1) * 2 * PLANE)
        planes[pair, :DIRS] = left[:, span]
        planes[pair, DIRS : 2 * DIRS] = right[:, span]
        planes[pair, 2 * DIRS : KERNELS] = loss[:, span]
        planes[pair, KERNELS:] = jnp.zeros((NZ - KERNELS, 2 * PLANE), jnp.float32)
    remaining = planes[...].reshape(nvx // 2 * NZ, 2 * PLANE)
    chosen = 0.0
    for _ in range(3):
        top = remaining.astype(jnp.bfloat16)
        chosen = chosen + jnp.dot(top, picks[...], preferred_element_type=jnp.float32)
        remaining = remaining - top.astype(jnp.float32)
    chosen = (chosen * (1.0 / (nvx * PLANE))).reshape(nvx // 2, NZ, 4 * LANES)
    for a in range(nvx):
        b = -a % nvx
        near, far = a % 2 * LANES, (2 + b % 2) * LANES
        sym[a] = chosen[a // 2, :, near : near + LANES] + chosen[b // 2, :, far : far + LANES]

    arrivals(arrived, 0)
    from_low, from_high = arrived_on.at[pl.ds(half, half)], arrived_on.at[pl.ds(0, half)]
    pl.when(low_sends)(pltpu.make_async_copy(from_low, from_low, on_recv.at[0]).wait)
    pl.when(high_sends)(pltpu.make_async_copy(from_high, from_high, on_recv.at[1]).wait)

    lane = lax.broadcasted_iota(jnp.int32, (1, 1, LANES), 2)
    used = lane < HALF
    quarter = LOCAL_V // 2

    def turn(values, by):
        return pltpu.roll(values, by, values.ndim - 1)

    blocks = (arrived[...] + arrived_on[...]).reshape(nvx, PARTS, NZ // 2, LANES)
    wide = []
    for part in range(PARTS):
        block = blocks[:, part]
        wide.append(jnp.concatenate([block, turn(block, LOCAL_V)], axis=1))
    moved[0] = jnp.where(lane < LOCAL_V, wide[0], jnp.where(used, turn(wide[1], LOCAL_V), 0.0))
    moved[1] = jnp.where(
        lane < quarter, turn(wide[1], LANES - quarter), jnp.where(used, turn(wide[2], quarter), 0.0)
    )

    def halo_copies(step):
        routes = [
            (state.at[step, 1], halo_y.at[step, 1], (me_c, owner_of(me_y + 1))),
            (state.at[step, 0], halo_y.at[step, 0], (me_c, owner_of(me_y - 1))),
            (state.at[step, :, pl.ds(mid, mid)], halo_x.at[step, :, pl.ds(mid, mid)], (me_c + 1, me_v)),
            (state.at[step, :, pl.ds(0, mid)], halo_x.at[step, :, pl.ds(0, mid)], (me_c - 1, me_v)),
        ]
        return [
            pltpu.make_async_remote_copy(
                src_ref=src,
                dst_ref=dst,
                send_sem=halo_send.at[n, step],
                recv_sem=halo_recv.at[n, step],
                device_id=to,
                device_id_type=MESH,
            )
            for n, (src, dst, to) in enumerate(routes)
        ]

    sends = [has_high_y, has_low_y, has_high_x, has_low_x]
    receives = [has_low_y, has_high_y, has_low_x, has_high_x]

    def speed_x(a):
        return (2 * a - (nvx - 1)) * 0.5 * SPACING

    def transport(step):
        copies = halo_copies(step)
        for copy, present in zip(copies, sends):
            pl.when(present)(copy.start)

        own = []
        for h in (0, 1):
            here = state[step, h]
            own.append(
                here * lanes[h]
                + pltpu.roll(here, 1, 1) * lanes[4]
                + pltpu.roll(here, NZ - 1, 1) * lanes[5]
            )

        for copy, present in zip(copies, receives):
            pl.when(present)(copy.wait_recv)

        for h in (0, 1):
            side = []
            for a in range(nvx):
                weight = COURANT * abs(speed_x(a))
                side.append(own[h][a] + (halo_x[step, h, a] - state[step, h, a]) * weight)
            moved[h] = jnp.stack(side) + halo_y[step, h] * lanes[2 + h]

    def advance(step, carry):
        rows = jnp.concatenate([moved[h].reshape(nvx * NZ, LANES) for h in (0, 1)], axis=1)

        span = 2 * LANES
        plane = jnp.dot(three_parts(rows), mats[: 3 * span], preferred_element_type=jnp.float32)
        plane = plane.reshape(nvx, NZ, span)
        real, imag = fourier(
            [plane[a, :, :LANES] for a in range(nvx)], [plane[a, :, LANES:] for a in range(nvx)], -1
        )
        spec[0] = jnp.stack(real)
        spec[1] = jnp.stack(imag)

        def weigh(w, carry):
            gains = [sym[a, pl.ds(w, 1), :] for a in range(nvx)]
            real, imag = fourier(
                [spec[0, a] * gains[a] for a in range(nvx)], [spec[1, a] * gains[a] for a in range(nvx)], 1
            )
            line = jnp.concatenate(
                [jnp.concatenate(real, axis=0), jnp.concatenate(imag, axis=0)], axis=1
            )
            tall = nvx * NZ
            back[pl.ds(pl.multiple_of(w * tall, tall), tall)] = three_parts(line)
            return carry

        lax.fori_loop(0, KERNELS, weigh, 0, unroll=True)
        found = jnp.dot(back[...], mats[3 * span :], preferred_element_type=jnp.float32)
        found = found.reshape(KERNELS, nvx * NZ, span)
        change = found[0] * found[2] + found[1] * found[3] - rows * found[4]
        after = rows + COLLISION_STEP * change
        for h in (0, 1):
            state[step, h] = after[:, h * LANES : (h + 1) * LANES].reshape(nvx, NZ, LANES)
        pl.when(step < STEPS - 1)(lambda: transport(step))
        return carry

    lax.fori_loop(0, STEPS, advance, 0)

    low, high = state[STEPS - 1, 0], state[STEPS - 1, 1]
    parts = [
        low,
        jnp.where(lane < quarter, turn(low, LOCAL_V), turn(high, quarter)),
        turn(high, LANES - quarter),
    ]
    stacked = [
        jnp.where(lane < LOCAL_V, part[:, : NZ // 2], turn(part, LOCAL_V)[:, NZ // 2 :]) for part in parts
    ]
    packed_back[...] = jnp.stack(stacked, axis=1).reshape(columns, NZ // 2, LANES)
    def send_home(to, column):
        send_block(packed_back, arrived_back, 1, to, to, me_y)

    in_place_order(send_home, 0, ring // 4)

    both = low + high
    sums_low, sums_high = jnp.sum(low, axis=0), jnp.sum(high, axis=0)
    along, squared = 0.0, 0.0
    for a in range(nvx):
        along = along + both[a] * (SPACING**3 * speed_x(a))
        squared = squared + both[a] * (SPACING**3 * speed_x(a) ** 2)
    totals = [
        along,
        sums_low * lanes[6] + sums_high * lanes[7],
        (sums_low + sums_high) * lanes[8],
        squared + sums_low * lanes[9] + sums_high * lanes[10],
    ]
    pl.when(moved_home)(uses_copy.wait_recv)
    counted = uses[...]
    shares = [
        jnp.sum(jnp.sum(total, axis=1, keepdims=True) * counted, axis=0, keepdims=True) for total in totals
    ]
    shares.append(jnp.zeros((NZ - MOMENTS, LANES), jnp.float32))
    share = jnp.concatenate(shares, axis=0)
    mine[...] = share
    all_others, rest = others.at[pl.ds(0, cells)], others.at[pl.ds(0, cells - 1)]

    def give(j, carry):
        to = lax.rem(me_c + j, cells)
        pltpu.make_async_remote_copy(
            src_ref=mine,
            dst_ref=others.at[me_c],
            send_sem=load_send,
            recv_sem=load_recv,
            device_id=(to, me_y),
            device_id_type=MESH,
        ).start()
        return carry

    lax.fori_loop(1, cells, give, 0)
    pl.when(moved_home)(lambda: give(0, None))

    in_place_order(send_home, ring // 4, ring)
    arrived_back[pl.ds(me_y, 1)] = packed_back[pl.ds(me_v, 1)]

    @pl.when(moved_home)
    def _():
        pltpu.make_async_copy(all_others, all_others, load_recv).wait()

    @pl.when(jnp.logical_not(moved_home))
    def _():
        others[pl.ds(me_c, 1)] = share[None]
        pltpu.make_async_copy(rest, rest, load_recv).wait()

    summed = jnp.sum(others[...], axis=0)
    picked = slot - PANEL_DEV * me_c
    columns_out = [
        jnp.sum(jnp.where(picked == k, summed, 0.0), axis=1, keepdims=True) for k in range(PANEL_DEV)
    ]
    loads[...] = jnp.concatenate(columns_out, axis=1)[:MOMENTS]

    arrivals(arrived_back, 1)
    for start in range(0, columns, LANES // NZ):
        stop = min(start + LANES // NZ, columns)
        block = arrived_back[start:stop]
        tall = jnp.concatenate([block, turn(block, LOCAL_V)], axis=1).reshape((stop - start) * NZ, LANES)
        out[:, 0, start * NZ : stop * NZ] = jnp.transpose(tall)[:LOCAL_V]

    departures(packed, 0)
    pl.when(sends_on)(pltpu.make_async_copy(packed_on, packed_on, on_send).wait)
    pl.when(gives)(give_copy.wait_send)
    departures(packed_back, 1)
    pl.when(moved_home)(uses_copy.wait_send)
    pl.when(moved_home)(pltpu.make_async_copy(all_others, all_others, load_send).wait)
    pl.when(jnp.logical_not(moved_home))(pltpu.make_async_copy(rest, rest, load_send).wait)

    def finish(step, carry):
        for copy, present in zip(halo_copies(step), sends):
            pl.when(present)(copy.wait_send)
        return carry

    lax.fori_loop(0, STEPS - 1, finish, 0)


def per_device(cells, columns, distribution, gain_left, gain_right, loss_kernel, wall_cell, wall_count, wall_panel):
    nvx = columns // PARTS
    local, _, width = distribution.shape
    f32 = jnp.float32
    loss = loss_kernel.reshape(1, -1)
    picks = jnp.asarray(weight_selectors())
    mats = jnp.asarray(plane_matrices())
    tables = jnp.asarray(lane_tables())
    rows = jnp.asarray(row_tables())
    anywhere = pl.BlockSpec(memory_space=pl.ANY)
    in_vmem = pl.BlockSpec(memory_space=pltpu.VMEM)
    dma = pltpu.SemaphoreType.DMA
    out, loads = pl.pallas_call(
        functools.partial(kernel, cells, columns),
        out_shape=(
            pltpu.VMEM((local, 1, width), f32),
            pltpu.VMEM((MOMENTS, PANEL_DEV), f32),
        ),
        in_specs=[anywhere] * 11,
        out_specs=(in_vmem, in_vmem),
        scratch_shapes=[
            pltpu.VMEM(distribution.shape, f32),
            pltpu.SMEM(wall_cell.shape, jnp.int32),
            pltpu.SMEM(wall_count.shape, jnp.int32),
            pltpu.SMEM(wall_panel.shape, jnp.int32),
            pltpu.VMEM(gain_left.shape, f32),
            pltpu.VMEM(gain_right.shape, f32),
            pltpu.VMEM(loss.shape, f32),
            pltpu.VMEM(picks.shape, jnp.bfloat16),
            pltpu.VMEM(mats.shape, jnp.bfloat16),
            pltpu.VMEM(tables.shape, f32),
            pltpu.VMEM(rows.shape, f32),
            pltpu.VMEM((columns + 2, NZ, LANES), f32),
            pltpu.VMEM((columns, NZ // 2, LANES), f32),
            pltpu.VMEM((columns, NZ // 2, LANES), f32),
            pltpu.VMEM((columns, NZ // 2, LANES), f32),
            pltpu.VMEM((columns, NZ // 2, LANES), f32),
            pltpu.VMEM((columns, NZ // 2, LANES), f32),
            pltpu.VMEM((2, nvx, NZ, LANES), f32),
            pltpu.VMEM((columns, NZ // 2, LANES), f32),
            pltpu.VMEM((columns, NZ // 2, LANES), f32),
            pltpu.VMEM((STEPS, 2, nvx, NZ, LANES), f32),
            pltpu.VMEM((STEPS - 1, 2, nvx, NZ, LANES), f32),
            pltpu.VMEM((STEPS - 1, 2, nvx, NZ, LANES), f32),
            pltpu.VMEM((nvx // 2, NZ, 2 * PLANE), f32),
            pltpu.VMEM((nvx, NZ, LANES), f32),
            pltpu.VMEM((2, nvx, NZ, LANES), f32),
            pltpu.VMEM((KERNELS * nvx * NZ, 6 * LANES), jnp.bfloat16),
            pltpu.VMEM((NZ, LANES), f32),
            pltpu.VMEM((NZ, LANES), f32),
            pltpu.VMEM((NZ, LANES), f32),
            pltpu.VMEM((cells, NZ, LANES), f32),
            dma((11,)),
            dma((4, STEPS - 1)),
            dma((4, STEPS - 1)),
            dma((2,)),
            dma((2,)),
            dma,
            dma((2,)),
            dma,
            dma,
            dma,
            dma,
            dma,
            dma,
        ],
        compiler_params=pltpu.CompilerParams(
            collective_id=0, has_side_effects=True, vmem_limit_bytes=VMEM_LIMIT
        ),
        cost_estimate=pl.CostEstimate(flops=1_000_000_000, bytes_accessed=2_000_000, transcendentals=0),
        name="collide",
    )(distribution, wall_cell, wall_count, wall_panel, gain_left, gain_right, loss, picks, mats, tables, rows)
    return out, loads


def solution(mesh):
    placed = (
        P("vel", "cell", None),
        P(),
        P(),
        P(),
        P("cell", "vel", None),
        P("cell", "vel"),
        P("cell", "vel", None),
    )
    return jax.shard_map(
        functools.partial(per_device, mesh.shape["cell"], mesh.shape["vel"]),
        mesh=mesh,
        in_specs=placed,
        out_specs=(P("vel", "cell", None), P(None, ("cell", "vel"))),
        check_vma=False,
    )
```

```python
import functools
import math

import jax
import jax.numpy as jnp
import ml_dtypes
import numpy as np
from jax import lax
from jax.experimental import pallas as pl
from jax.experimental.pallas import tpu as pltpu
from jax.sharding import PartitionSpec as P

NVY = 16
NVZ = 12
PLANE = NVY * NVZ
HALF = PLANE // 2
KEPT = NVZ // 2 + 1
KERNELS = 5
DIRS = 2
MOMENTS = 4
STEPS = 3
NZ = 8
WALL_SLOTS = 8
PANEL_DEV = 4
LOCAL_V = 64
PARTS = PLANE // LOCAL_V
LANES = 128
VMEM_LIMIT = 60 * 1024 * 1024

SPACING = 0.5
COURANT = 0.09
COLLISION_STEP = 0.3

MESH = pl.DeviceIdType.MESH


def split(values):
    high = values.astype(ml_dtypes.bfloat16)
    low = (values - high.astype(np.float64)).astype(ml_dtypes.bfloat16)
    return high, low


def plane_matrices():
    table = np.zeros((2 * LANES, 2 * LANES))
    for point in range(PLANE):
        b, c = divmod(point, NVZ)
        row = b // (NVY // 2) * LANES + point % HALF
        for kb in range(NVY):
            for kc in range(KEPT):
                angle = 2.0 * math.pi * ((b * kb % NVY) / NVY + (c * kc % NVZ) / NVZ)
                table[row, kb * KEPT + kc] = math.cos(angle)
                table[row, LANES + kb * KEPT + kc] = -math.sin(angle)
    high, low = split(table)
    return np.concatenate([high, high, low, high.T, high.T, low.T], axis=0)


def weight_selectors():
    table = np.zeros((2 * PLANE, 4 * LANES))
    for kb in range(NVY):
        for kc in range(KEPT):
            share = 0.5 if kc in (0, KEPT - 1) else 1.0
            column = kb * KEPT + kc
            there = kb * NVZ + kc
            mirror = -kb % NVY * NVZ + -kc % NVZ
            for half in (0, 1):
                table[half * PLANE + there, half * LANES + column] = share
                table[half * PLANE + mirror, (2 + half) * LANES + column] = share
    return table.astype(ml_dtypes.bfloat16)


def lane_tables():
    lane = np.arange(LANES)
    used = (lane < HALF).astype(np.float64)
    vz = (2 * (lane % NVZ) - (NVZ - 1)) * 0.5 * SPACING * used
    vy = [(2 * (lane // NVZ + h * NVY // 2) - (NVY - 1)) * 0.5 * SPACING * used for h in (0, 1)]
    z = np.arange(NZ)[:, None]
    rows = []
    for h in (0, 1):
        rows.append(1.0 - COURANT * (np.abs(vy[h]) + np.abs(vz)) + 0.0 * z)
    for h in (0, 1):
        rows.append(COURANT * np.abs(vy[h]) + 0.0 * z)
    rows.append(COURANT * np.maximum(vz, 0.0) * (z > 0))
    rows.append(COURANT * np.maximum(-vz, 0.0) * (z < NZ - 1))
    cube = SPACING**3
    rows.append(cube * vy[0] + 0.0 * z)
    rows.append(cube * vy[1] + 0.0 * z)
    rows.append(cube * vz + 0.0 * z)
    rows.append(cube * (vy[0] ** 2 + vz**2) + 0.0 * z)
    rows.append(cube * (vy[1] ** 2 + vz**2) + 0.0 * z)
    return np.stack(rows).astype(np.float32)


def row_tables():
    lane = np.arange(LANES)
    z = (np.arange(NZ)[:, None] + lane // LOCAL_V * (NZ // 2)) % NZ
    parts = []
    for part in range(PARTS):
        point = part * LOCAL_V + lane % LOCAL_V
        vy = (2 * (point // NVZ) - (NVY - 1)) * 0.5 * SPACING
        vz = (2 * (point % NVZ) - (NVZ - 1)) * 0.5 * SPACING
        parts.append([
            1.0 - COURANT * (np.abs(vy) + np.abs(vz)) + 0.0 * z,
            COURANT * np.maximum(vy, 0.0) + 0.0 * z,
            COURANT * np.maximum(-vy, 0.0) + 0.0 * z,
            COURANT * np.maximum(vz, 0.0) * (z > 0),
            COURANT * np.maximum(-vz, 0.0) * (z < NZ - 1),
        ])
    return np.array(parts).astype(np.float32)


def fourier(real, imag, sign):
    count = len(real)
    if count == 1:
        return real, imag
    even_r, even_i = fourier(real[::2], imag[::2], sign)
    odd_r, odd_i = fourier(real[1::2], imag[1::2], sign)
    out_r, out_i = [None] * count, [None] * count
    half = count // 2
    for k in range(half):
        r, i = odd_r[k], odd_i[k]
        if k == 0:
            pass
        elif 4 * k == count:
            r, i = (-i, r) if sign > 0 else (i, -r)
        else:
            cos = math.cos(2.0 * math.pi * k / count)
            sin = sign * math.sin(2.0 * math.pi * k / count)
            if 8 * k == count or 8 * k == 3 * count:
                size = math.sqrt(0.5)
                up, across = cos / abs(cos), sin / abs(sin)
                first = r - i if up == across else r + i
                second = r + i if up == across else (i - r)
                if up > 0:
                    r, i = (first * size, second * size)
                else:
                    r, i = (first * -size, second * -size)
            else:
                r, i = r * cos - i * sin, r * sin + i * cos
        out_r[k], out_i[k] = even_r[k] + r, even_i[k] + i
        out_r[k + half], out_i[k + half] = even_r[k] - r, even_i[k] - i
    return out_r, out_i


def three_parts(values):
    top = values.astype(jnp.bfloat16)
    rest = (values - top.astype(jnp.float32)).astype(jnp.bfloat16)
    return jnp.concatenate([top, rest, top], axis=1)


def kernel(
    cells, columns,
    x_in, wall_cell_in, wall_count_in, wall_panel_in, left_in, right_in, loss_in, picks_in, mats_in, lanes_in, own_in,
    out, loads,
    x_v, wall_cell, wall_count, wall_panel, left, right, loss, picks, mats, lanes, own_rows,
    field, packed, packed_on, from_mate, arrived, arrived_on, moved, packed_back, arrived_back, state, halo_x, halo_y,
    planes, sym, spec, back, my_uses, uses, mine, others,
    in_sems, halo_send, halo_recv, swap_send, swap_recv, on_send, on_recv, give_send, give_recv, load_send, load_recv, uses_send, uses_recv,
):
    nvx = columns // PARTS
    mid = nvx // 2
    me_c = lax.axis_index("cell")
    me_v = lax.axis_index("vel")

    lines = 4 if columns % 4 == 0 else 2
    ring = columns // lines
    lead = lines - 1

    def owner_of(column):
        line, place = column // ring, lax.rem(column, ring)
        return line * ring + lax.rem(place + lead - line + ring, ring)

    def column_of(device):
        line, place = device // ring, lax.rem(device, ring)
        return line * ring + lax.rem(place - lead + line + ring, ring)

    half = columns // 2
    goes_up = me_v >= half
    next_c = me_c + jnp.where(goes_up, 1, -1)
    has_next = jnp.logical_and(next_c >= 0, next_c < cells)
    even = lax.rem(me_c, 2) == 0
    mate = me_c + jnp.where(even, 1, -1)
    gives = next_c == mate
    sends_on = jnp.logical_and(has_next, jnp.logical_not(gives))
    low_sends = jnp.logical_and(even, me_c > 0)
    high_sends = jnp.logical_and(jnp.logical_not(even), me_c < cells - 1)
    me_y = column_of(me_v)
    my_owner = owner_of(me_v)
    line, place = me_v // ring, lax.rem(me_v, ring)

    def wrapped(value, count):
        return jnp.where(value >= count, value - count, value)

    across = [lines // 2 + (m + 1) // 2 * (1 if m % 2 else -1) for m in range(lines)]
    to_lines = [wrapped(line + shift % lines, lines) for shift in across]

    def visit_line(visit, there, m):
        column = there + to_lines[m] - lead
        column = wrapped(jnp.where(column < 0, column + ring, column), ring)
        visit(to_lines[m] * ring + there, to_lines[m] * ring + column)

    def farthest_first(visit, start, stop):
        def one_round(n, carry):
            away = (n + 1) // 2
            there = wrapped(place + ring // 2 + jnp.where(lax.rem(n, 2) == 1, away, -away), ring)
            for m in range(lines):
                visit_line(visit, there, m)
            return carry

        lax.fori_loop(start, min(stop, ring - 1), one_round, 0)
        if stop == ring:
            for m in range(lines - 1):
                visit_line(visit, place, m)

    def in_place_order(visit, start, stop):
        def one_round(there, carry):
            for m in range(lines - 1):
                visit_line(visit, there, m)
            pl.when(there != place)(lambda: visit_line(visit, there, lines - 1))
            return carry

        lax.fori_loop(start, stop, one_round, 0)

    pairs = [
        (x_in, x_v), (wall_cell_in, wall_cell), (wall_count_in, wall_count), (wall_panel_in, wall_panel),
        (left_in, left), (right_in, right), (loss_in, loss), (picks_in, picks), (mats_in, mats), (lanes_in, lanes), (own_in, own_rows),
    ]
    loads_in = [pltpu.make_async_copy(src, dst, in_sems.at[n]) for n, (src, dst) in enumerate(pairs)]
    loads_in[0].start()

    barrier = pltpu.get_barrier_semaphore()

    def greet_column(to, column):
        pl.semaphore_signal(barrier, inc=1, device_id=(me_c, to), device_id_type=MESH)
        greet_sender(to)

    def greet_sender(to):
        upward = to >= half
        present = jnp.logical_or(jnp.logical_and(upward, low_sends), jnp.logical_and(to < half, high_sends))

        @pl.when(present)
        def _():
            neighbour = me_c + jnp.where(upward, -1, 1)
            pl.semaphore_signal(barrier, inc=1, device_id=(neighbour, to), device_id_type=MESH)

    def greet_row(j, carry):
        to = lax.rem(me_c + j, cells)
        pl.semaphore_signal(barrier, inc=1, device_id=(to, my_owner), device_id_type=MESH)
        return carry

    has_low_x, has_high_x = me_c > 0, me_c < cells - 1
    has_low_y, has_high_y = me_y > 0, me_y < columns - 1
    moved_home = my_owner != me_v
    greetings = [(jnp.logical_and(moved_home, has_low_x), -1), (jnp.logical_and(moved_home, has_high_x), 1)]

    farthest_first(greet_column, 0, ring // 4)
    lax.fori_loop(1, cells, greet_row, 0)
    farthest_first(greet_column, ring // 4, ring)
    greet_sender(me_v)

    @pl.when(jnp.logical_not(gives))
    def _():
        pl.semaphore_signal(barrier, inc=1, device_id=(mate, me_v), device_id_type=MESH)

    greeted = columns - 1 + cells - 1 + jnp.where(gives, 1, jnp.where(sends_on, columns, 0))
    for present, way in greetings:
        greeted = greeted + jnp.where(present, 1, 0)

        @pl.when(present)
        def _():
            pl.semaphore_signal(barrier, inc=1, device_id=(me_c + way, me_v), device_id_type=MESH)

    for copy in loads_in[1:]:
        copy.start()

    loads_in[0].wait()
    width = NZ * columns
    for start in range(0, width, LANES):
        stop = min(start + LANES, width)
        tile = x_v[:, 0, start:stop]
        back_by_half = jnp.concatenate([tile[:, NZ // 2 :], tile[:, : NZ // 2]], axis=1)
        on_by_half = jnp.concatenate([tile[:, -(NZ // 2) :], tile[:, : -(NZ // 2)]], axis=1)
        place_z = lax.rem(lax.broadcasted_iota(jnp.int32, tile.shape, 1), NZ)
        shifted = jnp.where(place_z < NZ // 2, back_by_half, on_by_half)
        turned = jnp.transpose(jnp.concatenate([tile, shifted], axis=0))
        turned = turned.reshape((stop - start) // NZ, NZ, LANES)
        field[1 + start // NZ : 1 + stop // NZ] = turned
    field[0] = jnp.zeros((NZ, LANES), jnp.float32)
    field[columns + 1] = jnp.zeros((NZ, LANES), jnp.float32)

    loads_in[10].wait()
    part = lax.rem(me_v, PARTS)
    weight_x = COURANT * 0.5 * SPACING * jnp.abs(2 * (me_v // PARTS) - (nvx - 1)).astype(jnp.float32)
    here = field[1 : columns + 1]
    stays = (
        here * (own_rows[part, 0] - weight_x)
        + field[:columns] * own_rows[part, 1]
        + field[2:] * own_rows[part, 2]
        + pltpu.roll(here, 1, 1) * own_rows[part, 3]
        + pltpu.roll(here, NZ - 1, 1) * own_rows[part, 4]
    )
    packed[...] = stays[:, : NZ // 2]
    packed_on[...] = here[:, : NZ // 2] * weight_x

    @pl.when(jnp.logical_not(low_sends))
    def _():
        arrived_on[half:] = jnp.zeros((half, NZ // 2, LANES), jnp.float32)

    @pl.when(jnp.logical_not(high_sends))
    def _():
        arrived_on[:half] = jnp.zeros((half, NZ // 2, LANES), jnp.float32)

    depth = lax.broadcasted_iota(jnp.int32, (NZ, LANES), 0)
    slot = lax.broadcasted_iota(jnp.int32, (NZ, LANES), 1)
    for copy in loads_in[1:4]:
        copy.wait()
    counted = jnp.zeros((NZ, LANES), jnp.float32)
    per_owner = PANEL_DEV * columns
    for n in range(WALL_SLOTS):
        panel = wall_panel[0, 0, n]
        target = panel // per_owner * PANEL_DEV + lax.rem(panel, PANEL_DEV)
        target = jnp.where(n < wall_count[0, 0], target, -1)
        hit = jnp.logical_and(depth == wall_cell[0, 0, n], slot == target)
        counted = counted + jnp.where(hit, 1.0, 0.0)
    my_uses[...] = counted

    @pl.when(jnp.logical_not(moved_home))
    def _():
        uses[...] = counted

    pl.semaphore_wait(barrier, greeted)

    def send_block(source, target, which, to, source_slot, target_slot):
        pltpu.make_async_remote_copy(
            src_ref=source.at[source_slot],
            dst_ref=target.at[target_slot],
            send_sem=swap_send.at[which],
            recv_sem=swap_recv.at[which],
            device_id=(me_c, to),
            device_id_type=MESH,
        ).start()

    def arrivals(target, which):
        rest = target.at[pl.ds(0, columns - 1)]
        pltpu.make_async_copy(rest, rest, swap_recv.at[which]).wait()

    def departures(source, which):
        rest = source.at[pl.ds(0, columns - 1)]
        pltpu.make_async_copy(rest, rest, swap_send.at[which]).wait()

    on_way = jnp.where(goes_up, 0, 1)

    def send_on(to, column):
        pltpu.make_async_remote_copy(
            src_ref=packed_on.at[column],
            dst_ref=arrived_on.at[me_v],
            send_sem=on_send,
            recv_sem=on_recv.at[on_way],
            device_id=(next_c, to),
            device_id_type=MESH,
        ).start()

    def send_one(to, column):
        send_block(packed, arrived, 0, to, column, me_v)

    give_copy = pltpu.make_async_remote_copy(
        src_ref=packed_on,
        dst_ref=from_mate,
        send_sem=give_send,
        recv_sem=give_recv,
        device_id=(mate, me_v),
        device_id_type=MESH,
    )
    pl.when(gives)(give_copy.start)

    @pl.when(jnp.logical_not(gives))
    def _():
        pl.when(sends_on)(lambda: farthest_first(send_on, 0, ring // 4))
        give_copy.wait_recv()
        packed[...] = packed[...] + from_mate[...]

    farthest_first(send_one, 0, ring)
    arrived[pl.ds(me_v, 1)] = packed[pl.ds(me_y, 1)]

    @pl.when(sends_on)
    def _():
        farthest_first(send_on, ring // 4, ring)
        send_on(me_v, me_y)

    uses_copy = pltpu.make_async_remote_copy(
        src_ref=my_uses,
        dst_ref=uses,
        send_sem=uses_send,
        recv_sem=uses_recv,
        device_id=(me_c, my_owner),
        device_id_type=MESH,
    )
    pl.when(moved_home)(uses_copy.start)

    @pl.when(jnp.logical_not(has_low_x))
    def _():
        halo_x[:, :, mid:] = jnp.zeros((STEPS - 1, 2, mid, NZ, LANES), jnp.float32)

    @pl.when(jnp.logical_not(has_high_x))
    def _():
        halo_x[:, :, :mid] = jnp.zeros((STEPS - 1, 2, mid, NZ, LANES), jnp.float32)

    @pl.when(jnp.logical_not(has_low_y))
    def _():
        halo_y[:, 1] = jnp.zeros((STEPS - 1, nvx, NZ, LANES), jnp.float32)

    @pl.when(jnp.logical_not(has_high_y))
    def _():
        halo_y[:, 0] = jnp.zeros((STEPS - 1, nvx, NZ, LANES), jnp.float32)

    for copy in loads_in[4:10]:
        copy.wait()
    for pair in range(nvx // 2):
        span = slice(pair * 2 * PLANE, (pair + 1) * 2 * PLANE)
        planes[pair, :DIRS] = left[:, span]
        planes[pair, DIRS : 2 * DIRS] = right[:, span]
        planes[pair, 2 * DIRS : KERNELS] = loss[:, span]
        planes[pair, KERNELS:] = jnp.zeros((NZ - KERNELS, 2 * PLANE), jnp.float32)
    remaining = planes[...].reshape(nvx // 2 * NZ, 2 * PLANE)
    chosen = 0.0
    for _ in range(3):
        top = remaining.astype(jnp.bfloat16)
        chosen = chosen + jnp.dot(top, picks[...], preferred_element_type=jnp.float32)
        remaining = remaining - top.astype(jnp.float32)
    chosen = (chosen * (1.0 / (nvx * PLANE))).reshape(nvx // 2, NZ, 4 * LANES)
    for a in range(nvx):
        b = -a % nvx
        near, far = a % 2 * LANES, (2 + b % 2) * LANES
        sym[a] = chosen[a // 2, :, near : near + LANES] + chosen[b // 2, :, far : far + LANES]

    arrivals(arrived, 0)
    from_low, from_high = arrived_on.at[pl.ds(half, half)], arrived_on.at[pl.ds(0, half)]
    pl.when(low_sends)(pltpu.make_async_copy(from_low, from_low, on_recv.at[0]).wait)
    pl.when(high_sends)(pltpu.make_async_copy(from_high, from_high, on_recv.at[1]).wait)

    lane = lax.broadcasted_iota(jnp.int32, (1, 1, LANES), 2)
    used = lane < HALF
    quarter = LOCAL_V // 2

    def turn(values, by):
        return pltpu.roll(values, by, values.ndim - 1)

    blocks = (arrived[...] + arrived_on[...]).reshape(nvx, PARTS, NZ // 2, LANES)
    wide = []
    for part in range(PARTS):
        block = blocks[:, part]
        wide.append(jnp.concatenate([block, turn(block, LOCAL_V)], axis=1))
    moved[0] = jnp.where(lane < LOCAL_V, wide[0], jnp.where(used, turn(wide[1], LOCAL_V), 0.0))
    moved[1] = jnp.where(
        lane < quarter, turn(wide[1], LANES - quarter), jnp.where(used, turn(wide[2], quarter), 0.0)
    )

    def halo_copies(step):
        routes = [
            (state.at[step, 1], halo_y.at[step, 1], (me_c, owner_of(me_y + 1))),
            (state.at[step, 0], halo_y.at[step, 0], (me_c, owner_of(me_y - 1))),
            (state.at[step, :, pl.ds(mid, mid)], halo_x.at[step, :, pl.ds(mid, mid)], (me_c + 1, me_v)),
            (state.at[step, :, pl.ds(0, mid)], halo_x.at[step, :, pl.ds(0, mid)], (me_c - 1, me_v)),
        ]
        return [
            pltpu.make_async_remote_copy(
                src_ref=src,
                dst_ref=dst,
                send_sem=halo_send.at[n, step],
                recv_sem=halo_recv.at[n, step],
                device_id=to,
                device_id_type=MESH,
            )
            for n, (src, dst, to) in enumerate(routes)
        ]

    sends = [has_high_y, has_low_y, has_high_x, has_low_x]
    receives = [has_low_y, has_high_y, has_low_x, has_high_x]

    def speed_x(a):
        return (2 * a - (nvx - 1)) * 0.5 * SPACING

    def transport(step):
        copies = halo_copies(step)
        for copy, present in zip(copies, sends):
            pl.when(present)(copy.start)

        own = []
        for h in (0, 1):
            here = state[step, h]
            own.append(
                here * lanes[h]
                + pltpu.roll(here, 1, 1) * lanes[4]
                + pltpu.roll(here, NZ - 1, 1) * lanes[5]
            )

        for copy, present in zip(copies, receives):
            pl.when(present)(copy.wait_recv)

        for h in (0, 1):
            side = []
            for a in range(nvx):
                weight = COURANT * abs(speed_x(a))
                side.append(own[h][a] + (halo_x[step, h, a] - state[step, h, a]) * weight)
            moved[h] = jnp.stack(side) + halo_y[step, h] * lanes[2 + h]

    def advance(step, carry):
        rows = jnp.concatenate([moved[h].reshape(nvx * NZ, LANES) for h in (0, 1)], axis=1)

        span = 2 * LANES
        plane = jnp.dot(three_parts(rows), mats[: 3 * span], preferred_element_type=jnp.float32)
        plane = plane.reshape(nvx, NZ, span)
        real, imag = fourier(
            [plane[a, :, :LANES] for a in range(nvx)], [plane[a, :, LANES:] for a in range(nvx)], -1
        )
        spec[0] = jnp.stack(real)
        spec[1] = jnp.stack(imag)

        def weigh(w, carry):
            gains = [sym[a, pl.ds(w, 1), :] for a in range(nvx)]
            real, imag = fourier(
                [spec[0, a] * gains[a] for a in range(nvx)], [spec[1, a] * gains[a] for a in range(nvx)], 1
            )
            line = jnp.concatenate(
                [jnp.concatenate(real, axis=0), jnp.concatenate(imag, axis=0)], axis=1
            )
            tall = nvx * NZ
            back[pl.ds(pl.multiple_of(w * tall, tall), tall)] = three_parts(line)
            return carry

        lax.fori_loop(0, KERNELS, weigh, 0, unroll=True)
        found = jnp.dot(back[...], mats[3 * span :], preferred_element_type=jnp.float32)
        found = found.reshape(KERNELS, nvx * NZ, span)
        change = found[0] * found[2] + found[1] * found[3] - rows * found[4]
        after = rows + COLLISION_STEP * change
        for h in (0, 1):
            state[step, h] = after[:, h * LANES : (h + 1) * LANES].reshape(nvx, NZ, LANES)
        pl.when(step < STEPS - 1)(lambda: transport(step))
        return carry

    lax.fori_loop(0, STEPS, advance, 0)

    low, high = state[STEPS - 1, 0], state[STEPS - 1, 1]
    parts = [
        low,
        jnp.where(lane < quarter, turn(low, LOCAL_V), turn(high, quarter)),
        turn(high, LANES - quarter),
    ]
    stacked = [
        jnp.where(lane < LOCAL_V, part[:, : NZ // 2], turn(part, LOCAL_V)[:, NZ // 2 :]) for part in parts
    ]
    packed_back[...] = jnp.stack(stacked, axis=1).reshape(columns, NZ // 2, LANES)
    def send_home(to, column):
        send_block(packed_back, arrived_back, 1, to, to, me_y)

    in_place_order(send_home, 0, ring // 6)

    both = low + high
    sums_low, sums_high = jnp.sum(low, axis=0), jnp.sum(high, axis=0)
    along, squared = 0.0, 0.0
    for a in range(nvx):
        along = along + both[a] * (SPACING**3 * speed_x(a))
        squared = squared + both[a] * (SPACING**3 * speed_x(a) ** 2)
    totals = [
        along,
        sums_low * lanes[6] + sums_high * lanes[7],
        (sums_low + sums_high) * lanes[8],
        squared + sums_low * lanes[9] + sums_high * lanes[10],
    ]
    pl.when(moved_home)(uses_copy.wait_recv)
    counted = uses[...]
    shares = [
        jnp.sum(jnp.sum(total, axis=1, keepdims=True) * counted, axis=0, keepdims=True) for total in totals
    ]
    shares.append(jnp.zeros((NZ - MOMENTS, LANES), jnp.float32))
    share = jnp.concatenate(shares, axis=0)
    mine[...] = share
    all_others, rest = others.at[pl.ds(0, cells)], others.at[pl.ds(0, cells - 1)]

    def give(j, carry):
        to = lax.rem(me_c + j, cells)
        pltpu.make_async_remote_copy(
            src_ref=mine,
            dst_ref=others.at[me_c],
            send_sem=load_send,
            recv_sem=load_recv,
            device_id=(to, me_y),
            device_id_type=MESH,
        ).start()
        return carry

    lax.fori_loop(1, cells, give, 0)
    pl.when(moved_home)(lambda: give(0, None))

    in_place_order(send_home, ring // 6, ring)
    arrived_back[pl.ds(me_y, 1)] = packed_back[pl.ds(me_v, 1)]

    @pl.when(moved_home)
    def _():
        pltpu.make_async_copy(all_others, all_others, load_recv).wait()

    @pl.when(jnp.logical_not(moved_home))
    def _():
        others[pl.ds(me_c, 1)] = share[None]
        pltpu.make_async_copy(rest, rest, load_recv).wait()

    summed = jnp.sum(others[...], axis=0)
    picked = slot - PANEL_DEV * me_c
    columns_out = [
        jnp.sum(jnp.where(picked == k, summed, 0.0), axis=1, keepdims=True) for k in range(PANEL_DEV)
    ]
    loads[...] = jnp.concatenate(columns_out, axis=1)[:MOMENTS]

    arrivals(arrived_back, 1)
    for start in range(0, columns, LANES // NZ):
        stop = min(start + LANES // NZ, columns)
        block = arrived_back[start:stop]
        tall = jnp.concatenate([block, turn(block, LOCAL_V)], axis=1).reshape((stop - start) * NZ, LANES)
        out[:, 0, start * NZ : stop * NZ] = jnp.transpose(tall)[:LOCAL_V]

    departures(packed, 0)
    pl.when(sends_on)(pltpu.make_async_copy(packed_on, packed_on, on_send).wait)
    pl.when(gives)(give_copy.wait_send)
    departures(packed_back, 1)
    pl.when(moved_home)(uses_copy.wait_send)
    pl.when(moved_home)(pltpu.make_async_copy(all_others, all_others, load_send).wait)
    pl.when(jnp.logical_not(moved_home))(pltpu.make_async_copy(rest, rest, load_send).wait)

    def finish(step, carry):
        for copy, present in zip(halo_copies(step), sends):
            pl.when(present)(copy.wait_send)
        return carry

    lax.fori_loop(0, STEPS - 1, finish, 0)


def per_device(cells, columns, distribution, gain_left, gain_right, loss_kernel, wall_cell, wall_count, wall_panel):
    nvx = columns // PARTS
    local, _, width = distribution.shape
    f32 = jnp.float32
    loss = loss_kernel.reshape(1, -1)
    picks = jnp.asarray(weight_selectors())
    mats = jnp.asarray(plane_matrices())
    tables = jnp.asarray(lane_tables())
    rows = jnp.asarray(row_tables())
    anywhere = pl.BlockSpec(memory_space=pl.ANY)
    in_vmem = pl.BlockSpec(memory_space=pltpu.VMEM)
    dma = pltpu.SemaphoreType.DMA
    out, loads = pl.pallas_call(
        functools.partial(kernel, cells, columns),
        out_shape=(
            pltpu.VMEM((local, 1, width), f32),
            pltpu.VMEM((MOMENTS, PANEL_DEV), f32),
        ),
        in_specs=[anywhere] * 11,
        out_specs=(in_vmem, in_vmem),
        scratch_shapes=[
            pltpu.VMEM(distribution.shape, f32),
            pltpu.SMEM(wall_cell.shape, jnp.int32),
            pltpu.SMEM(wall_count.shape, jnp.int32),
            pltpu.SMEM(wall_panel.shape, jnp.int32),
            pltpu.VMEM(gain_left.shape, f32),
            pltpu.VMEM(gain_right.shape, f32),
            pltpu.VMEM(loss.shape, f32),
            pltpu.VMEM(picks.shape, jnp.bfloat16),
            pltpu.VMEM(mats.shape, jnp.bfloat16),
            pltpu.VMEM(tables.shape, f32),
            pltpu.VMEM(rows.shape, f32),
            pltpu.VMEM((columns + 2, NZ, LANES), f32),
            pltpu.VMEM((columns, NZ // 2, LANES), f32),
            pltpu.VMEM((columns, NZ // 2, LANES), f32),
            pltpu.VMEM((columns, NZ // 2, LANES), f32),
            pltpu.VMEM((columns, NZ // 2, LANES), f32),
            pltpu.VMEM((columns, NZ // 2, LANES), f32),
            pltpu.VMEM((2, nvx, NZ, LANES), f32),
            pltpu.VMEM((columns, NZ // 2, LANES), f32),
            pltpu.VMEM((columns, NZ // 2, LANES), f32),
            pltpu.VMEM((STEPS, 2, nvx, NZ, LANES), f32),
            pltpu.VMEM((STEPS - 1, 2, nvx, NZ, LANES), f32),
            pltpu.VMEM((STEPS - 1, 2, nvx, NZ, LANES), f32),
            pltpu.VMEM((nvx // 2, NZ, 2 * PLANE), f32),
            pltpu.VMEM((nvx, NZ, LANES), f32),
            pltpu.VMEM((2, nvx, NZ, LANES), f32),
            pltpu.VMEM((KERNELS * nvx * NZ, 6 * LANES), jnp.bfloat16),
            pltpu.VMEM((NZ, LANES), f32),
            pltpu.VMEM((NZ, LANES), f32),
            pltpu.VMEM((NZ, LANES), f32),
            pltpu.VMEM((cells, NZ, LANES), f32),
            dma((11,)),
            dma((4, STEPS - 1)),
            dma((4, STEPS - 1)),
            dma((2,)),
            dma((2,)),
            dma,
            dma((2,)),
            dma,
            dma,
            dma,
            dma,
            dma,
            dma,
        ],
        compiler_params=pltpu.CompilerParams(
            collective_id=0, has_side_effects=True, vmem_limit_bytes=VMEM_LIMIT
        ),
        cost_estimate=pl.CostEstimate(flops=1_000_000_000, bytes_accessed=2_000_000, transcendentals=0),
        name="collide",
    )(distribution, wall_cell, wall_count, wall_panel, gain_left, gain_right, loss, picks, mats, tables, rows)
    return out, loads


def solution(mesh):
    placed = (
        P("vel", "cell", None),
        P(),
        P(),
        P(),
        P("cell", "vel", None),
        P("cell", "vel"),
        P("cell", "vel", None),
    )
    return jax.shard_map(
        functools.partial(per_device, mesh.shape["cell"], mesh.shape["vel"]),
        mesh=mesh,
        in_specs=placed,
        out_specs=(P("vel", "cell", None), P(None, ("cell", "vel"))),
        check_vma=False,
    )
```

```python
import functools
import math

import jax
import jax.numpy as jnp
import ml_dtypes
import numpy as np
from jax import lax
from jax.experimental import pallas as pl
from jax.experimental.pallas import tpu as pltpu
from jax.sharding import PartitionSpec as P

NVY = 16
NVZ = 12
PLANE = NVY * NVZ
HALF = PLANE // 2
KEPT = NVZ // 2 + 1
KERNELS = 5
DIRS = 2
MOMENTS = 4
STEPS = 3
NZ = 8
WALL_SLOTS = 8
PANEL_DEV = 4
LOCAL_V = 64
PARTS = PLANE // LOCAL_V
LANES = 128
VMEM_LIMIT = 60 * 1024 * 1024

SPACING = 0.5
COURANT = 0.09
COLLISION_STEP = 0.3

MESH = pl.DeviceIdType.MESH


def split(values):
    high = values.astype(ml_dtypes.bfloat16)
    low = (values - high.astype(np.float64)).astype(ml_dtypes.bfloat16)
    return high, low


def plane_matrices():
    table = np.zeros((2 * LANES, 2 * LANES))
    for point in range(PLANE):
        b, c = divmod(point, NVZ)
        row = b // (NVY // 2) * LANES + point % HALF
        for kb in range(NVY):
            for kc in range(KEPT):
                angle = 2.0 * math.pi * ((b * kb % NVY) / NVY + (c * kc % NVZ) / NVZ)
                table[row, kb * KEPT + kc] = math.cos(angle)
                table[row, LANES + kb * KEPT + kc] = -math.sin(angle)
    high, low = split(table)
    return np.concatenate([high, high, low, high.T, high.T, low.T], axis=0)


def weight_selectors():
    table = np.zeros((2 * PLANE, 4 * LANES))
    for kb in range(NVY):
        for kc in range(KEPT):
            share = 0.5 if kc in (0, KEPT - 1) else 1.0
            column = kb * KEPT + kc
            there = kb * NVZ + kc
            mirror = -kb % NVY * NVZ + -kc % NVZ
            for half in (0, 1):
                table[half * PLANE + there, half * LANES + column] = share
                table[half * PLANE + mirror, (2 + half) * LANES + column] = share
    return table.astype(ml_dtypes.bfloat16)


def lane_tables():
    lane = np.arange(LANES)
    used = (lane < HALF).astype(np.float64)
    vz = (2 * (lane % NVZ) - (NVZ - 1)) * 0.5 * SPACING * used
    vy = [(2 * (lane // NVZ + h * NVY // 2) - (NVY - 1)) * 0.5 * SPACING * used for h in (0, 1)]
    z = np.arange(NZ)[:, None]
    rows = []
    for h in (0, 1):
        rows.append(1.0 - COURANT * (np.abs(vy[h]) + np.abs(vz)) + 0.0 * z)
    for h in (0, 1):
        rows.append(COURANT * np.abs(vy[h]) + 0.0 * z)
    rows.append(COURANT * np.maximum(vz, 0.0) * (z > 0))
    rows.append(COURANT * np.maximum(-vz, 0.0) * (z < NZ - 1))
    cube = SPACING**3
    rows.append(cube * vy[0] + 0.0 * z)
    rows.append(cube * vy[1] + 0.0 * z)
    rows.append(cube * vz + 0.0 * z)
    rows.append(cube * (vy[0] ** 2 + vz**2) + 0.0 * z)
    rows.append(cube * (vy[1] ** 2 + vz**2) + 0.0 * z)
    return np.stack(rows).astype(np.float32)


def row_tables():
    lane = np.arange(LANES)
    z = (np.arange(NZ)[:, None] + lane // LOCAL_V * (NZ // 2)) % NZ
    parts = []
    for part in range(PARTS):
        point = part * LOCAL_V + lane % LOCAL_V
        vy = (2 * (point // NVZ) - (NVY - 1)) * 0.5 * SPACING
        vz = (2 * (point % NVZ) - (NVZ - 1)) * 0.5 * SPACING
        parts.append([
            1.0 - COURANT * (np.abs(vy) + np.abs(vz)) + 0.0 * z,
            COURANT * np.maximum(vy, 0.0) + 0.0 * z,
            COURANT * np.maximum(-vy, 0.0) + 0.0 * z,
            COURANT * np.maximum(vz, 0.0) * (z > 0),
            COURANT * np.maximum(-vz, 0.0) * (z < NZ - 1),
        ])
    return np.array(parts).astype(np.float32)


def fourier(real, imag, sign):
    count = len(real)
    if count == 1:
        return real, imag
    even_r, even_i = fourier(real[::2], imag[::2], sign)
    odd_r, odd_i = fourier(real[1::2], imag[1::2], sign)
    out_r, out_i = [None] * count, [None] * count
    half = count // 2
    for k in range(half):
        r, i = odd_r[k], odd_i[k]
        if k == 0:
            pass
        elif 4 * k == count:
            r, i = (-i, r) if sign > 0 else (i, -r)
        else:
            cos = math.cos(2.0 * math.pi * k / count)
            sin = sign * math.sin(2.0 * math.pi * k / count)
            if 8 * k == count or 8 * k == 3 * count:
                size = math.sqrt(0.5)
                up, across = cos / abs(cos), sin / abs(sin)
                first = r - i if up == across else r + i
                second = r + i if up == across else (i - r)
                if up > 0:
                    r, i = (first * size, second * size)
                else:
                    r, i = (first * -size, second * -size)
            else:
                r, i = r * cos - i * sin, r * sin + i * cos
        out_r[k], out_i[k] = even_r[k] + r, even_i[k] + i
        out_r[k + half], out_i[k + half] = even_r[k] - r, even_i[k] - i
    return out_r, out_i


def three_parts(values):
    top = values.astype(jnp.bfloat16)
    rest = (values - top.astype(jnp.float32)).astype(jnp.bfloat16)
    return jnp.concatenate([top, rest, top], axis=1)


def kernel(
    cells, columns,
    x_in, wall_cell_in, wall_count_in, wall_panel_in, left_in, right_in, loss_in, picks_in, mats_in, lanes_in, own_in,
    out, loads,
    x_v, wall_cell, wall_count, wall_panel, left, right, loss, picks, mats, lanes, own_rows,
    field, packed, packed_on, from_mate, arrived, arrived_on, moved, packed_back, arrived_back, state, halo_x, halo_y,
    planes, sym, spec, back, my_uses, uses, mine, others,
    in_sems, halo_send, halo_recv, swap_send, swap_recv, on_send, on_recv, give_send, give_recv, load_send, load_recv, uses_send, uses_recv,
):
    nvx = columns // PARTS
    mid = nvx // 2
    me_c = lax.axis_index("cell")
    me_v = lax.axis_index("vel")

    lines = 4 if columns % 4 == 0 else 2
    ring = columns // lines

    def owner_of(column):
        line, place = column // ring, lax.rem(column, ring)
        return line * ring + lax.rem(place + 1 - line + ring, ring)

    def column_of(device):
        line, place = device // ring, lax.rem(device, ring)
        return line * ring + lax.rem(place - 1 + line + ring, ring)

    half = columns // 2
    goes_up = me_v >= half
    next_c = me_c + jnp.where(goes_up, 1, -1)
    has_next = jnp.logical_and(next_c >= 0, next_c < cells)
    even = lax.rem(me_c, 2) == 0
    mate = me_c + jnp.where(even, 1, -1)
    gives = next_c == mate
    sends_on = jnp.logical_and(has_next, jnp.logical_not(gives))
    low_sends = jnp.logical_and(even, me_c > 0)
    high_sends = jnp.logical_and(jnp.logical_not(even), me_c < cells - 1)
    me_y = column_of(me_v)
    my_owner = owner_of(me_v)
    line, place = me_v // ring, lax.rem(me_v, ring)

    def wrapped(value, count):
        return jnp.where(value >= count, value - count, value)

    across = [lines // 2 + (m + 1) // 2 * (1 if m % 2 else -1) for m in range(lines)]
    to_lines = [wrapped(line + shift % lines, lines) for shift in across]

    def visit_line(visit, there, m):
        column = there + to_lines[m] - 1
        column = wrapped(jnp.where(column < 0, column + ring, column), ring)
        visit(to_lines[m] * ring + there, to_lines[m] * ring + column)

    def farthest_first(visit, start, stop):
        def one_round(n, carry):
            away = (n + 1) // 2
            there = wrapped(place + ring // 2 + jnp.where(lax.rem(n, 2) == 1, away, -away), ring)
            for m in range(lines):
                visit_line(visit, there, m)
            return carry

        lax.fori_loop(start, min(stop, ring - 1), one_round, 0)
        if stop == ring:
            for m in range(lines - 1):
                visit_line(visit, place, m)

    def in_place_order(visit, start, stop):
        def one_round(there, carry):
            for m in range(lines - 1):
                visit_line(visit, there, m)
            pl.when(there != place)(lambda: visit_line(visit, there, lines - 1))
            return carry

        lax.fori_loop(start, stop, one_round, 0)

    pairs = [
        (x_in, x_v), (wall_cell_in, wall_cell), (wall_count_in, wall_count), (wall_panel_in, wall_panel),
        (left_in, left), (right_in, right), (loss_in, loss), (picks_in, picks), (mats_in, mats), (lanes_in, lanes), (own_in, own_rows),
    ]
    loads_in = [pltpu.make_async_copy(src, dst, in_sems.at[n]) for n, (src, dst) in enumerate(pairs)]
    loads_in[0].start()

    barrier = pltpu.get_barrier_semaphore()

    def greet_column(to, column):
        pl.semaphore_signal(barrier, inc=1, device_id=(me_c, to), device_id_type=MESH)
        greet_sender(to)

    def greet_sender(to):
        upward = to >= half
        present = jnp.logical_or(jnp.logical_and(upward, low_sends), jnp.logical_and(to < half, high_sends))

        @pl.when(present)
        def _():
            neighbour = me_c + jnp.where(upward, -1, 1)
            pl.semaphore_signal(barrier, inc=1, device_id=(neighbour, to), device_id_type=MESH)

    def greet_row(j, carry):
        to = lax.rem(me_c + j, cells)
        pl.semaphore_signal(barrier, inc=1, device_id=(to, my_owner), device_id_type=MESH)
        return carry

    has_low_x, has_high_x = me_c > 0, me_c < cells - 1
    has_low_y, has_high_y = me_y > 0, me_y < columns - 1
    moved_home = my_owner != me_v
    greetings = [(jnp.logical_and(moved_home, has_low_x), -1), (jnp.logical_and(moved_home, has_high_x), 1)]

    farthest_first(greet_column, 0, ring // 4)
    lax.fori_loop(1, cells, greet_row, 0)
    farthest_first(greet_column, ring // 4, ring)
    greet_sender(me_v)

    @pl.when(jnp.logical_not(gives))
    def _():
        pl.semaphore_signal(barrier, inc=1, device_id=(mate, me_v), device_id_type=MESH)

    greeted = columns - 1 + cells - 1 + jnp.where(gives, 1, jnp.where(sends_on, columns, 0))
    for present, way in greetings:
        greeted = greeted + jnp.where(present, 1, 0)

        @pl.when(present)
        def _():
            pl.semaphore_signal(barrier, inc=1, device_id=(me_c + way, me_v), device_id_type=MESH)

    for copy in loads_in[1:]:
        copy.start()

    loads_in[0].wait()
    width = NZ * columns
    for start in range(0, width, LANES):
        stop = min(start + LANES, width)
        tile = x_v[:, 0, start:stop]
        back_by_half = jnp.concatenate([tile[:, NZ // 2 :], tile[:, : NZ // 2]], axis=1)
        on_by_half = jnp.concatenate([tile[:, -(NZ // 2) :], tile[:, : -(NZ // 2)]], axis=1)
        place_z = lax.rem(lax.broadcasted_iota(jnp.int32, tile.shape, 1), NZ)
        shifted = jnp.where(place_z < NZ // 2, back_by_half, on_by_half)
        turned = jnp.transpose(jnp.concatenate([tile, shifted], axis=0))
        turned = turned.reshape((stop - start) // NZ, NZ, LANES)
        field[1 + start // NZ : 1 + stop // NZ] = turned
    field[0] = jnp.zeros((NZ, LANES), jnp.float32)
    field[columns + 1] = jnp.zeros((NZ, LANES), jnp.float32)

    loads_in[10].wait()
    part = lax.rem(me_v, PARTS)
    weight_x = COURANT * 0.5 * SPACING * jnp.abs(2 * (me_v // PARTS) - (nvx - 1)).astype(jnp.float32)
    here = field[1 : columns + 1]
    stays = (
        here * (own_rows[part, 0] - weight_x)
        + field[:columns] * own_rows[part, 1]
        + field[2:] * own_rows[part, 2]
        + pltpu.roll(here, 1, 1) * own_rows[part, 3]
        + pltpu.roll(here, NZ - 1, 1) * own_rows[part, 4]
    )
    packed[...] = stays[:, : NZ // 2]
    packed_on[...] = here[:, : NZ // 2] * weight_x

    @pl.when(jnp.logical_not(low_sends))
    def _():
        arrived_on[half:] = jnp.zeros((half, NZ // 2, LANES), jnp.float32)

    @pl.when(jnp.logical_not(high_sends))
    def _():
        arrived_on[:half] = jnp.zeros((half, NZ // 2, LANES), jnp.float32)

    depth = lax.broadcasted_iota(jnp.int32, (NZ, LANES), 0)
    slot = lax.broadcasted_iota(jnp.int32, (NZ, LANES), 1)
    for copy in loads_in[1:4]:
        copy.wait()
    counted = jnp.zeros((NZ, LANES), jnp.float32)
    per_owner = PANEL_DEV * columns
    for n in range(WALL_SLOTS):
        panel = wall_panel[0, 0, n]
        target = panel // per_owner * PANEL_DEV + lax.rem(panel, PANEL_DEV)
        target = jnp.where(n < wall_count[0, 0], target, -1)
        hit = jnp.logical_and(depth == wall_cell[0, 0, n], slot == target)
        counted = counted + jnp.where(hit, 1.0, 0.0)
    my_uses[...] = counted

    @pl.when(jnp.logical_not(moved_home))
    def _():
        uses[...] = counted

    pl.semaphore_wait(barrier, greeted)

    def send_block(source, target, which, to, source_slot, target_slot):
        pltpu.make_async_remote_copy(
            src_ref=source.at[source_slot],
            dst_ref=target.at[target_slot],
            send_sem=swap_send.at[which],
            recv_sem=swap_recv.at[which],
            device_id=(me_c, to),
            device_id_type=MESH,
        ).start()

    def arrivals(target, which):
        rest = target.at[pl.ds(0, columns - 1)]
        pltpu.make_async_copy(rest, rest, swap_recv.at[which]).wait()

    def departures(source, which):
        rest = source.at[pl.ds(0, columns - 1)]
        pltpu.make_async_copy(rest, rest, swap_send.at[which]).wait()

    on_way = jnp.where(goes_up, 0, 1)

    def send_on(to, column):
        pltpu.make_async_remote_copy(
            src_ref=packed_on.at[column],
            dst_ref=arrived_on.at[me_v],
            send_sem=on_send,
            recv_sem=on_recv.at[on_way],
            device_id=(next_c, to),
            device_id_type=MESH,
        ).start()

    def send_one(to, column):
        send_block(packed, arrived, 0, to, column, me_v)

    give_copy = pltpu.make_async_remote_copy(
        src_ref=packed_on,
        dst_ref=from_mate,
        send_sem=give_send,
        recv_sem=give_recv,
        device_id=(mate, me_v),
        device_id_type=MESH,
    )
    pl.when(gives)(give_copy.start)

    @pl.when(jnp.logical_not(gives))
    def _():
        pl.when(sends_on)(lambda: farthest_first(send_on, 0, ring // 4))
        give_copy.wait_recv()
        packed[...] = packed[...] + from_mate[...]

    farthest_first(send_one, 0, ring)
    arrived[pl.ds(me_v, 1)] = packed[pl.ds(me_y, 1)]

    @pl.when(sends_on)
    def _():
        farthest_first(send_on, ring // 4, ring)
        send_on(me_v, me_y)

    uses_copy = pltpu.make_async_remote_copy(
        src_ref=my_uses,
        dst_ref=uses,
        send_sem=uses_send,
        recv_sem=uses_recv,
        device_id=(me_c, my_owner),
        device_id_type=MESH,
    )
    pl.when(moved_home)(uses_copy.start)

    @pl.when(jnp.logical_not(has_low_x))
    def _():
        halo_x[:, :, mid:] = jnp.zeros((STEPS - 1, 2, mid, NZ, LANES), jnp.float32)

    @pl.when(jnp.logical_not(has_high_x))
    def _():
        halo_x[:, :, :mid] = jnp.zeros((STEPS - 1, 2, mid, NZ, LANES), jnp.float32)

    @pl.when(jnp.logical_not(has_low_y))
    def _():
        halo_y[:, 1] = jnp.zeros((STEPS - 1, nvx, NZ, LANES), jnp.float32)

    @pl.when(jnp.logical_not(has_high_y))
    def _():
        halo_y[:, 0] = jnp.zeros((STEPS - 1, nvx, NZ, LANES), jnp.float32)

    for copy in loads_in[4:10]:
        copy.wait()
    for pair in range(nvx // 2):
        span = slice(pair * 2 * PLANE, (pair + 1) * 2 * PLANE)
        planes[pair, :DIRS] = left[:, span]
        planes[pair, DIRS : 2 * DIRS] = right[:, span]
        planes[pair, 2 * DIRS : KERNELS] = loss[:, span]
        planes[pair, KERNELS:] = jnp.zeros((NZ - KERNELS, 2 * PLANE), jnp.float32)
    remaining = planes[...].reshape(nvx // 2 * NZ, 2 * PLANE)
    chosen = 0.0
    for _ in range(3):
        top = remaining.astype(jnp.bfloat16)
        chosen = chosen + jnp.dot(top, picks[...], preferred_element_type=jnp.float32)
        remaining = remaining - top.astype(jnp.float32)
    chosen = (chosen * (1.0 / (nvx * PLANE))).reshape(nvx // 2, NZ, 4 * LANES)
    for a in range(nvx):
        b = -a % nvx
        near, far = a % 2 * LANES, (2 + b % 2) * LANES
        sym[a] = chosen[a // 2, :, near : near + LANES] + chosen[b // 2, :, far : far + LANES]

    arrivals(arrived, 0)
    from_low, from_high = arrived_on.at[pl.ds(half, half)], arrived_on.at[pl.ds(0, half)]
    pl.when(low_sends)(pltpu.make_async_copy(from_low, from_low, on_recv.at[0]).wait)
    pl.when(high_sends)(pltpu.make_async_copy(from_high, from_high, on_recv.at[1]).wait)

    lane = lax.broadcasted_iota(jnp.int32, (1, 1, LANES), 2)
    used = lane < HALF
    quarter = LOCAL_V // 2

    def turn(values, by):
        return pltpu.roll(values, by, values.ndim - 1)

    blocks = (arrived[...] + arrived_on[...]).reshape(nvx, PARTS, NZ // 2, LANES)
    wide = []
    for part in range(PARTS):
        block = blocks[:, part]
        wide.append(jnp.concatenate([block, turn(block, LOCAL_V)], axis=1))
    moved[0] = jnp.where(lane < LOCAL_V, wide[0], jnp.where(used, turn(wide[1], LOCAL_V), 0.0))
    moved[1] = jnp.where(
        lane < quarter, turn(wide[1], LANES - quarter), jnp.where(used, turn(wide[2], quarter), 0.0)
    )

    def halo_copies(step):
        routes = [
            (state.at[step, 1], halo_y.at[step, 1], (me_c, owner_of(me_y + 1))),
            (state.at[step, 0], halo_y.at[step, 0], (me_c, owner_of(me_y - 1))),
            (state.at[step, :, pl.ds(mid, mid)], halo_x.at[step, :, pl.ds(mid, mid)], (me_c + 1, me_v)),
            (state.at[step, :, pl.ds(0, mid)], halo_x.at[step, :, pl.ds(0, mid)], (me_c - 1, me_v)),
        ]
        return [
            pltpu.make_async_remote_copy(
                src_ref=src,
                dst_ref=dst,
                send_sem=halo_send.at[n, step],
                recv_sem=halo_recv.at[n, step],
                device_id=to,
                device_id_type=MESH,
            )
            for n, (src, dst, to) in enumerate(routes)
        ]

    sends = [has_high_y, has_low_y, has_high_x, has_low_x]
    receives = [has_low_y, has_high_y, has_low_x, has_high_x]

    def speed_x(a):
        return (2 * a - (nvx - 1)) * 0.5 * SPACING

    def transport(step):
        copies = halo_copies(step)
        for copy, present in zip(copies, sends):
            pl.when(present)(copy.start)

        own = []
        for h in (0, 1):
            here = state[step, h]
            own.append(
                here * lanes[h]
                + pltpu.roll(here, 1, 1) * lanes[4]
                + pltpu.roll(here, NZ - 1, 1) * lanes[5]
            )

        for copy, present in zip(copies, receives):
            pl.when(present)(copy.wait_recv)

        for h in (0, 1):
            side = []
            for a in range(nvx):
                weight = COURANT * abs(speed_x(a))
                side.append(own[h][a] + (halo_x[step, h, a] - state[step, h, a]) * weight)
            moved[h] = jnp.stack(side) + halo_y[step, h] * lanes[2 + h]

    def advance(step, carry):
        rows = jnp.concatenate([moved[h].reshape(nvx * NZ, LANES) for h in (0, 1)], axis=1)

        span = 2 * LANES
        plane = jnp.dot(three_parts(rows), mats[: 3 * span], preferred_element_type=jnp.float32)
        plane = plane.reshape(nvx, NZ, span)
        real, imag = fourier(
            [plane[a, :, :LANES] for a in range(nvx)], [plane[a, :, LANES:] for a in range(nvx)], -1
        )
        spec[0] = jnp.stack(real)
        spec[1] = jnp.stack(imag)

        def weigh(w, carry):
            gains = [sym[a, pl.ds(w, 1), :] for a in range(nvx)]
            real, imag = fourier(
                [spec[0, a] * gains[a] for a in range(nvx)], [spec[1, a] * gains[a] for a in range(nvx)], 1
            )
            line = jnp.concatenate(
                [jnp.concatenate(real, axis=0), jnp.concatenate(imag, axis=0)], axis=1
            )
            tall = nvx * NZ
            back[pl.ds(pl.multiple_of(w * tall, tall), tall)] = three_parts(line)
            return carry

        lax.fori_loop(0, KERNELS, weigh, 0, unroll=True)
        found = jnp.dot(back[...], mats[3 * span :], preferred_element_type=jnp.float32)
        found = found.reshape(KERNELS, nvx * NZ, span)
        change = found[0] * found[2] + found[1] * found[3] - rows * found[4]
        after = rows + COLLISION_STEP * change
        for h in (0, 1):
            state[step, h] = after[:, h * LANES : (h + 1) * LANES].reshape(nvx, NZ, LANES)
        pl.when(step < STEPS - 1)(lambda: transport(step))
        return carry

    lax.fori_loop(0, STEPS, advance, 0)

    low, high = state[STEPS - 1, 0], state[STEPS - 1, 1]
    parts = [
        low,
        jnp.where(lane < quarter, turn(low, LOCAL_V), turn(high, quarter)),
        turn(high, LANES - quarter),
    ]
    stacked = [
        jnp.where(lane < LOCAL_V, part[:, : NZ // 2], turn(part, LOCAL_V)[:, NZ // 2 :]) for part in parts
    ]
    packed_back[...] = jnp.stack(stacked, axis=1).reshape(columns, NZ // 2, LANES)
    def send_home(to, column):
        send_block(packed_back, arrived_back, 1, to, to, me_y)

    in_place_order(send_home, 0, 1)

    both = low + high
    sums_low, sums_high = jnp.sum(low, axis=0), jnp.sum(high, axis=0)
    along, squared = 0.0, 0.0
    for a in range(nvx):
        along = along + both[a] * (SPACING**3 * speed_x(a))
        squared = squared + both[a] * (SPACING**3 * speed_x(a) ** 2)
    totals = [
        along,
        sums_low * lanes[6] + sums_high * lanes[7],
        (sums_low + sums_high) * lanes[8],
        squared + sums_low * lanes[9] + sums_high * lanes[10],
    ]
    pl.when(moved_home)(uses_copy.wait_recv)
    counted = uses[...]
    shares = [
        jnp.sum(jnp.sum(total, axis=1, keepdims=True) * counted, axis=0, keepdims=True) for total in totals
    ]
    shares.append(jnp.zeros((NZ - MOMENTS, LANES), jnp.float32))
    share = jnp.concatenate(shares, axis=0)
    mine[...] = share
    all_others, rest = others.at[pl.ds(0, cells)], others.at[pl.ds(0, cells - 1)]

    def give(j, carry):
        to = lax.rem(me_c + j, cells)
        pltpu.make_async_remote_copy(
            src_ref=mine,
            dst_ref=others.at[me_c],
            send_sem=load_send,
            recv_sem=load_recv,
            device_id=(to, me_y),
            device_id_type=MESH,
        ).start()
        return carry

    lax.fori_loop(1, cells, give, 0)
    pl.when(moved_home)(lambda: give(0, None))

    in_place_order(send_home, 1, ring)
    arrived_back[pl.ds(me_y, 1)] = packed_back[pl.ds(me_v, 1)]

    @pl.when(moved_home)
    def _():
        pltpu.make_async_copy(all_others, all_others, load_recv).wait()

    @pl.when(jnp.logical_not(moved_home))
    def _():
        others[pl.ds(me_c, 1)] = share[None]
        pltpu.make_async_copy(rest, rest, load_recv).wait()

    summed = jnp.sum(others[...], axis=0)
    picked = slot - PANEL_DEV * me_c
    columns_out = [
        jnp.sum(jnp.where(picked == k, summed, 0.0), axis=1, keepdims=True) for k in range(PANEL_DEV)
    ]
    loads[...] = jnp.concatenate(columns_out, axis=1)[:MOMENTS]

    arrivals(arrived_back, 1)
    for start in range(0, columns, LANES // NZ):
        stop = min(start + LANES // NZ, columns)
        block = arrived_back[start:stop]
        tall = jnp.concatenate([block, turn(block, LOCAL_V)], axis=1).reshape((stop - start) * NZ, LANES)
        out[:, 0, start * NZ : stop * NZ] = jnp.transpose(tall)[:LOCAL_V]

    departures(packed, 0)
    pl.when(sends_on)(pltpu.make_async_copy(packed_on, packed_on, on_send).wait)
    pl.when(gives)(give_copy.wait_send)
    departures(packed_back, 1)
    pl.when(moved_home)(uses_copy.wait_send)
    pl.when(moved_home)(pltpu.make_async_copy(all_others, all_others, load_send).wait)
    pl.when(jnp.logical_not(moved_home))(pltpu.make_async_copy(rest, rest, load_send).wait)

    def finish(step, carry):
        for copy, present in zip(halo_copies(step), sends):
            pl.when(present)(copy.wait_send)
        return carry

    lax.fori_loop(0, STEPS - 1, finish, 0)


def per_device(cells, columns, distribution, gain_left, gain_right, loss_kernel, wall_cell, wall_count, wall_panel):
    nvx = columns // PARTS
    local, _, width = distribution.shape
    f32 = jnp.float32
    loss = loss_kernel.reshape(1, -1)
    picks = jnp.asarray(weight_selectors())
    mats = jnp.asarray(plane_matrices())
    tables = jnp.asarray(lane_tables())
    rows = jnp.asarray(row_tables())
    anywhere = pl.BlockSpec(memory_space=pl.ANY)
    in_vmem = pl.BlockSpec(memory_space=pltpu.VMEM)
    dma = pltpu.SemaphoreType.DMA
    out, loads = pl.pallas_call(
        functools.partial(kernel, cells, columns),
        out_shape=(
            pltpu.VMEM((local, 1, width), f32),
            pltpu.VMEM((MOMENTS, PANEL_DEV), f32),
        ),
        in_specs=[anywhere] * 11,
        out_specs=(in_vmem, in_vmem),
        scratch_shapes=[
            pltpu.VMEM(distribution.shape, f32),
            pltpu.SMEM(wall_cell.shape, jnp.int32),
            pltpu.SMEM(wall_count.shape, jnp.int32),
            pltpu.SMEM(wall_panel.shape, jnp.int32),
            pltpu.VMEM(gain_left.shape, f32),
            pltpu.VMEM(gain_right.shape, f32),
            pltpu.VMEM(loss.shape, f32),
            pltpu.VMEM(picks.shape, jnp.bfloat16),
            pltpu.VMEM(mats.shape, jnp.bfloat16),
            pltpu.VMEM(tables.shape, f32),
            pltpu.VMEM(rows.shape, f32),
            pltpu.VMEM((columns + 2, NZ, LANES), f32),
            pltpu.VMEM((columns, NZ // 2, LANES), f32),
            pltpu.VMEM((columns, NZ // 2, LANES), f32),
            pltpu.VMEM((columns, NZ // 2, LANES), f32),
            pltpu.VMEM((columns, NZ // 2, LANES), f32),
            pltpu.VMEM((columns, NZ // 2, LANES), f32),
            pltpu.VMEM((2, nvx, NZ, LANES), f32),
            pltpu.VMEM((columns, NZ // 2, LANES), f32),
            pltpu.VMEM((columns, NZ // 2, LANES), f32),
            pltpu.VMEM((STEPS, 2, nvx, NZ, LANES), f32),
            pltpu.VMEM((STEPS - 1, 2, nvx, NZ, LANES), f32),
            pltpu.VMEM((STEPS - 1, 2, nvx, NZ, LANES), f32),
            pltpu.VMEM((nvx // 2, NZ, 2 * PLANE), f32),
            pltpu.VMEM((nvx, NZ, LANES), f32),
            pltpu.VMEM((2, nvx, NZ, LANES), f32),
            pltpu.VMEM((KERNELS * nvx * NZ, 6 * LANES), jnp.bfloat16),
            pltpu.VMEM((NZ, LANES), f32),
            pltpu.VMEM((NZ, LANES), f32),
            pltpu.VMEM((NZ, LANES), f32),
            pltpu.VMEM((cells, NZ, LANES), f32),
            dma((11,)),
            dma((4, STEPS - 1)),
            dma((4, STEPS - 1)),
            dma((2,)),
            dma((2,)),
            dma,
            dma((2,)),
            dma,
            dma,
            dma,
            dma,
            dma,
            dma,
        ],
        compiler_params=pltpu.CompilerParams(
            collective_id=0, has_side_effects=True, vmem_limit_bytes=VMEM_LIMIT
        ),
        cost_estimate=pl.CostEstimate(flops=1_000_000_000, bytes_accessed=2_000_000, transcendentals=0),
        name="collide",
    )(distribution, wall_cell, wall_count, wall_panel, gain_left, gain_right, loss, picks, mats, tables, rows)
    return out, loads


def solution(mesh):
    placed = (
        P("vel", "cell", None),
        P(),
        P(),
        P(),
        P("cell", "vel", None),
        P("cell", "vel"),
        P("cell", "vel", None),
    )
    return jax.shard_map(
        functools.partial(per_device, mesh.shape["cell"], mesh.shape["vel"]),
        mesh=mesh,
        in_specs=placed,
        out_specs=(P("vel", "cell", None), P(None, ("cell", "vel"))),
        check_vma=False,
    )
```
